32 devices in a mesh: dp: 8 (over z, y), tensor: 4 (over x, core).
Axes of the slice: x: 2, y: 2, z: 4, core: 2. Of those that a mesh axis runs over, the one named last changes fastest.
Arguments:
- tokens: bfloat16 [8, 1024, 1024], P('dp', 'tensor'), may hold values from -6 to 6
- segments: int32 [8, 1024], P('dp'), may hold values from 0 to 4, as said below
- routes: int32 [8, 1024, 8], P('dp'), may hold values from 0 to 31, all different within a row
- priority: int32 [8, 1024], P('dp'), may hold values from 0 to 1023, as said below
- norm_attn: bfloat16 [1024], P('dp'), may hold values from 0.5 to 1.5
- w_query: bfloat16 [1024, 1024], P('dp', 'tensor'), may hold values from -0.1875 to 0.1875
- w_key: bfloat16 [1024, 512], P('dp', 'tensor'), may hold values from -0.1875 to 0.1875
- w_value: bfloat16 [1024, 512], P('dp', 'tensor'), may hold values from -0.1875 to 0.1875
- w_out: bfloat16 [1024, 1024], P('dp', 'tensor'), may hold values from -1 to 1
- norm_moe: bfloat16 [1024], P('dp'), may hold values from 0.5 to 1.5
- w_router: bfloat16 [1024, 32], P('dp'), may hold values from -0.09375 to 0.09375
- w_gate: bfloat16 [32, 1024, 512], P(None, 'dp', 'tensor'), may hold values from -0.1875 to 0.1875
- w_up: bfloat16 [32, 1024, 512], P(None, 'dp', 'tensor'), may hold values from -0.1875 to 0.1875
- w_down: bfloat16 [32, 1024, 512], P(None, 'dp', 'tensor'), may hold values from -1 to 1
- cotangent: bfloat16 [8, 1024, 1024], P('dp', 'tensor'), may hold values from -6 to 6
Outputs:
- block_out: bfloat16 [8, 1024, 1024], P('dp', 'tensor')
- tokens_grad: float32 [8, 1024, 1024], P('dp', 'tensor')
- norm_attn_grad: float32 [1024], P('dp')
- query_grad: float32 [1024, 1024], P('dp', 'tensor')
- key_grad: float32 [1024, 512], P('dp', 'tensor')
- value_grad: float32 [1024, 512], P('dp', 'tensor')
- out_grad: float32 [1024, 1024], P('dp', 'tensor')
- norm_moe_grad: float32 [1024], P('dp')
- router_grad: float32 [1024, 32], P('dp')
- gate_grad: float32 [32, 1024, 512], P(None, 'dp', 'tensor')
- up_grad: float32 [32, 1024, 512], P(None, 'dp', 'tensor')
- down_grad: float32 [32, 1024, 512], P(None, 'dp', 'tensor')
The draws below stay inside these ranges and needn't reach their ends.
Inputs may be any that keep to these rules, and one draw needn't show every extreme that they name: `segments`: numbers start at 0 in each sequence, never fall along it, and end at 4 in every sequence. `priority`: each run of 1 sequence of one data group holds every number once.
All inputs are finite; a program needn't handle non-finite values.
Results may differ from the reference program's by a relative error of at most 0.014.
Values may be sent and summed in bfloat16 or wider, within the bound.
No kernel may reach another device: no remote copies, remote signals or barrier semaphores. Data moves between devices by JAX's collectives and lax.ppermute only.
A program may use at most 192 MiB of HBM per device.

```python
import math
import jax
import jax.numpy as jnp
from jax import lax

D = 1024
H = 16
KEY_VALUE_HEADS = 8
HEAD_SIZE = 64
E = 32
TOP = 8
FF = 512
LEN = 1024
SEQS = 1
BATCH = 8
GROUPS = 8
CAP = 256
QCOLS = 1024
KVCOLS = 512
N_DP = 8


def draw_segments(key, part):
    key = jax.random.fold_in(key, 11)
    key_first, key_start, key_end = jax.random.split(key, 3)
    first_cut = jax.random.randint(key_first, (BATCH, 1), 1, LEN // 16 + 1)
    start_doc = jax.random.randint(key_start, (BATCH, 1), LEN // 16 + 1, LEN // 8 + 1)
    end_doc = jax.random.randint(key_end, (BATCH, 1), LEN - LEN // 8, LEN - 1)
    spots = jnp.arange(LEN, dtype=jnp.int32)[None, :]
    change = (spots == first_cut) | (spots == start_doc) | (spots == end_doc) | (spots == LEN - 1)
    return jnp.cumsum(change.astype(jnp.int32), axis=1).astype(jnp.int32)


def draw_priority(key, part):
    key = jax.random.fold_in(key, 23)
    group_keys = jax.random.split(key, GROUPS)
    orders = jax.vmap(lambda group_key: jax.random.permutation(group_key, SEQS * LEN))(group_keys)
    return orders.reshape(BATCH, LEN).astype(jnp.int32)


def block_levels(stream_key, extent, shards, low, top_value):
    def one(axis_at, shards_of):
        draws = jax.random.uniform(jax.random.fold_in(jax.random.fold_in(stream_key, 6), axis_at), (shards_of,), jnp.float32, low / len(shards), top_value / len(shards))
        return jnp.repeat(jnp.exp(draws), extent[axis_at] // shards_of).reshape((-1,) + (1,) * (len(extent) - axis_at - 1))

    level = one(*shards[0])
    for cut in shards[1:]:
        level = level * one(*cut)
    return level


def choose_distinct(key, rows, amount, top, lift):
    sequence = jax.random.permutation(jax.random.fold_in(key, 1), amount)
    favour = sequence
    for power in range(3):
        favour = favour * favour // amount
    favour = favour * lift // amount
    chance = jax.random.randint(jax.random.fold_in(key, 2), (rows, amount), 0, 4096) + favour
    fixed_rows = jax.random.permutation(jax.random.fold_in(key, 3), rows)[jnp.arange(amount) % rows]
    chance = jnp.where(jnp.arange(rows)[:, None] == fixed_rows[None, :], 1 << 14, chance)
    score = chance * amount + jnp.arange(amount)
    return lax.top_k(score.astype(jnp.int32), top)[1].astype(jnp.int32)


def gaussian(key, dims, width, reach, shards=(), kind=jnp.bfloat16):
    values = jax.random.normal(key, dims, jnp.float32) * width
    if len(shards) > 0:
        values = block_levels(key, dims, shards, -0.22, 0.18) * values
    return jnp.clip(values, min=-reach, max=reach).astype(kind)


def setup_inputs(seed: int = 0) -> dict:
    keys = jax.random.split(jax.random.key(seed), 16)
    tokens = gaussian(keys[0], (BATCH, LEN, D), 1.0, 6.0, ((0, 8), (1, 4)))
    segments = draw_segments(jax.random.fold_in(keys[15], 71), 0)
    routes = choose_distinct(keys[2], BATCH * LEN, E, TOP, 2048).reshape((BATCH, LEN, TOP))
    priority = draw_priority(jax.random.fold_in(keys[15], 71), 0)
    norm_attn = jnp.clip(1.0 + 0.1 * jax.random.normal(keys[4], (D,), jnp.float32), 0.5, 1.5).astype(jnp.bfloat16)
    w_query = gaussian(keys[5], (D, QCOLS), D ** -0.5, 0.1875, ((0, 8), (1, 4)))
    w_key = gaussian(keys[6], (D, KVCOLS), D ** -0.5, 0.1875, ((0, 8), (1, 4)))
    w_value = gaussian(keys[7], (D, KVCOLS), D ** -0.5, 0.1875, ((0, 8), (1, 4)))
    w_out = gaussian(keys[8], (D, QCOLS), (QCOLS // 32) ** -0.5, 1.0, ((0, 8), (1, 4)))
    norm_moe = jnp.clip(1.0 + 0.1 * jax.random.normal(keys[9], (D,), jnp.float32), 0.5, 1.5).astype(jnp.bfloat16)
    w_router = gaussian(keys[10], (D, E), (4 * D) ** -0.5, 0.09375, ((0, 8),))
    w_gate = gaussian(keys[11], (E, D, FF), D ** -0.5, 0.1875, ((1, 8), (2, 4)))
    w_up = gaussian(keys[12], (E, D, FF), D ** -0.5, 0.1875, ((1, 8), (2, 4)))
    w_down = gaussian(keys[13], (E, D, FF), (FF // 16) ** -0.5, 1.0, ((1, 8), (2, 4)))
    cotangent = gaussian(keys[14], (BATCH, LEN, D), 1.0, 6.0, ((0, 8), (1, 4)))
    return dict(tokens=tokens, segments=segments, routes=routes, priority=priority, norm_attn=norm_attn, w_query=w_query, w_key=w_key, w_value=w_value, w_out=w_out, norm_moe=norm_moe, w_router=w_router, w_gate=w_gate, w_up=w_up, w_down=w_down, cotangent=cotangent)


@jax.custom_vjp
def reduced_precision(v):
    return lax.optimization_barrier(v.astype(jnp.bfloat16)).astype(jnp.float32)

@jax.custom_vjp
def reduced_precision_backward(v):
    return v

def low_keep(v):
    return (reduced_precision(v), None)

def low_pass(kept, grad):
    return (grad,)

def back_keep(v):
    return (v, None)

def back_low(kept, grad):
    return (reduced_precision(grad),)
reduced_precision.defvjp(low_keep, low_pass)
reduced_precision_backward.defvjp(back_keep, back_low)
EPSILON = 1e-06
TOP_PRECISION = lax.Precision.HIGHEST
FLOOR_SCORE = -1e+30

def rms_norm(value_rows, gain):
    return value_rows * lax.rsqrt(lax.optimization_barrier(jnp.mean(value_rows * value_rows, axis=-1, keepdims=True)) + EPSILON) * gain

def positions(segments):
    complete_length = segments.shape[-1]
    spots = jnp.broadcast_to(jnp.arange(complete_length, dtype=jnp.int32), segments.shape)
    change = jnp.concatenate([jnp.ones(segments.shape[:-1] + (1,), dtype=jnp.bool_), segments[..., 1:] != segments[..., :-1]], axis=-1)
    starts = lax.cummax(jnp.where(change, spots, 0), axis=segments.ndim - 1)
    return spots - starts

def rope_tables(places, head_dim):
    half_dim = head_dim // 2
    inverse = jnp.exp(jnp.arange(half_dim, dtype=jnp.float32) * (-2.0 * math.log(10000.0) / head_dim))
    angle = places.astype(jnp.float32)[..., None] * inverse
    return (jnp.cos(angle)[..., None, :], jnp.sin(angle)[..., None, :])

def rotate(value_rows, cosine, sine):
    half_dim = value_rows.shape[-1] // 2
    front = value_rows[..., :half_dim]
    rear = value_rows[..., half_dim:]
    return jnp.concatenate([front * cosine - rear * sine, rear * cosine + front * sine], axis=-1)

def slot_plan(routes_flat, priority_flat, expert_count, capacity):
    token_count = routes_flat.shape[0]
    labels = jnp.arange(expert_count, dtype=jnp.int32)
    hit_counts = lax.optimization_barrier(jnp.sum((routes_flat[:, :, None] == labels).astype(jnp.int32), axis=1, dtype=jnp.int32))
    by_priority = jnp.zeros((token_count,), jnp.int32).at[priority_flat].set(jnp.arange(token_count, dtype=jnp.int32))
    ordered_hits = hit_counts[by_priority]
    earlier = jnp.cumsum(ordered_hits, axis=0, dtype=jnp.int32) - ordered_hits
    pair_rank = jnp.take_along_axis(earlier[priority_flat], routes_flat, axis=1)
    kept_pairs = pair_rank < capacity
    slot_place = jnp.where(kept_pairs, pair_rank, capacity)
    owners = jnp.broadcast_to(jnp.arange(token_count, dtype=jnp.int32)[:, None], routes_flat.shape)
    slot_table = jnp.full((expert_count, capacity), token_count, jnp.int32).at[routes_flat, slot_place].set(owners, mode='drop')
    return (kept_pairs, jnp.minimum(pair_rank, capacity - 1), slot_table)

def forward_group(segments, routes_flat, priority_flat, inputs, gain_attn, query_matrix, key_matrix, value_matrix, output_matrix, gain_moe, router_w, gate_w, up_w, down_w):
    sequence_count, complete_length, model_dim = inputs.shape
    token_count = sequence_count * complete_length
    group_size = H // KEY_VALUE_HEADS
    scale = 1.0 / math.sqrt(HEAD_SIZE)
    cosine, sine = rope_tables(positions(segments), HEAD_SIZE)
    attention_input = reduced_precision(rms_norm(inputs, gain_attn))
    query_rows = reduced_precision_backward(jnp.einsum('vew,wj->vej', attention_input, query_matrix, precision=TOP_PRECISION))
    key_projected = reduced_precision_backward(jnp.einsum('vew,wj->vej', attention_input, key_matrix, precision=TOP_PRECISION))
    value_rows = reduced_precision(reduced_precision_backward(jnp.einsum('vew,wj->vej', attention_input, value_matrix, precision=TOP_PRECISION))).reshape(sequence_count, complete_length, KEY_VALUE_HEADS, HEAD_SIZE)
    query_rows = reduced_precision(rotate(query_rows.reshape(sequence_count, complete_length, H, HEAD_SIZE), cosine, sine)).reshape(sequence_count, complete_length, KEY_VALUE_HEADS, group_size, HEAD_SIZE)
    key_projected = reduced_precision(rotate(key_projected.reshape(sequence_count, complete_length, KEY_VALUE_HEADS, HEAD_SIZE), cosine, sine))
    scores = reduced_precision_backward(scale * jnp.einsum('sqkgd,stkd->skgqt', query_rows, key_projected, precision=TOP_PRECISION))
    spots = jnp.arange(complete_length, dtype=jnp.int32)
    allowed = (segments[:, :, None] == segments[:, None, :]) & (spots[:, None] >= spots[None, :])
    masked = jnp.where(allowed[:, None, None], scores, FLOOR_SCORE)
    top_score = lax.optimization_barrier(jnp.max(masked, axis=-1, keepdims=True))
    lifted = jnp.exp(masked - top_score)
    shares = reduced_precision(lifted / lax.optimization_barrier(jnp.sum(lifted, axis=-1, keepdims=True)))
    mixed_result = jnp.einsum('skgqt,stkd->sqkgd', shares, value_rows, precision=TOP_PRECISION).reshape(sequence_count, complete_length, H * HEAD_SIZE)
    mixed_result = reduced_precision(reduced_precision_backward(mixed_result))
    attention_output = reduced_precision_backward(jnp.einsum('kgr,fr->kgf', mixed_result, output_matrix, precision=TOP_PRECISION))
    after_attn = inputs + attention_output
    moe_in = reduced_precision(rms_norm(after_attn, gain_moe)).reshape(token_count, model_dim)
    logits = jnp.dot(moe_in, router_w, precision=TOP_PRECISION, preferred_element_type=jnp.float32)
    chosen = jnp.take_along_axis(logits, routes_flat, axis=1)
    gate_lift = jnp.exp(chosen - lax.optimization_barrier(jnp.max(chosen, axis=1, keepdims=True)))
    gates = gate_lift / lax.optimization_barrier(jnp.sum(gate_lift, axis=1, keepdims=True))
    kept_pairs, pair_slot, slot_table = slot_plan(routes_flat, priority_flat, E, CAP)
    padded = jnp.concatenate([moe_in, jnp.zeros((1, model_dim), moe_in.dtype)], axis=0)
    picked = padded[slot_table]
    gate_pre = reduced_precision_backward(jnp.einsum('ecd,edf->ecf', picked, gate_w, precision=TOP_PRECISION))
    up_pre = reduced_precision_backward(jnp.einsum('ecd,edf->ecf', picked, up_w, precision=TOP_PRECISION))
    hidden = reduced_precision(jax.nn.silu(gate_pre) * up_pre)
    expert_out = reduced_precision_backward(jnp.einsum('ecf,edf->ecd', hidden, down_w, precision=TOP_PRECISION))
    gathered = expert_out[routes_flat, pair_slot]
    branch = lax.optimization_barrier(jnp.sum(jnp.where(kept_pairs, gates, 0.0)[:, :, None] * gathered, axis=1))
    branch = reduced_precision_backward(branch.reshape(sequence_count, complete_length, model_dim))
    return after_attn + branch

def reference(tokens, segments, routes, priority, norm_attn, w_query, w_key, w_value, w_out, norm_moe, w_router, w_gate, w_up, w_down, cotangent):
    params = tuple((weight.astype(jnp.float32) for weight in (norm_attn, w_query, w_key, w_value, w_out, norm_moe, w_router, w_gate, w_up, w_down)))
    seg_in = segments.reshape(N_DP, SEQS, LEN)
    route_in = routes.reshape(N_DP, SEQS * LEN, TOP)
    prio_in = priority.reshape(N_DP, SEQS * LEN)
    token_in = tokens.astype(jnp.float32).reshape(N_DP, SEQS, LEN, D)
    cot_in = cotangent.astype(jnp.float32).reshape(N_DP, SEQS, LEN, D)

    def group_step(totals, inputs):
        seg_group, route_group, prio_group, token_group, cot_group = inputs

        def primal(token_value, *weights):
            return forward_group(seg_group, route_group, prio_group, token_value, *weights)
        result, pullback = jax.vjp(primal, token_group, *params)
        gradients = pullback(cot_group)
        summed = tuple((total + grad for total, grad in zip(totals, gradients[1:])))
        return (summed, (result.astype(jnp.bfloat16), gradients[0]))
    start = tuple((jnp.zeros(weight.shape, jnp.float32) for weight in params))
    totals, (outputs, input_grads) = lax.scan(group_step, start, (seg_in, route_in, prio_in, token_in, cot_in))
    return (outputs.reshape(BATCH, LEN, D), input_grads.reshape(BATCH, LEN, D), totals[0], totals[1], totals[2], totals[3], totals[4], totals[5], totals[6], totals[7], totals[8], totals[9])
```

```python
import functools
import math

import jax
import jax.numpy as jnp
from jax import lax
from jax.experimental import pallas as pl
from jax.experimental.pallas import tpu as pltpu
from jax.sharding import Mesh, PartitionSpec as P

HEAD_SIZE = 64
EPSILON = 1e-06
FLOOR_SCORE = -1e30
VMEM_LIMIT = 60 * 1024 * 1024
DP = ("o", "u", "y")
POOL = ("u", "y", "x", "c")
ORDERS = (("u", "y", "x"), ("y", "x", "u"), ("x", "u", "y"))
PIECE = 384
BLK = 256
BF = jnp.bfloat16
F32 = jnp.float32


def swap(value, axis):
    return lax.ppermute(value, axis, [(0, 1), (1, 0)])


def mm(left, right):
    return lax.dot_general(left, right, (((1,), (0,)), ((), ())), preferred_element_type=F32)


def mm_nt(left, right):
    return lax.dot_general(left, right, (((1,), (1,)), ((), ())), preferred_element_type=F32)


def mm_tn(left, right):
    return lax.dot_general(left, right, (((0,), (0,)), ((), ())), preferred_element_type=F32)


def lanes(shape):
    return lax.broadcasted_iota(jnp.int32, shape, 1)


def turn_halves(value):
    first = lanes(value.shape) % HEAD_SIZE < HEAD_SIZE // 2
    half = HEAD_SIZE // 2
    return jnp.where(first, pltpu.roll(value, 128 - half, 1), pltpu.roll(value, half, 1))


def both_halves(value, which):
    low = lanes(value.shape) < HEAD_SIZE
    turned = pltpu.roll(value, HEAD_SIZE, 1)
    return jnp.where(low, value, turned) if which == 0 else jnp.where(low, turned, value)


def stack_heads(pair):
    low = lanes(pair.shape) < HEAD_SIZE
    zero = jnp.zeros_like(pair)
    return jnp.concatenate([jnp.where(low, pair, zero), jnp.where(low, zero, pair)], axis=0)


def join_heads(stacked):
    rows = stacked.shape[0] // 2
    low = lanes((rows, stacked.shape[1])) < HEAD_SIZE
    return jnp.where(low, stacked[:rows], stacked[rows:])


def allowed_keys(start_col, block, width):
    rows = start_col.shape[0]
    cols = lax.broadcasted_iota(jnp.int32, (rows, width), 1)
    row_ids = block * rows + lax.broadcasted_iota(jnp.int32, (rows, width), 0)
    keep = (cols >= start_col) & (cols <= row_ids)
    return jnp.concatenate([keep, keep], axis=0)


def attend_forward_kernel(
    table, offs, t0, t1, t2, t3, wa, wb, gain, cosine, sine, start,
    ain_o, wqkv_o, wob_o, q_o, kd_o, vd_o, mix_o, lse_o, keep_o, send_o,
):
    blocks, shard = wb.shape[0], wb.shape[1]
    for b in range(blocks):
        at = pl.multiple_of(table[b] * shard, shard)
        wqkv_o[pl.ds(at, shard), :] = wa[b, :shard, :]
        wob_o[pl.ds(at, shard), :] = wb[b]
    for r, piece in enumerate((t0, t1, t2, t3)):
        at = pl.multiple_of(offs[r], BLK)
        rows = pl.ds(at, BLK)
        value = piece[...].astype(F32)
        factor = lax.rsqrt(jnp.mean(value * value, axis=-1, keepdims=True) + EPSILON)
        normed = (value * factor * gain[...]).astype(BF)
        ain_o[rows, :] = normed
        qkv = mm(normed, wqkv_o[...])
        cos_b, sin_b = cosine[rows, :], sine[rows, :]
        for part in range(3):
            raw = qkv[:, part * 128 : part * 128 + 128]
            turned = (raw * cos_b + turn_halves(raw) * sin_b).astype(BF)
            if part < 2:
                q_o[rows, part * 128 : part * 128 + 128] = turned * 0.125
            else:
                wide = turned.astype(F32)
                for kv in range(2):
                    kd_o[kv, rows, :] = both_halves(wide, kv).astype(BF)
        value_rows = qkv[:, 384:512].astype(BF).astype(F32)
        for kv in range(2):
            vd_o[kv, rows, :] = both_halves(value_rows, kv).astype(BF)
    total = ain_o.shape[0]
    for block in range(total // BLK):
        width = (block + 1) * BLK
        rows = pl.ds(block * BLK, BLK)
        keep = allowed_keys(start[rows, :], block, width)
        logs = jnp.zeros((BLK, 128), F32)
        for kv in range(2):
            query = stack_heads(q_o[rows, kv * 128 : kv * 128 + 128])
            scores = jnp.where(keep, mm_nt(query, kd_o[kv, :width, :]), FLOOR_SCORE)
            top = jnp.max(scores, axis=-1, keepdims=True)
            lifted = jnp.exp(scores - top)
            summed = jnp.sum(lifted, axis=-1, keepdims=True)
            shares = (lifted * (1.0 / summed)).astype(BF)
            mixed = join_heads(mm(shares, vd_o[kv, :width, :]))
            mix_o[rows, kv * 128 : kv * 128 + 128] = mixed.astype(BF)
            log_total = top + jnp.log(summed)
            lane = lanes(logs.shape)
            logs = jnp.where(lane == 2 * kv, log_total[:BLK], logs)
            logs = jnp.where(lane == 2 * kv + 1, log_total[BLK:], logs)
        lse_o[rows, :] = logs
    for r in range(4):
        rows = pl.ds(pl.multiple_of(offs[r], BLK), BLK)
        part = mm_nt(mix_o[rows, :], wob_o[:, :256])
        if r % 2 == 0:
            keep_o[r // 2] = part
        else:
            send_o[r // 2] = part.astype(BF)


def attend_backward_kernel(
    offs, a0, a1, a2, a3, wqkv, wob, q, kd, vd, mix, lse, start, ain, cosine, sine,
    keep_o, send_o, wg_o, og_o, gcol_o, aog, mgrad, dqkv, dk, dv,
):
    total = ain.shape[0]
    for r, piece in enumerate((a0, a1, a2, a3)):
        aog[pl.ds(pl.multiple_of(offs[r], BLK), BLK), :] = piece[...]
    mgrad[...] = mm(aog[...], wob[:, :256]).astype(BF)
    og_o[...] = mm_tn(aog[...], mix[...])
    dk[...] = jnp.zeros_like(dk)
    dv[...] = jnp.zeros_like(dv)
    for block in range(total // BLK):
        width = (block + 1) * BLK
        rows = pl.ds(block * BLK, BLK)
        keep = allowed_keys(start[rows, :], block, width)
        logs = lse[rows, :]
        lane = lanes(logs.shape)
        cos_b, sin_b = cosine[rows, :], sine[rows, :]
        for kv in range(2):
            cols = slice(kv * 128, kv * 128 + 128)
            query = stack_heads(q[rows, cols])
            out_grad = stack_heads(mgrad[rows, cols])
            log_total = jnp.concatenate(
                [
                    jnp.sum(jnp.where(lane == 2 * kv + h, logs, 0.0), axis=1, keepdims=True)
                    for h in range(2)
                ],
                axis=0,
            )
            keys = kd[kv, :width, :]
            scores = jnp.where(keep, mm_nt(query, keys), FLOOR_SCORE)
            shares = jnp.exp(scores - log_total)
            share_grad = mm_nt(out_grad, vd[kv, :width, :])
            inner = jnp.sum(shares * share_grad, axis=-1, keepdims=True)
            score_grad = (shares * (share_grad - inner)).astype(BF)
            query_grad = join_heads(mm(score_grad, keys)) * 0.125
            query_grad = query_grad * cos_b - turn_halves(query_grad) * sin_b
            dqkv[rows, cols] = query_grad.astype(BF)
            dk[kv, :width, :] += mm_tn(score_grad, query)
            dv[kv, :width, :] += mm_tn(shares.astype(BF), out_grad)
    joined = []
    for acc in (dk, dv):
        pair = [acc[kv] + pltpu.roll(acc[kv], HEAD_SIZE, 1) for kv in range(2)]
        joined.append(jnp.where(lanes(pair[0].shape) < HEAD_SIZE, pair[0], pair[1]))
    key_grad = joined[0] * cosine[...] - turn_halves(joined[0]) * sine[...]
    dqkv[:, 256:384] = key_grad.astype(BF)
    dqkv[:, 384:512] = joined[1].astype(BF)
    wg_o[...] = mm_tn(ain[...], dqkv[...]).astype(BF)
    ones = jnp.ones((BLK, 128), BF)
    gain_sum = jnp.zeros(gcol_o.shape, F32)
    for r in range(4):
        rows = pl.ds(pl.multiple_of(offs[r], BLK), BLK)
        part = mm_nt(dqkv[rows, :], wqkv[...])
        gain_sum += mm_tn((part * ain[rows, :].astype(F32)).astype(BF), ones)
        if r % 2 == 0:
            keep_o[r // 2] = part
        else:
            send_o[r // 2] = part.astype(BF)
    gcol_o[...] = gain_sum.astype(BF)


def route_kernel(tok, keep, got, cross, gain, wr, routes, after_o, ma_o, mb_o, mc_o, gates_o):
    after = tok[...].astype(F32) + (keep[0] + got[0].astype(F32) + cross[...].astype(F32))
    after_o[...] = after
    factor = lax.rsqrt(jnp.mean(after * after, axis=-1, keepdims=True) + EPSILON)
    moe_in = (after * factor * gain[...]).astype(BF)
    logits = mm(moe_in, wr[...])
    lane = lanes(logits.shape)
    routed = lane < 0
    for k in range(routes.shape[1]):
        routed = routed | (routes[:, k : k + 1] == lane)
    top = jnp.max(jnp.where(routed, logits, FLOOR_SCORE), axis=1, keepdims=True)
    lifted = jnp.where(routed, jnp.exp(jnp.where(routed, logits - top, 0.0)), 0.0)
    gates = lifted / jnp.sum(lifted, axis=1, keepdims=True)
    gates_o[...] = gates
    high = gates.astype(BF).astype(F32)
    middle = (gates - high).astype(BF).astype(F32)
    low = gates - high - middle
    extra = high + pltpu.roll(middle, 32, 1) + pltpu.roll(low, 64, 1)
    ma_o[...] = moe_in[:, :PIECE]
    mb_o[...] = moe_in[:, PIECE : 2 * PIECE]
    mc_o[:, : PIECE - 128] = moe_in[:, 2 * PIECE :]
    mc_o[:, PIECE - 128 :] = extra.astype(BF)


def expert_kernel(n_weights, n_sends, first, meta, *refs):
    refs = list(refs)
    take = lambda n: [refs.pop(0) for _ in range(n)]
    tok_k, tok_c = take(3), take(3)
    dy_k, dy_c = take(3), take(3)
    (rank,) = take(1)
    weights = take(n_weights)
    prev = [] if first else take(12)
    outs = take(12)
    grads = take(n_sends)
    mat, acc, pick_s, dy_s, pre_s = take(5)
    step = pl.program_id(0)
    shard = weights[0].shape[2]
    hidden = mat.shape[1] // 3
    own_expert = meta[0]

    @pl.when(step == 0)
    def _():
        for i, buf in enumerate(weights):
            for b in range(buf.shape[0]):
                at = pl.multiple_of(meta[1 + i] + b // 4 * shard, shard)
                for m in range(3):
                    col = m * hidden + b % 4 * 128
                    mat[pl.ds(at, shard), col : col + 128] = buf[b, m]
        acc[...] = jnp.zeros_like(acc)

    slots = BLK
    row_ids = lax.broadcasted_iota(jnp.int32, (slots, rank.shape[-1]), 0)
    pick = jnp.where(rank[0] == row_ids, 1.0, 0.0).astype(BF)
    half = rank.shape[-1] // 2
    pick_k, pick_c = pick[:, :half], pick[:, half:]

    def gather(kept, other):
        flat = lambda ref: ref[...].reshape(half, ref.shape[-1])
        return mm(pick_k, flat(kept)) + mm(pick_c, flat(other))

    last = None
    for i in range(3):
        got = gather(tok_k[i], tok_c[i])
        width = min(PIECE, pick_s.shape[1] - i * PIECE)
        pick_s[:, i * PIECE : i * PIECE + width] = got[:, :width].astype(BF)
        last = got
        got = gather(dy_k[i], dy_c[i])
        dy_s[:, i * PIECE : i * PIECE + width] = got[:, :width].astype(BF)
    extra = last[:, PIECE - 128 :]
    lane = lanes(extra.shape)
    mine = (lane % 32 == own_expert) & (lane < 96)
    gate = jnp.sum(jnp.where(mine, extra, 0.0), axis=1, keepdims=True)
    picked, dy = pick_s[...], dy_s[...]
    gate_pre = mm(picked, mat[:, :hidden])
    up_pre = mm(picked, mat[:, hidden : 2 * hidden])
    back = mm(dy, mat[:, 2 * hidden :])
    sigma = 1.0 / (1.0 + jnp.exp(-gate_pre))
    active = gate_pre * sigma
    hid = active * up_pre
    gate_dot = jnp.sum(hid.astype(BF).astype(F32) * back, axis=1, keepdims=True)
    weighted = (gate * hid).astype(BF)
    back = back * gate
    pre_s[:, :hidden] = (back * up_pre * sigma * (1.0 + gate_pre * (1.0 - sigma))).astype(BF)
    pre_s[:, hidden:] = (back * active).astype(BF)
    pre_grad = pre_s[...]
    picked_grad = mm_nt(pre_grad, mat[:, : 2 * hidden]).astype(BF)
    expert_out = mm_nt(weighted, mat[:, 2 * hidden :]).astype(BF)
    acc[:, : 2 * hidden] += mm_tn(picked, pre_grad)
    acc[:, 2 * hidden :] += mm_tn(dy, weighted)
    dot_high = gate_dot.astype(BF).astype(F32)
    dot_low = gate_dot - dot_high
    note = jnp.where(lane == own_expert, dot_high, 0.0)
    note = jnp.where(lane == own_expert + 32, dot_low, note).astype(BF)

    def put(place, side, chosen, value):
        index = place + 3 * side
        summed = mm_tn(chosen, value)
        if not first:
            summed += prev[index][...].reshape(summed.shape).astype(F32)
        outs[index][...] = summed.astype(BF).reshape(outs[index].shape)

    for side, chosen in ((1, pick_c), (0, pick_k)):
        for i in range(3):
            part = picked_grad[:, i * PIECE : (i + 1) * PIECE]
            if i == 2:
                part = jnp.concatenate([part, note], axis=1)
            put(i, side, chosen, part)
            put(6 + i, side, chosen, expert_out[:, i * PIECE : (i + 1) * PIECE])

    @pl.when(step == pl.num_programs(0) - 1)
    def _():
        for i, buf in enumerate(grads):
            for b in range(buf.shape[0]):
                at = pl.multiple_of(meta[1 + i] + b // 4 * shard, shard)
                for m in range(3):
                    col = m * hidden + b % 4 * 128
                    buf[b, m] = acc[pl.ds(at, shard), col : col + 128].astype(BF)


def back_kernel(
    after, ak, ar, bk, br, ck, cr, gain, wr, gates, cot, after_grad_o, aog_o, small_o
):
    both = lambda a, b: a[...].astype(F32) + b[...].astype(F32)
    last = both(ck, cr)
    upstream = jnp.concatenate([both(ak, ar), both(bk, br), last[:, : PIECE - 128]], axis=1)
    extra = last[:, PIECE - 128 :]
    lane = lanes(extra.shape)
    gate_dot = jnp.where(lane < 32, extra + pltpu.roll(extra, 96, 1), 0.0)
    share = gates[...]
    logit_grad = share * (gate_dot - jnp.sum(share * gate_dot, axis=1, keepdims=True))
    high = logit_grad.astype(BF)
    low = (logit_grad - high.astype(F32)).astype(BF)
    router = wr[...]
    upstream += mm_nt(high, router) + mm_nt(low, router)
    value = after[...]
    factor = lax.rsqrt(jnp.mean(value * value, axis=-1, keepdims=True) + EPSILON)
    normed = value * factor
    moe_in = (normed * gain[...]).astype(BF)
    scaled = upstream * gain[...]
    inward = factor * (scaled - normed * jnp.mean(scaled * normed, axis=-1, keepdims=True))
    after_grad = cot[...].astype(F32) + inward
    after_grad_o[...] = after_grad
    aog_o[...] = after_grad.astype(BF)
    column = jnp.where(lane == 32, 1.0, 0.0).astype(BF)
    small_o[...] = (
        mm_tn(moe_in, high) + mm_tn(moe_in, low) + mm_tn((upstream * normed).astype(BF), column)
    )


def finish_kernel(tok, keep, got, cross, gain, after_grad, out):
    upstream = keep[0] + got[0].astype(F32) + cross[...].astype(F32)
    value = tok[...].astype(F32)
    factor = lax.rsqrt(jnp.mean(value * value, axis=-1, keepdims=True) + EPSILON)
    normed = value * factor
    scaled = upstream * gain[...]
    inward = factor * (scaled - normed * jnp.mean(scaled * normed, axis=-1, keepdims=True))
    out[...] = after_grad[...] + inward


def spec_of(space):
    return pl.BlockSpec(memory_space=space)


def simple_call(kernel, outs, n_scalar, n_in, scratch=(), flops=0, moved=0):
    return pl.pallas_call(
        kernel,
        out_shape=[jax.ShapeDtypeStruct(s, d) for s, d in outs],
        in_specs=[spec_of(pltpu.SMEM)] * n_scalar + [spec_of(pltpu.VMEM)] * n_in,
        out_specs=[spec_of(pltpu.VMEM)] * len(outs),
        scratch_shapes=list(scratch),
        compiler_params=pltpu.CompilerParams(vmem_limit_bytes=VMEM_LIMIT),
        cost_estimate=pl.CostEstimate(flops=flops, bytes_accessed=moved, transcendentals=0),
    )


def gather_dp(value, count):
    me = lax.axis_index(DP)
    if count <= 8:
        parts = [value]
        for s in range(1, count):
            parts.append(lax.ppermute(value, DP, [((i + s) % count, i) for i in range(count)]))
        return jnp.stack(parts), (me + jnp.arange(count, dtype=jnp.int32)) % count
    return lax.all_gather(value, DP, axis=0), jnp.arange(count, dtype=jnp.int32)


def gather_pool(pieces):
    kept, other = [], []
    for piece, order in zip(pieces, ORDERS):
        buf = piece
        for axis in order:
            buf = jnp.stack([buf, swap(buf, axis)])
        kept.append(buf)
        other.append(swap(buf, "c"))
    return kept, other


def scatter_pool(kept, other):
    pairs = []
    for keep, send, order in zip(kept, other, ORDERS):
        buf = keep.astype(F32) + swap(send, "c").astype(F32)
        for axis in reversed(order[1:]):
            buf = buf[0] + swap(buf[1].astype(BF), axis).astype(F32)
        pairs.append((buf[0].astype(BF), swap(buf[1].astype(BF), order[0])))
    return pairs


def gather_tensor(value):
    cross = swap(value, "x")
    return [value, swap(value, "c"), cross, swap(cross, "c")]


def sum_tensor(keep, send):
    got = swap(send, "c")
    cross = swap((keep[1] + got[1].astype(F32)).astype(BF), "x")
    return got, cross


def pool_spec(order, width):
    shape = tuple(2 if axis == "x" else 1 for axis in reversed(order)) + (BLK, width)
    zero = jnp.int32(0)

    def index(g):
        place = {"x": 0, "u": g // 2, "y": g % 2}
        return tuple(place[axis] for axis in reversed(order)) + (0, 0)

    del zero
    return pl.BlockSpec(shape, index)


def local(
    tokens, segments, routes, priority, norm_attn, w_query, w_key, w_value, w_out, norm_moe,
    w_router, w_gate, w_up, w_down, cotangent,
):
    _, rows, dim = tokens.shape
    n_outer = lax.axis_size("o")
    n_dp = 4 * n_outer
    shard = w_query.shape[0]
    length = 4 * rows
    top = routes.shape[2]
    experts = w_gate.shape[0]
    per_device = experts // 16
    capacity = length * top // experts
    hidden = 4 * w_gate.shape[2]
    at_x, at_c = lax.axis_index("x"), lax.axis_index("c")
    at_t = at_x * 2 + at_c
    at_o = lax.axis_index("o")
    at_pool = lax.axis_index(POOL)

    tok = tokens[0]
    cot = cotangent[0]
    tok_parts = gather_tensor(tok)
    gains = jnp.zeros((16, 512), BF)
    gains = gains.at[0, :shard].set(norm_attn).at[0, shard : 2 * shard].set(norm_moe)
    pack_a = jnp.concatenate([jnp.concatenate([w_query, w_key, w_value], axis=1), gains], axis=0)
    pack_b = jnp.concatenate([w_out, w_router, jnp.zeros((shard, 128 - experts), BF)], axis=1)
    wa, table = gather_dp(pack_a, n_dp)
    wb, _ = gather_dp(pack_b, n_dp)
    both_gains = wa[:, shard, : 2 * shard].astype(F32)
    if n_dp <= 8:
        both_gains = lax.dynamic_slice_in_dim(
            jnp.concatenate([both_gains, both_gains], axis=0), n_dp - table[0], n_dp, 0
        )
    gain_attn = both_gains[:, :shard].reshape(1, dim)
    gain_moe = both_gains[:, shard:].reshape(1, dim)

    expert_mats, bases = [], None
    for j in range(per_device):
        part = jnp.stack([w[j * 16 : (j + 1) * 16] for w in (w_gate, w_up, w_down)], axis=1)
        part = lax.all_to_all(part, POOL, 0, 0, tiled=True)
        if n_outer == 2:
            expert_mats.append([part, swap(part, "o")])
            bases = [at_o * 4 * shard, (1 - at_o) * 4 * shard]
        else:
            expert_mats.append([lax.all_gather(part, "o", axis=0, tiled=True)])
            bases = [jnp.int32(0)]

    seg = segments[0]
    start = jnp.zeros_like(seg)
    for s in range(1, 5):
        start = jnp.where(seg >= s, jnp.sum((seg < s).astype(jnp.int32)), start)
    place = (jnp.arange(length, dtype=jnp.int32) - start).astype(F32)
    lane = jnp.arange(128, dtype=jnp.int32)
    half = HEAD_SIZE // 2
    inverse = jnp.exp((lane % half).astype(F32) * (-2.0 * math.log(10000.0) / HEAD_SIZE))
    angle = place[:, None] * inverse[None, :]
    cosine = jnp.cos(angle)
    sine = jnp.sin(angle) * jnp.where(lane % HEAD_SIZE < half, -1.0, 1.0)
    start_col = start[:, None]

    plan = jnp.concatenate([routes[0].T, priority], axis=0)
    plan = plan.reshape(top + 1, 2, 2, rows)
    plan = jnp.where(at_x == 1, plan[:, ::-1], plan)
    plan = jnp.where(at_c == 1, plan[:, :, ::-1], plan)
    plan = plan.swapaxes(1, 2).reshape(top + 1, length)
    plan = jnp.stack([plan, swap(plan, "y")])
    plan = jnp.concatenate([plan, swap(plan, "u")], axis=0)
    own = [j * 16 + at_pool for j in range(per_device)]
    hits = jnp.stack([jnp.any(plan[:, :top] == e, axis=1) for e in own], axis=1)
    first = plan[:, top]
    less = (first[:, :, None] < first[:, None, :]).astype(BF)
    rank = jnp.einsum("gjs,gst->gjt", hits.astype(BF), less, preferred_element_type=F32)
    rank = rank.astype(jnp.int32)
    rank = jnp.where(hits & (rank < capacity), rank, -1)

    table = table.astype(jnp.int32)
    offs = (jnp.bitwise_xor(at_t, jnp.arange(4, dtype=jnp.int32)) * rows).astype(jnp.int32)
    heads = w_query.shape[1]
    ain, wqkv, wob, q, kd, vd, mix, lse, keep, send = simple_call(
        attend_forward_kernel,
        [
            ((length, dim), BF),
            ((dim, 512), BF),
            ((dim, PIECE), BF),
            ((length, heads), BF),
            ((2, length, 128), BF),
            ((2, length, 128), BF),
            ((length, heads), BF),
            ((length, 128), F32),
            ((2, rows, dim), F32),
            ((2, rows, dim), BF),
        ],
        2,
        10,
        flops=3 * 10**9,
        moved=16 * 2**20,
    )(table, offs, *tok_parts, wa, wb, gain_attn, cosine, sine, start_col)

    got, cross = sum_tensor(keep, send)
    route_col = lax.dynamic_slice_in_dim(routes[0], at_t * rows, rows, 0)
    router = wob[:, 256:]
    after, ma, mb, mc, gates = simple_call(
        route_kernel,
        [
            ((rows, dim), F32),
            ((rows, PIECE), BF),
            ((rows, PIECE), BF),
            ((rows, PIECE), BF),
            ((rows, 128), F32),
        ],
        0,
        7,
        flops=10**8,
        moved=4 * 2**20,
    )(tok, keep, got, cross, gain_moe, router, route_col)

    dy_kept, dy_other = gather_pool([cot[:, i * PIECE : (i + 1) * PIECE] for i in range(3)])
    tok_kept, tok_other = gather_pool([ma, mb, mc])

    widths = [PIECE, PIECE, PIECE]
    dy_widths = [PIECE, PIECE, dim - 2 * PIECE]
    tok_specs = [pool_spec(o, w) for o, w in zip(ORDERS, widths)]
    dy_specs = [pool_spec(o, w) for o, w in zip(ORDERS, dy_widths)]
    out_specs = tok_specs * 2 + dy_specs * 2
    out_shapes = [jax.ShapeDtypeStruct((2, 2, 2, rows, w), BF) for w in widths * 2 + dy_widths * 2]
    prev = []
    weight_grads = []
    for j in range(per_device):
        mats = expert_mats[j]
        whole = [pl.BlockSpec(m.shape, lambda g: (0, 0, 0, 0), pipeline_mode=pl.Buffered(1)) for m in mats]
        meta = jnp.stack([own[j]] + bases).astype(jnp.int32)
        result = pl.pallas_call(
            functools.partial(expert_kernel, len(mats), len(mats), j == 0),
            grid=(4,),
            in_specs=[spec_of(pltpu.SMEM)]
            + tok_specs * 2
            + dy_specs * 2
            + [pl.BlockSpec((1, 1, length), lambda g: (g, 0, 0))]
            + whole
            + (out_specs if prev else []),
            out_specs=out_specs + whole,
            out_shape=out_shapes + [jax.ShapeDtypeStruct(m.shape, BF) for m in mats],
            scratch_shapes=[
                pltpu.VMEM((dim, 3 * hidden), BF),
                pltpu.VMEM((dim, 3 * hidden), F32),
                pltpu.VMEM((capacity, dim), BF),
                pltpu.VMEM((capacity, dim), BF),
                pltpu.VMEM((capacity, 2 * hidden), BF),
            ],
            compiler_params=pltpu.CompilerParams(vmem_limit_bytes=VMEM_LIMIT),
            cost_estimate=pl.CostEstimate(flops=19 * 10**9, bytes_accessed=48 * 2**20, transcendentals=0),
        )(meta, *tok_kept, *tok_other, *dy_kept, *dy_other, rank[:, j : j + 1], *mats, *prev)
        prev = result[:12]
        weight_grads.append(result[12:])

    pairs = scatter_pool(prev[:3], prev[3:6])
    out_pairs = scatter_pool(prev[6:9], prev[9:12])

    after_grad, aog, small = simple_call(
        back_kernel,
        [((rows, dim), F32), ((rows, dim), BF), ((dim, 128), F32)],
        0,
        11,
        flops=10**9,
        moved=6 * 2**20,
    )(after, *pairs[0], *pairs[1], *pairs[2], gain_moe, router, gates, cot)
    aog_parts = gather_tensor(aog)

    keep, send, wg, og, gcol = simple_call(
        attend_backward_kernel,
        [
            ((2, rows, dim), F32),
            ((2, rows, dim), BF),
            ((dim, 512), BF),
            ((dim, 256), F32),
            ((dim, 128), BF),
        ],
        1,
        15,
        scratch=[
            pltpu.VMEM((length, dim), BF),
            pltpu.VMEM((length, heads), BF),
            pltpu.VMEM((length, 512), BF),
            pltpu.VMEM((2, length, 128), F32),
            pltpu.VMEM((2, length, 128), F32),
        ],
        flops=9 * 10**9,
        moved=20 * 2**20,
    )(offs, *aog_parts, wqkv, wob, q, kd, vd, mix, lse, start_col, ain, cosine, sine)

    got, cross = sum_tensor(keep, send)
    tokens_grad = simple_call(
        finish_kernel, [((rows, dim), F32)], 0, 6, flops=10**7, moved=6 * 2**20
    )(tok, keep, got, cross, gain_attn, after_grad)[0]

    moe_out = jnp.concatenate([a.astype(F32) + b.astype(F32) for a, b in out_pairs], axis=1)
    block_out = (after + moe_out).astype(BF)

    side = lax.psum_scatter(
        jnp.concatenate([og, small], axis=1), DP, scatter_dimension=0, tiled=True
    )
    tail = jnp.concatenate([wg, gcol], axis=1).reshape(n_dp, shard, 640)
    tail = jnp.sum(lax.all_to_all(tail, DP, 0, 0, tiled=True).astype(F32), axis=0)
    narrow = jnp.concatenate([side[:, 256 : 256 + experts + 1], tail[:, 512:513]], axis=1)
    narrow = narrow + swap(narrow, "x")
    narrow = narrow + swap(narrow, "c")
    moved = []
    for j in range(per_device):
        if n_outer == 2:
            mine, sent = weight_grads[j]
            summed = (mine.astype(F32) + swap(sent, "o").astype(F32)).astype(BF)
        else:
            summed = lax.psum_scatter(weight_grads[j][0], "o", scatter_dimension=0, tiled=True)
        moved.append(lax.all_to_all(summed, POOL, 0, 0, tiled=True))
    gate_grad, up_grad, down_grad = (
        jnp.concatenate([part[:, m] for part in moved], axis=0).astype(F32) for m in range(3)
    )
    return (
        block_out[None],
        tokens_grad[None],
        narrow[:, experts + 1] / norm_attn.astype(F32),
        tail[:, :256],
        tail[:, 256:384],
        tail[:, 384:512],
        side[:, :256],
        narrow[:, experts],
        narrow[:, :experts],
        gate_grad,
        up_grad,
        down_grad,
    )


def solution(mesh):
    devices = mesh.devices
    fine = Mesh(devices.reshape(devices.shape[0] // 4, 2, 2, 2, 2), ("o", "u", "y", "x", "c"))
    dp, tensor = DP, ("x", "c")
    in_specs = (
        P(dp, tensor, None),
        P(dp, None),
        P(dp, None, None),
        P(dp, None),
        P(dp),
        P(dp, tensor),
        P(dp, tensor),
        P(dp, tensor),
        P(dp, tensor),
        P(dp),
        P(dp, None),
        P(None, dp, tensor),
        P(None, dp, tensor),
        P(None, dp, tensor),
        P(dp, tensor, None),
    )
    out_specs = (
        P(dp, tensor, None),
        P(dp, tensor, None),
        P(dp),
        P(dp, tensor),
        P(dp, tensor),
        P(dp, tensor),
        P(dp, tensor),
        P(dp),
        P(dp, None),
        P(None, dp, tensor),
        P(None, dp, tensor),
        P(None, dp, tensor),
    )
    return jax.shard_map(local, mesh=fine, in_specs=in_specs, out_specs=out_specs, check_vma=False)
```

```python
import functools
import math

import jax
import jax.numpy as jnp
from jax import lax
from jax.experimental import pallas as pl
from jax.experimental.pallas import tpu as pltpu
from jax.sharding import Mesh, PartitionSpec as P

HEAD_SIZE = 64
EPSILON = 1e-06
FLOOR_SCORE = -1e30
VMEM_LIMIT = 60 * 1024 * 1024
DP = ("o", "u", "y")
POOL = ("u", "y", "x", "c")
ORDERS = (("u", "y", "x"), ("y", "x", "u"), ("x", "u", "y"))
TOK = (512, 256, 256)
SECOND = (384, 256, 384)
NOTES = 128
BLK = 256
BF = jnp.bfloat16
F32 = jnp.float32


def after_all(value, *others):
    return lax.optimization_barrier((value,) + others)[0]


def together(values, *others):
    return lax.optimization_barrier((*values, *others))[: len(values)]


def cuts(dim):
    found, a, b = [], 0, 0
    for i, (first, second) in enumerate(zip(TOK, SECOND)):
        found.append((a, a + first, b, b + second, first + (NOTES if i == 2 else 0)))
        a, b = a + first, b + second
    assert a == b == dim
    return found


def swap(value, axis):
    return lax.ppermute(value, axis, [(0, 1), (1, 0)])


def mm(left, right):
    return lax.dot_general(left, right, (((1,), (0,)), ((), ())), preferred_element_type=F32)


def mm_nt(left, right):
    return lax.dot_general(left, right, (((1,), (1,)), ((), ())), preferred_element_type=F32)


def mm_tn(left, right):
    return lax.dot_general(left, right, (((0,), (0,)), ((), ())), preferred_element_type=F32)


def lanes(shape):
    return lax.broadcasted_iota(jnp.int32, shape, 1)


def turn_halves(value):
    first = lanes(value.shape) % HEAD_SIZE < HEAD_SIZE // 2
    half = HEAD_SIZE // 2
    return jnp.where(first, pltpu.roll(value, 128 - half, 1), pltpu.roll(value, half, 1))


def both_halves(value, which):
    low = lanes(value.shape) < HEAD_SIZE
    turned = pltpu.roll(value, HEAD_SIZE, 1)
    return jnp.where(low, value, turned) if which == 0 else jnp.where(low, turned, value)


def stack_heads(pair):
    low = lanes(pair.shape) < HEAD_SIZE
    zero = jnp.zeros_like(pair)
    return jnp.concatenate([jnp.where(low, pair, zero), jnp.where(low, zero, pair)], axis=0)


def join_heads(stacked):
    rows = stacked.shape[0] // 2
    low = lanes((rows, stacked.shape[1])) < HEAD_SIZE
    return jnp.where(low, stacked[:rows], stacked[rows:])


def allowed_keys(start_col, block, width):
    rows = start_col.shape[0]
    cols = lax.broadcasted_iota(jnp.int32, (rows, width), 1)
    row_ids = block * rows + lax.broadcasted_iota(jnp.int32, (rows, width), 0)
    keep = (cols >= start_col) & (cols <= row_ids)
    return jnp.concatenate([keep, keep], axis=0)


def attend_forward_kernel(n_parts, shard, table, offs, t0, t1, t2, t3, *refs):
    parts, refs = refs[:n_parts], refs[n_parts:]
    gain_in, cosine, sine, start, ain_o, wqkv_o, gains_o, q_o, kd_o, vd_o, mix_o, lse_o = refs
    gains_o[...] = gain_in[...]
    base = 0
    for part in parts:
        for b in range(part.shape[0]):
            at = pl.multiple_of(table[base + b] * shard, shard)
            wqkv_o[pl.ds(at, shard), :] = part[b, :shard, :]
            if shard == 128:
                note = part[b, shard:, :].astype(F32)
                for row in range(2):
                    gains_o[row : row + 1, pl.ds(at, 128)] = note[row : row + 1, :128]
        base += part.shape[0]
    gain = gains_o[0:1, :]
    for r, piece in enumerate((t0, t1, t2, t3)):
        at = pl.multiple_of(offs[r], BLK)
        rows = pl.ds(at, BLK)
        value = piece[...].astype(F32)
        factor = lax.rsqrt(jnp.mean(value * value, axis=-1, keepdims=True) + EPSILON)
        normed = (value * factor * gain).astype(BF)
        ain_o[rows, :] = normed
        qkv = mm(normed, wqkv_o[...])
        cos_b, sin_b = cosine[rows, :], sine[rows, :]
        for part in range(3):
            raw = qkv[:, part * 128 : part * 128 + 128]
            turned = (raw * cos_b + turn_halves(raw) * sin_b).astype(BF)
            if part < 2:
                q_o[rows, part * 128 : part * 128 + 128] = turned * 0.125
            else:
                wide = turned.astype(F32)
                for kv in range(2):
                    kd_o[kv, rows, :] = both_halves(wide, kv).astype(BF)
        value_rows = qkv[:, 384:512].astype(BF).astype(F32)
        for kv in range(2):
            vd_o[kv, rows, :] = both_halves(value_rows, kv).astype(BF)
    total = ain_o.shape[0]
    for block in range(total // BLK):
        width = (block + 1) * BLK
        rows = pl.ds(block * BLK, BLK)
        keep = allowed_keys(start[rows, :], block, width)
        logs = jnp.zeros((BLK, 128), F32)
        for kv in range(2):
            query = stack_heads(q_o[rows, kv * 128 : kv * 128 + 128])
            scores = jnp.where(keep, mm_nt(query, kd_o[kv, :width, :]), FLOOR_SCORE)
            top = jnp.max(scores, axis=-1, keepdims=True)
            lifted = jnp.exp(scores - top)
            summed = jnp.sum(lifted, axis=-1, keepdims=True)
            shares = (lifted * (1.0 / summed)).astype(BF)
            mixed = join_heads(mm(shares, vd_o[kv, :width, :]))
            mix_o[rows, kv * 128 : kv * 128 + 128] = mixed.astype(BF)
            log_total = top + jnp.log(summed)
            lane = lanes(logs.shape)
            logs = jnp.where(lane == 2 * kv, log_total[:BLK], logs)
            logs = jnp.where(lane == 2 * kv + 1, log_total[BLK:], logs)
        lse_o[rows, :] = logs


def project_kernel(n_parts, table, offs, mix, *refs):
    parts, (keep_o, send_o, wob) = refs[:n_parts], refs[n_parts:]
    base = 0
    for part in parts:
        shard = part.shape[1]
        for b in range(part.shape[0]):
            wob[pl.ds(pl.multiple_of(table[base + b] * shard, shard), shard), :] = part[b]
        base += part.shape[0]
    for r in range(4):
        rows = pl.ds(pl.multiple_of(offs[r], BLK), BLK)
        part = mm_nt(mix[rows, :], wob[:, :256])
        if r % 2 == 0:
            keep_o[r // 2] = part
        else:
            send_o[r // 2] = part.astype(BF)


def attend_backward_kernel(
    n_blocks, dests, offs, a0, a1, a2, a3, wqkv, wob, q, kd, vd, lse, start, ain, cosine, sine,
    keep_o, send_o, *refs,
):
    wg_o, (aog, mgrad, dqkv, dk, dv, flat) = refs[:n_blocks], refs[n_blocks:]
    total = ain.shape[0]
    for r, piece in enumerate((a0, a1, a2, a3)):
        aog[pl.ds(pl.multiple_of(offs[r], BLK), BLK), :] = piece[...]
    mgrad[...] = mm(aog[...], wob[:, :256]).astype(BF)
    dk[...] = jnp.zeros_like(dk)
    dv[...] = jnp.zeros_like(dv)
    for block in range(total // BLK):
        width = (block + 1) * BLK
        rows = pl.ds(block * BLK, BLK)
        keep = allowed_keys(start[rows, :], block, width)
        logs = lse[rows, :]
        lane = lanes(logs.shape)
        cos_b, sin_b = cosine[rows, :], sine[rows, :]
        for kv in range(2):
            cols = slice(kv * 128, kv * 128 + 128)
            query = stack_heads(q[rows, cols])
            out_grad = stack_heads(mgrad[rows, cols])
            log_total = jnp.concatenate(
                [
                    jnp.sum(jnp.where(lane == 2 * kv + h, logs, 0.0), axis=1, keepdims=True)
                    for h in range(2)
                ],
                axis=0,
            )
            keys = kd[kv, :width, :]
            scores = jnp.where(keep, mm_nt(query, keys), FLOOR_SCORE)
            shares = jnp.exp(scores - log_total)
            share_grad = mm_nt(out_grad, vd[kv, :width, :])
            inner = jnp.sum(shares * share_grad, axis=-1, keepdims=True)
            score_grad = (shares * (share_grad - inner)).astype(BF)
            query_grad = join_heads(mm(score_grad, keys)) * 0.125
            query_grad = query_grad * cos_b - turn_halves(query_grad) * sin_b
            dqkv[rows, cols] = query_grad.astype(BF)
            dk[kv, :width, :] += mm_tn(score_grad, query)
            dv[kv, :width, :] += mm_tn(shares.astype(BF), out_grad)
    joined = []
    for acc in (dk, dv):
        pair = [acc[kv] + pltpu.roll(acc[kv], HEAD_SIZE, 1) for kv in range(2)]
        joined.append(jnp.where(lanes(pair[0].shape) < HEAD_SIZE, pair[0], pair[1]))
    key_grad = joined[0] * cosine[...] - turn_halves(joined[0]) * sine[...]
    dqkv[:, 256:384] = key_grad.astype(BF)
    dqkv[:, 384:512] = joined[1].astype(BF)
    flat[:, :512] = mm_tn(ain[...], dqkv[...]).astype(BF)
    ones = jnp.ones((BLK, 128), BF)
    gain_sum = jnp.zeros((ain.shape[1], 128), F32)
    for r in range(4):
        rows = pl.ds(pl.multiple_of(offs[r], BLK), BLK)
        part = mm_nt(dqkv[rows, :], wqkv[...])
        gain_sum += mm_tn((part * ain[rows, :].astype(F32)).astype(BF), ones)
        if r % 2 == 0:
            keep_o[r // 2] = part
        else:
            send_o[r // 2] = part.astype(BF)
    flat[:, 512:] = gain_sum.astype(BF)
    spread(flat, dests, wg_o)


def spread(flat, dests, outs):
    done = 0
    for out in outs:
        shard = out.shape[1]
        for i in range(out.shape[0]):
            at = pl.multiple_of(dests[done + i] * shard, shard)
            out[i] = flat[pl.ds(at, shard), :]
        done += out.shape[0]


def out_grad_kernel(n_blocks, dests, offs, a0, a1, a2, a3, mix, small, *refs):
    outs, (aog, flat) = refs[:n_blocks], refs[n_blocks:]
    for r, piece in enumerate((a0, a1, a2, a3)):
        aog[pl.ds(pl.multiple_of(offs[r], BLK), BLK), :] = piece[...]
    flat[:, :256] = mm_tn(aog[...], mix[...]).astype(BF)
    flat[:, 256:] = small[...].astype(BF)
    spread(flat, dests, outs)


def route_kernel(
    tok, keep, got, cross, gains, wob, routes, cot, after_o, ma_o, mb_o, mc_o, gates_o
):
    after = tok[...].astype(F32) + (keep[0] + got[0].astype(F32) + cross[...].astype(F32))
    after_o[...] = after
    factor = lax.rsqrt(jnp.mean(after * after, axis=-1, keepdims=True) + EPSILON)
    moe_in = (after * factor * gains[1:2, :]).astype(BF)
    logits = mm(moe_in, wob[:, 256:])
    lane = lanes(logits.shape)
    routed = lane < 0
    for k in range(routes.shape[1]):
        routed = routed | (routes[:, k : k + 1] == lane)
    top = jnp.max(jnp.where(routed, logits, FLOOR_SCORE), axis=1, keepdims=True)
    lifted = jnp.where(routed, jnp.exp(jnp.where(routed, logits - top, 0.0)), 0.0)
    gates = lifted / jnp.sum(lifted, axis=1, keepdims=True)
    gates_o[...] = gates
    high = gates.astype(BF).astype(F32)
    middle = (gates - high).astype(BF).astype(F32)
    low = gates - high - middle
    extra = high + pltpu.roll(middle, 32, 1) + pltpu.roll(low, 64, 1)
    for out, (a, b, c, d, at) in zip((ma_o, mb_o, mc_o), cuts(cot.shape[1])):
        out[:, : b - a] = moe_in[:, a:b]
        out[:, at:] = cot[:, c:d]
    mc_o[:, TOK[2] : TOK[2] + NOTES] = extra.astype(BF)


def place_weights(meta, parts, mat, kinds):
    hidden = mat.shape[1] // len(kinds)
    done = 0
    for part in parts:
        shard = part.shape[2]
        for b in range(part.shape[0]):
            block = done + b
            at = meta[5 + block // 16] + block % 16 // 4 * shard if len(parts) > 1 else block // 4 * shard
            at = pl.multiple_of(at, shard)
            for i, m in enumerate(kinds):
                col = i * hidden + block % 4 * 128
                mat[pl.ds(at, shard), col : col + 128] = part[b, m]
        done += part.shape[0]


def one_hot(rank):
    row_ids = lax.broadcasted_iota(jnp.int32, (BLK, rank.shape[-1]), 0)
    return jnp.where(rank == row_ids, 1.0, 0.0).astype(BF)


def expert_kernel(n_mats, first, meta, *refs):
    refs = list(refs)
    take = lambda n: [refs.pop(0) for _ in range(n)]
    tok_k, tok_c = take(3), take(3)
    (rank,) = take(1)
    mats = take(n_mats)
    prev = [] if first else take(6)
    outs = take(6)
    pick_o, dy_o, pre_o, weighted_o, mat = take(5)
    hidden = mat.shape[1] // 3
    own_expert = meta[0]

    @pl.when(pl.program_id(0) == 0)
    def _():
        place_weights(meta, mats, mat, (0, 1, 2))

    pick = one_hot(rank[0])
    half = pick.shape[1] // 2
    pick_k, pick_c = pick[:, :half], pick[:, half:]
    flat = lambda ref: ref[...].reshape(half, ref.shape[-1])
    spans = cuts(pick_o.shape[1])
    for i, (a, b, c, d, at) in enumerate(spans):
        got = mm(pick_k, flat(tok_k[i])) + mm(pick_c, flat(tok_c[i]))
        pick_o[:, a:b] = got[:, : b - a].astype(BF)
        dy_o[:, c:d] = got[:, at:].astype(BF)
    extra = got[:, TOK[2] : TOK[2] + NOTES]
    lane = lanes(extra.shape)
    mine = (lane % 32 == own_expert) & (lane < 96)
    gate = jnp.sum(jnp.where(mine, extra, 0.0), axis=1, keepdims=True)
    picked, dy = pick_o[...], dy_o[...]
    gate_pre = mm(picked, mat[:, :hidden])
    up_pre = mm(picked, mat[:, hidden : 2 * hidden])
    back = mm(dy, mat[:, 2 * hidden :])
    sigma = 1.0 / (1.0 + jnp.exp(-gate_pre))
    active = gate_pre * sigma
    hid = active * up_pre
    gate_dot = jnp.sum(hid.astype(BF).astype(F32) * back, axis=1, keepdims=True)
    weighted_o[...] = (gate * hid).astype(BF)
    back = back * gate
    pre_o[:, :hidden] = (back * up_pre * sigma * (1.0 + gate_pre * (1.0 - sigma))).astype(BF)
    pre_o[:, hidden:] = (back * active).astype(BF)
    picked_grad = mm_nt(pre_o[...], mat[:, : 2 * hidden]).astype(BF)
    expert_out = mm_nt(weighted_o[...], mat[:, 2 * hidden :]).astype(BF)
    dot_high = gate_dot.astype(BF).astype(F32)
    dot_low = gate_dot - dot_high
    note = jnp.where(lane == own_expert, dot_high, 0.0)
    note = jnp.where(lane == own_expert + 32, dot_low, note).astype(BF)
    for side, chosen in ((1, pick_c), (0, pick_k)):
        for i, (a, b, c, d, _) in enumerate(spans):
            part = [picked_grad[:, a:b]] + ([note] if i == 2 else []) + [expert_out[:, c:d]]
            part = jnp.concatenate(part, axis=1)
            index = i + 3 * side
            summed = mm_tn(chosen, part)
            if not first:
                summed += prev[index][...].reshape(summed.shape).astype(F32)
            outs[index][...] = summed.astype(BF).reshape(outs[index].shape)


def weight_grad_kernel(blocks, meta, picked, dy, pre, weighted, *outs):
    shard = outs[0].shape[2]
    grads = (mm_tn(picked[...], pre[...]).astype(BF), mm_tn(dy[...], weighted[...]).astype(BF))
    hidden = weighted.shape[1]
    for step in range(4):

        @pl.when(pl.program_id(0) == step)
        def _(step=step):
            for b in range(blocks):
                block, n = step * blocks + b, 0
                while block >= outs[n].shape[0]:
                    block -= outs[n].shape[0]
                    n += 1
                rows = slice(b // 4 * shard, b // 4 * shard + shard)
                for m in range(3):
                    col = m % 2 * hidden + b % 4 * 128
                    outs[n][block, m] = grads[m // 2][rows, col : col + 128]


def back_kernel(
    after, ak, ar, bk, br, ck, cr, gains, wob, gates, cot, after_grad_o, aog_o, small_o, block_o
):
    both = lambda a, b: a[...].astype(F32) + b[...].astype(F32)
    sums = [both(ak, ar), both(bk, br), both(ck, cr)]
    spans = cuts(after.shape[1])
    upstream = jnp.concatenate([v[:, : b - a] for v, (a, b, *_) in zip(sums, spans)], axis=1)
    moe_out = jnp.concatenate([v[:, span[4] :] for v, span in zip(sums, spans)], axis=1)
    block_o[...] = (after[...] + moe_out).astype(BF)
    extra = sums[2][:, TOK[2] : TOK[2] + NOTES]
    lane = lanes(extra.shape)
    gate_dot = jnp.where(lane < 32, extra + pltpu.roll(extra, 96, 1), 0.0)
    share = gates[...]
    logit_grad = share * (gate_dot - jnp.sum(share * gate_dot, axis=1, keepdims=True))
    high = logit_grad.astype(BF)
    low = (logit_grad - high.astype(F32)).astype(BF)
    router = wob[:, 256:]
    gain = gains[1:2, :]
    upstream += mm_nt(high, router) + mm_nt(low, router)
    value = after[...]
    factor = lax.rsqrt(jnp.mean(value * value, axis=-1, keepdims=True) + EPSILON)
    normed = value * factor
    moe_in = (normed * gain).astype(BF)
    scaled = upstream * gain
    inward = factor * (scaled - normed * jnp.mean(scaled * normed, axis=-1, keepdims=True))
    after_grad = cot[...].astype(F32) + inward
    after_grad_o[...] = after_grad
    aog_o[...] = after_grad.astype(BF)
    column = jnp.where(lane == 32, 1.0, 0.0).astype(BF)
    small_o[...] = (
        mm_tn(moe_in, high) + mm_tn(moe_in, low) + mm_tn((upstream * normed).astype(BF), column)
    )


def finish_kernel(tok, keep, got, cross, gains, after_grad, out):
    upstream = keep[0] + got[0].astype(F32) + cross[...].astype(F32)
    value = tok[...].astype(F32)
    factor = lax.rsqrt(jnp.mean(value * value, axis=-1, keepdims=True) + EPSILON)
    normed = value * factor
    scaled = upstream * gains[0:1, :]
    inward = factor * (scaled - normed * jnp.mean(scaled * normed, axis=-1, keepdims=True))
    out[...] = after_grad[...] + inward


def spec_of(space):
    return pl.BlockSpec(memory_space=space)


def cost(micros):
    return pl.CostEstimate(flops=1, bytes_accessed=int(micros * 750000), transcendentals=0)


def simple_call(kernel, outs, n_scalar, n_in, micros, scratch=()):
    return pl.pallas_call(
        kernel,
        out_shape=[jax.ShapeDtypeStruct(s, d) for s, d in outs],
        in_specs=[spec_of(pltpu.SMEM)] * n_scalar + [spec_of(pltpu.VMEM)] * n_in,
        out_specs=[spec_of(pltpu.VMEM)] * len(outs),
        scratch_shapes=list(scratch),
        compiler_params=pltpu.CompilerParams(vmem_limit_bytes=VMEM_LIMIT),
        cost_estimate=cost(micros),
    )


def gather_pool(pieces, beside):
    bufs = pieces
    for step in range(4):
        moving = beside(step)(*bufs)
        axes = [(order + ("c",))[step] for order in ORDERS]
        came = together([swap(buf, axis) for buf, axis in zip(bufs, axes)], *moving)
        if step < 3:
            bufs = [jnp.stack([buf, new]) for buf, new in zip(bufs, came)]
    return list(bufs), list(came)


def scatter_pool(kept, other, fill):
    add = lambda a, b: (a.astype(F32) + b.astype(F32)).astype(BF)
    bufs = kept
    for step in range(4):
        moving = fill(step, bufs if step else other)
        if step == 0:
            came = [swap(send, "c") for send in other]
        else:
            axes = [order[3 - step] for order in ORDERS]
            came = [swap(buf[1], axis) for buf, axis in zip(bufs, axes)]
            bufs = [buf[0] for buf in bufs]
        came = together(came, *moving)
        if step < 3:
            bufs = together([add(a, b) for a, b in zip(bufs, came)])
    return list(zip(bufs, came))


def gather_tensor(value):
    cross = swap(value, "x")
    return [value, swap(value, "c"), cross, swap(cross, "c")]


def sum_tensor(keep, send):
    got = swap(send, "c")
    cross = swap((keep[1] + got[1].astype(F32)).astype(BF), "x")
    return got, cross


def pool_spec(order, width):
    shape = tuple(2 if axis == "x" else 1 for axis in reversed(order)) + (BLK, width)

    def index(g, meta):
        place = {"x": 0, "u": g // 2, "y": g % 2}
        return tuple(place[axis] for axis in reversed(order)) + (0, 0)

    return pl.BlockSpec(shape, index)


def local(
    tokens, segments, routes, priority, norm_attn, w_query, w_key, w_value, w_out, norm_moe,
    w_router, w_gate, w_up, w_down, cotangent,
):
    _, rows, dim = tokens.shape
    n_outer = lax.axis_size("o")
    n_dp = 4 * n_outer
    shard = w_query.shape[0]
    length = 4 * rows
    top = routes.shape[2]
    experts = w_gate.shape[0]
    per_device = experts // 16
    capacity = length * top // experts
    hidden = 4 * w_gate.shape[2]
    widths = [at + d - c for _, _, c, d, at in cuts(dim)]
    at_x, at_c = lax.axis_index("x"), lax.axis_index("c")
    at_t = at_x * 2 + at_c
    at_pool = lax.axis_index(POOL)

    at_dp, at_z, at_y = lax.axis_index(DP), lax.axis_index(("o", "u")), lax.axis_index("y")
    steps = lambda n: jnp.arange(n, dtype=jnp.int32)

    tok = tokens[0]
    cot = cotangent[0]
    tok_parts = gather_tensor(tok)
    own_mats = []

    def weight_part(j):
        return jnp.stack([w[j * 16 : (j + 1) * 16] for w in (w_gate, w_up, w_down)], axis=1)

    first_mats = lax.all_to_all(weight_part(0), POOL, 0, 0, tiled=True)

    parts_in = []

    def part_in(*markers):
        if n_outer != 2:
            return ()
        j, i = divmod(len(parts_in), 4)
        parts_in.append(swap(after_all(own_mats[j][4 * i : 4 * i + 4], *markers), "o"))
        return (parts_in[-1],)

    seg = segments[0]
    start = jnp.zeros_like(seg)
    for s in range(1, 5):
        start = jnp.where(seg >= s, jnp.sum((seg < s).astype(jnp.int32)), start)
    place = (jnp.arange(length, dtype=jnp.int32) - start).astype(F32)
    lane = jnp.arange(128, dtype=jnp.int32)
    half = HEAD_SIZE // 2
    inverse = jnp.exp((lane % half).astype(F32) * (-2.0 * math.log(10000.0) / HEAD_SIZE))
    angle = place[:, None] * inverse[None, :]
    cosine = jnp.cos(angle)
    sine = jnp.sin(angle) * jnp.where(lane % HEAD_SIZE < half, -1.0, 1.0)
    start_col = start[:, None]

    notes = jnp.pad(jnp.stack([norm_attn, norm_moe]), ((0, 14), (0, 512 - shard)))
    pack = jnp.concatenate([w_query, w_key, w_value], axis=1)
    pack_b = jnp.concatenate([w_out, w_router, jnp.zeros((shard, 128 - experts), BF)], axis=1)
    if n_dp == 8:
        pack = jnp.concatenate(
            [jnp.concatenate([pack, pack_b], axis=1), jnp.pad(notes, ((0, 0), (0, 384)))], axis=0
        )
        rest = [lax.ppermute(pack, ("o", "u"), [(i, i ^ s) for i in range(4)]) for s in (1, 2, 3)]
        near = jnp.stack([pack, *together(rest, cosine, sine, start_col)])
        wa = [near[:, :, :512]]
        wa.append(swap(wa[0], "y"))
        wb = [near[:, :shard, 512:]]
        wb.append(swap(wb[0], "y"))
        table = jnp.bitwise_xor(at_z, steps(8) % 4) * 2 + jnp.bitwise_xor(at_y, steps(8) // 4)
        gains = jnp.zeros((8, dim), F32)
    else:
        wa = [lax.all_gather(pack, DP, axis=0)]
        wb = [lax.all_gather(pack_b, DP, axis=0)]
        table = steps(n_dp)
        gains = jnp.stack([lax.all_gather(g, DP, axis=0, tiled=True) for g in (norm_attn, norm_moe)])
        gains = jnp.pad(gains.astype(F32), ((0, 6), (0, 0)))

    table = table.astype(jnp.int32)
    next_part = weight_part(1)
    own_mats.append(first_mats)
    *tok_parts, next_part = together((*tok_parts, next_part), *wa, first_mats)
    own_mats.append(lax.all_to_all(next_part, POOL, 0, 0, tiled=True))
    moving = part_in(tok_parts[0])
    plan = after_all(jnp.concatenate([routes[0].T, priority], axis=0), tok_parts[0])
    plan = jnp.stack([plan, swap(plan, "y")])
    offs = (jnp.bitwise_xor(at_t, steps(4)) * rows).astype(jnp.int32)
    heads = w_query.shape[1]
    ain, wqkv, gains, q, kd, vd, mix, lse = simple_call(
        functools.partial(attend_forward_kernel, len(wa), shard),
        [
            ((length, dim), BF),
            ((dim, 512), BF),
            ((8, dim), F32),
            ((length, heads), BF),
            ((2, length, 128), BF),
            ((2, length, 128), BF),
            ((length, heads), BF),
            ((length, 128), F32),
        ],
        2,
        8 + len(wa),
        11,
    )(table, offs, *tok_parts, *wa, gains, cosine, sine, start_col)
    keep, send, wob = simple_call(
        functools.partial(project_kernel, len(wb)),
        [((2, rows, dim), F32), ((2, rows, dim), BF), ((dim, 384), BF)],
        2,
        1 + len(wb),
        4,
    )(table, offs, mix, *wb)
    keep, send, wob = together((keep, send, wob), *moving)
    moving = part_in(send)
    got, cross = sum_tensor(keep, send)
    got, cross, own_mats[1], plan = together((got, cross, own_mats[1], plan), *moving)
    route_col = lax.dynamic_slice_in_dim(routes[0], at_t * rows, rows, 0)
    after, ma, mb, mc, gates = simple_call(
        route_kernel,
        [
            ((rows, dim), F32),
            *[((rows, width), BF) for width in widths],
            ((rows, 128), F32),
        ],
        0,
        8,
        4,
    )(tok, keep, got, cross, gains, wob, route_col, cot)

    own = [j * 16 + at_pool for j in range(per_device)]
    plan = jnp.concatenate([plan, swap(plan, "u")], axis=0)
    hits = jnp.stack([jnp.any(plan[:, :top] == e, axis=1) for e in own], axis=1)
    first = plan[:, top]
    less = (first[:, :, None] < first[:, None, :]).astype(BF)
    rank = jnp.einsum("gjs,gst->gjt", hits.astype(BF), less, preferred_element_type=F32)
    rank = rank.astype(jnp.int32)
    rank = jnp.where(hits & (rank < capacity), rank, -1)
    rank = rank.reshape(4, per_device, 2, 2, rows)
    rank = jnp.where(at_x == 1, rank[:, :, ::-1], rank)
    rank = jnp.where(at_c == 1, rank[:, :, :, ::-1], rank)
    rank = rank.swapaxes(2, 3).reshape(4, per_device, length)

    def beside(step):
        return lambda *markers: sum((part_in(*markers) for _ in range((1, 1, 2, 1)[step])), ()) + (
            (plan, plan, rank)[step : step + 1]
        )

    tok_kept, tok_other = gather_pool([ma, mb, mc], beside)
    if n_outer == 2:
        ready_mats = lambda j: [own_mats[j]] + parts_in[4 * j : 4 * j + 4]
    else:
        all_mats = [lax.all_gather(m, "o", axis=0, tiled=True) for m in own_mats]
        ready_mats = lambda j: [all_mats[j]]
    at_o = lax.axis_index("o")
    bases = [at_o * 4 * shard, (1 - at_o) * 4 * shard] if n_outer == 2 else [0, 0]
    bases = jnp.stack([jnp.int32(base) for base in bases])

    params = dict(compiler_params=pltpu.CompilerParams(vmem_limit_bytes=VMEM_LIMIT))
    tok_specs = [pool_spec(o, w) for o, w in zip(ORDERS, widths)]
    slot_spec = lambda width: pl.BlockSpec((BLK, width), lambda g, meta: (g, 0))
    rank_spec = pl.BlockSpec((1, 1, length), lambda g, meta: (g, 0, 0))
    mat_shape = (n_outer * 16, 3, shard, hidden // 4)
    mat_spec = lambda m: pl.BlockSpec(
        m.shape, lambda g, meta: (0, 0, 0, 0), pipeline_mode=pl.Buffered(1)
    )
    down_spec = lambda m: pl.BlockSpec(
        (m.shape[0], 1) + m.shape[2:], lambda g, meta: (0, 2, 0, 0), pipeline_mode=pl.Buffered(1)
    )
    pool_shapes = [jax.ShapeDtypeStruct((2, 2, 2, rows, w), BF) for w in widths]
    slots = 4 * capacity
    groups = steps(4)
    metas = [jnp.concatenate([e[None], groups, bases]).astype(jnp.int32) for e in own]
    chunk = dim // 4
    full = lambda width: pl.BlockSpec((slots, width), lambda i, meta: (0, 0))
    turned = lambda i, meta: jnp.where(meta[5] == 0, i ^ 2, i) if n_outer == 2 else i
    chunk_spec = pl.BlockSpec((slots, chunk), lambda i, meta: (0, turned(i, meta)))
    grad_shape = lambda n: jax.ShapeDtypeStruct((n,) + mat_shape[1:], BF)
    whole = lambda n: pl.BlockSpec((n,) + mat_shape[1:], lambda i, meta: (0, 0, 0, 0))

    def weight_grads_of(meta, saved):
        counts = [4, 4, 4, 4, 16] if n_outer == 2 else [16 * n_outer]
        return pl.pallas_call(
            functools.partial(weight_grad_kernel, chunk // shard * 4),
            grid_spec=pltpu.PrefetchScalarGridSpec(
                num_scalar_prefetch=1,
                grid=(4,),
                in_specs=[chunk_spec, chunk_spec, full(2 * hidden), full(hidden)],
                out_specs=[whole(n) for n in counts],
            ),
            out_shape=[grad_shape(n) for n in counts],
            cost_estimate=cost(9),
            **params,
        )(meta, *saved)

    prev, weighted, saved = [], [], []
    parts_out = []

    def part_out(sends, *markers):
        if n_outer != 2:
            return ()
        parts_out.append(swap(after_all(sends[len(parts_out) % 4], *markers), "o"))
        return (parts_out[-1],)

    for j in range(per_device):
        if j == 0:
            moving = part_in(*tok_other)
        else:
            prev = together(prev, *moving)
            first_grads = weight_grads_of(after_all(metas[0], prev[0]), saved[0])
            metas[j] = after_all(metas[j], first_grads[0])
            moving = part_out(first_grads[:4], first_grads[0])
            moving += part_out(first_grads[:4], first_grads[0])
        result = pl.pallas_call(
            functools.partial(expert_kernel, len(ready_mats(j)), j == 0),
            grid_spec=pltpu.PrefetchScalarGridSpec(
                num_scalar_prefetch=1,
                grid=(4,),
                in_specs=tok_specs * 2
                + [rank_spec]
                + [mat_spec(m) for m in ready_mats(j)]
                + (tok_specs * 2 if prev else []),
                out_specs=tok_specs * 2
                + [slot_spec(dim), slot_spec(dim), slot_spec(2 * hidden), slot_spec(hidden)],
                scratch_shapes=[pltpu.VMEM((dim, 3 * hidden), BF)],
            ),
            out_shape=pool_shapes * 2
            + [jax.ShapeDtypeStruct((slots, w), BF) for w in (dim, dim, 2 * hidden, hidden)],
            cost_estimate=cost(29),
            **params,
        )(
            metas[j], *tok_kept, *tok_other, rank[:, j : j + 1], *ready_mats(j), *prev,
        )
        prev = result[:6]
        weighted.append(result[9])
        saved.append(result[6:10])

    prev = together(prev, *moving)
    last_grads = []

    moved = []

    def total(mine, parts):
        return (mine.astype(F32) + jnp.concatenate(parts, axis=0).astype(F32)).astype(BF)

    def fill(step, bufs):
        if step == 0:
            last_grads.extend(weight_grads_of(after_all(metas[1], prev[0]), saved[1]))
            return part_out(first_grads[:4], *bufs) + (last_grads[0],)
        if step == 2 and n_outer == 2:
            value = total(first_grads[4], parts_out[:4])
            moved.append(lax.all_to_all(after_all(value, *bufs), POOL, 0, 0, tiled=True))
        moving = part_out((first_grads if len(parts_out) < 4 else last_grads)[:4], *bufs)
        return moving + (part_out(last_grads[:4], *bufs) if step == 1 else ())

    pairs = scatter_pool(prev[:3], prev[3:], fill)

    after_grad, aog, small, block_out = simple_call(
        back_kernel,
        [((rows, dim), F32), ((rows, dim), BF), ((dim, 128), F32), ((rows, dim), BF)],
        0,
        11,
        5,
    )(after, *pairs[0], *pairs[1], *pairs[2], gains, wob, gates, cot)
    near, cross = swap(aog, "c"), swap(aog, "x")
    moving = part_out(last_grads[:4], aog)
    near, cross = together((near, cross), *moving)
    aog_parts = [aog, near, cross, swap(cross, "c")]

    n_tails = 2 if n_dp == 8 else 1
    dests = jnp.bitwise_xor(at_z, steps(8) % 4) * 2 + jnp.bitwise_xor(at_y, steps(8) // 4)
    dests = (dests if n_dp == 8 else steps(n_dp)).astype(jnp.int32)
    tail_shape = lambda width: [((n_dp // n_tails, shard, width), BF)] * n_tails
    sides = simple_call(
        functools.partial(out_grad_kernel, n_tails),
        tail_shape(384),
        2,
        6,
        2,
        scratch=[pltpu.VMEM((length, dim), BF), pltpu.VMEM((dim, 384), BF)],
    )(dests, offs, *aog_parts, mix, small)

    aog_parts = together(aog_parts, *sides)
    if n_outer == 2:
        last_sum = after_all(total(last_grads[4], parts_out[4:]), *aog_parts)
    else:
        first_sum, last_sum = (
            lax.psum_scatter(g[0], "o", scatter_dimension=0, tiled=True)
            for g in (first_grads, last_grads)
        )
        moved.append(lax.all_to_all(first_sum, POOL, 0, 0, tiled=True))
    moved.append(lax.all_to_all(last_sum, POOL, 0, 0, tiled=True))
    sides = list(sides)
    if n_tails == 2:
        sides[1] = swap(sides[1], "y")
    keep, send, *tails = simple_call(
        functools.partial(attend_backward_kernel, n_tails),
        [((2, rows, dim), F32), ((2, rows, dim), BF)] + tail_shape(640),
        2,
        14,
        60,
        scratch=[
            pltpu.VMEM((length, dim), BF),
            pltpu.VMEM((length, heads), BF),
            pltpu.VMEM((length, 512), BF),
            pltpu.VMEM((2, length, 128), F32),
            pltpu.VMEM((2, length, 128), F32),
            pltpu.VMEM((dim, 640), BF),
        ],
    )(dests, offs, *aog_parts, wqkv, wob, q, kd, vd, lse, start_col, ain, cosine, sine)
    keep, send, *tails = together((keep, send, *tails), *sides)

    got = swap(send, "c")
    tails = list(tails)
    if n_tails == 2:
        tails[1] = swap(tails[1], "y")
    got, *tails = together((got, *tails))
    cross = swap((keep[1] + got[1].astype(F32)).astype(BF), "x")
    if n_tails == 2:
        ends = [
            jnp.concatenate([sum(p[s].astype(F32) for p in part) for part in (sides, tails)], axis=1)
            for s in range(4)
        ]
        for s in range(1, 4):
            perm = [(i, i ^ s) for i in range(4)]
            ends[s] = lax.ppermute(ends[s].astype(BF), ("o", "u"), perm).astype(F32)
        ends = sum(ends)
    else:
        ends = jnp.concatenate([sides[0], tails[0]], axis=2).astype(F32).reshape(dim, 1024)
        ends = lax.psum_scatter(ends, DP, scatter_dimension=0, tiled=True)
    side, tail = ends[:, :384], ends[:, 384:]
    tokens_grad = simple_call(finish_kernel, [((rows, dim), F32)], 0, 6, 4)(
        tok, keep, got, cross, gains, after_grad
    )[0]

    narrow = jnp.concatenate([side[:, 256 : 256 + experts + 1], tail[:, 512:513]], axis=1)
    narrow = narrow + swap(narrow, "x")
    narrow = narrow + swap(narrow, "c")
    gate_grad, up_grad, down_grad = (
        jnp.concatenate([part[:, m] for part in moved], axis=0).astype(F32) for m in range(3)
    )
    return (
        block_out[None],
        tokens_grad[None],
        narrow[:, experts + 1] / norm_attn.astype(F32),
        tail[:, :256],
        tail[:, 256:384],
        tail[:, 384:512],
        side[:, :256],
        narrow[:, experts],
        narrow[:, :experts],
        gate_grad,
        up_grad,
        down_grad,
    )


def solution(mesh):
    devices = mesh.devices
    fine = Mesh(devices.reshape(devices.shape[0] // 4, 2, 2, 2, 2), ("o", "u", "y", "x", "c"))
    dp, tensor = DP, ("x", "c")
    in_specs = (
        P(dp, tensor, None),
        P(dp, None),
        P(dp, None, None),
        P(dp, None),
        P(dp),
        P(dp, tensor),
        P(dp, tensor),
        P(dp, tensor),
        P(dp, tensor),
        P(dp),
        P(dp, None),
        P(None, dp, tensor),
        P(None, dp, tensor),
        P(None, dp, tensor),
        P(dp, tensor, None),
    )
    out_specs = (
        P(dp, tensor, None),
        P(dp, tensor, None),
        P(dp),
        P(dp, tensor),
        P(dp, tensor),
        P(dp, tensor),
        P(dp, tensor),
        P(dp),
        P(dp, None),
        P(None, dp, tensor),
        P(None, dp, tensor),
        P(None, dp, tensor),
    )
    return jax.shard_map(local, mesh=fine, in_specs=in_specs, out_specs=out_specs, check_vma=False)
```

```python
import functools
import math

import jax
import jax.numpy as jnp
from jax import lax
from jax.experimental import pallas as pl
from jax.experimental.pallas import tpu as pltpu
from jax.sharding import Mesh, PartitionSpec as P

HEAD_SIZE = 64
EPSILON = 1e-06
FLOOR_SCORE = -1e30
VMEM_LIMIT = 60 * 1024 * 1024
DP = ("o", "u", "y")
POOL = ("u", "y", "x", "c")
ORDERS = (("u", "y", "x"), ("y", "x", "u"), ("x", "u", "y"))
TOK = (512, 256, 256)
SECOND = (384, 256, 384)
NOTES = 128
BLK = 256
BF = jnp.bfloat16
F32 = jnp.float32


def after_all(value, *others):
    return lax.optimization_barrier((value,) + others)[0]


def together(values, *others):
    return lax.optimization_barrier((*values, *others))[: len(values)]


def cuts(dim):
    found, a, b = [], 0, 0
    for i, (first, second) in enumerate(zip(TOK, SECOND)):
        found.append((a, a + first, b, b + second, first + (NOTES if i == 2 else 0)))
        a, b = a + first, b + second
    assert a == b == dim
    return found


def swap(value, axis):
    return lax.ppermute(value, axis, [(0, 1), (1, 0)])


def mm(left, right):
    return lax.dot_general(left, right, (((1,), (0,)), ((), ())), preferred_element_type=F32)


def mm_nt(left, right):
    return lax.dot_general(left, right, (((1,), (1,)), ((), ())), preferred_element_type=F32)


def mm_tn(left, right):
    return lax.dot_general(left, right, (((0,), (0,)), ((), ())), preferred_element_type=F32)


def lanes(shape):
    return lax.broadcasted_iota(jnp.int32, shape, 1)


def turn_halves(value):
    first = lanes(value.shape) % HEAD_SIZE < HEAD_SIZE // 2
    half = HEAD_SIZE // 2
    return jnp.where(first, pltpu.roll(value, 128 - half, 1), pltpu.roll(value, half, 1))


def both_halves(value, which):
    low = lanes(value.shape) < HEAD_SIZE
    turned = pltpu.roll(value, HEAD_SIZE, 1)
    return jnp.where(low, value, turned) if which == 0 else jnp.where(low, turned, value)


def stack_heads(pair):
    low = lanes(pair.shape) < HEAD_SIZE
    zero = jnp.zeros_like(pair)
    return jnp.concatenate([jnp.where(low, pair, zero), jnp.where(low, zero, pair)], axis=0)


def join_heads(stacked):
    rows = stacked.shape[0] // 2
    low = lanes((rows, stacked.shape[1])) < HEAD_SIZE
    return jnp.where(low, stacked[:rows], stacked[rows:])


def allowed_keys(start_col, block, width):
    rows = start_col.shape[0]
    cols = lax.broadcasted_iota(jnp.int32, (rows, width), 1)
    row_ids = block * rows + lax.broadcasted_iota(jnp.int32, (rows, width), 0)
    keep = (cols >= start_col) & (cols <= row_ids)
    return jnp.concatenate([keep, keep], axis=0)


def attend_forward_kernel(n_parts, shard, table, offs, t0, t1, t2, t3, *refs):
    parts, refs = refs[:n_parts], refs[n_parts:]
    gain_in, cosine, sine, start, ain_o, wqkv_o, gains_o, q_o, kd_o, vd_o, mix_o, lse_o = refs
    gains_o[...] = gain_in[...]
    base = 0
    for part in parts:
        for b in range(part.shape[0]):
            at = pl.multiple_of(table[base + b] * shard, shard)
            wqkv_o[pl.ds(at, shard), :] = part[b, :shard, :]
            if shard == 128:
                note = part[b, shard:, :].astype(F32)
                for row in range(2):
                    gains_o[row : row + 1, pl.ds(at, 128)] = note[row : row + 1, :128]
        base += part.shape[0]
    gain = gains_o[0:1, :]
    for r, piece in enumerate((t0, t1, t2, t3)):
        at = pl.multiple_of(offs[r], BLK)
        rows = pl.ds(at, BLK)
        value = piece[...].astype(F32)
        factor = lax.rsqrt(jnp.mean(value * value, axis=-1, keepdims=True) + EPSILON)
        normed = (value * factor * gain).astype(BF)
        ain_o[rows, :] = normed
        qkv = mm(normed, wqkv_o[...])
        cos_b, sin_b = cosine[rows, :], sine[rows, :]
        for part in range(3):
            raw = qkv[:, part * 128 : part * 128 + 128]
            turned = (raw * cos_b + turn_halves(raw) * sin_b).astype(BF)
            if part < 2:
                q_o[rows, part * 128 : part * 128 + 128] = turned * 0.125
            else:
                wide = turned.astype(F32)
                for kv in range(2):
                    kd_o[kv, rows, :] = both_halves(wide, kv).astype(BF)
        value_rows = qkv[:, 384:512].astype(BF).astype(F32)
        for kv in range(2):
            vd_o[kv, rows, :] = both_halves(value_rows, kv).astype(BF)
    total = ain_o.shape[0]
    for block in range(total // BLK):
        width = (block + 1) * BLK
        rows = pl.ds(block * BLK, BLK)
        keep = allowed_keys(start[rows, :], block, width)
        logs = jnp.zeros((BLK, 128), F32)
        for kv in range(2):
            query = stack_heads(q_o[rows, kv * 128 : kv * 128 + 128])
            scores = jnp.where(keep, mm_nt(query, kd_o[kv, :width, :]), FLOOR_SCORE)
            top = jnp.max(scores, axis=-1, keepdims=True)
            lifted = jnp.exp(scores - top)
            summed = jnp.sum(lifted, axis=-1, keepdims=True)
            shares = (lifted * (1.0 / summed)).astype(BF)
            mixed = join_heads(mm(shares, vd_o[kv, :width, :]))
            mix_o[rows, kv * 128 : kv * 128 + 128] = mixed.astype(BF)
            log_total = top + jnp.log(summed)
            lane = lanes(logs.shape)
            logs = jnp.where(lane == 2 * kv, log_total[:BLK], logs)
            logs = jnp.where(lane == 2 * kv + 1, log_total[BLK:], logs)
        lse_o[rows, :] = logs


def project_kernel(n_parts, table, offs, mix, *refs):
    parts, (keep_o, send_o, wob) = refs[:n_parts], refs[n_parts:]
    base = 0
    for part in parts:
        shard = part.shape[1]
        for b in range(part.shape[0]):
            wob[pl.ds(pl.multiple_of(table[base + b] * shard, shard), shard), :] = part[b]
        base += part.shape[0]
    for r in range(4):
        rows = pl.ds(pl.multiple_of(offs[r], BLK), BLK)
        part = mm_nt(mix[rows, :], wob[:, :256])
        if r % 2 == 0:
            keep_o[r // 2] = part
        else:
            send_o[r // 2] = part.astype(BF)


def attend_backward_kernel(
    n_blocks, dests, offs, a0, a1, a2, a3, wqkv, wob, q, kd, vd, lse, start, ain, cosine, sine,
    keep_o, send_o, *refs,
):
    wg_o, (aog, mgrad, dqkv, dk, dv, flat) = refs[:n_blocks], refs[n_blocks:]
    total = ain.shape[0]
    for r, piece in enumerate((a0, a1, a2, a3)):
        aog[pl.ds(pl.multiple_of(offs[r], BLK), BLK), :] = piece[...]
    mgrad[...] = mm(aog[...], wob[:, :256]).astype(BF)
    dk[...] = jnp.zeros_like(dk)
    dv[...] = jnp.zeros_like(dv)
    for block in range(total // BLK):
        width = (block + 1) * BLK
        rows = pl.ds(block * BLK, BLK)
        keep = allowed_keys(start[rows, :], block, width)
        logs = lse[rows, :]
        lane = lanes(logs.shape)
        cos_b, sin_b = cosine[rows, :], sine[rows, :]
        for kv in range(2):
            cols = slice(kv * 128, kv * 128 + 128)
            query = stack_heads(q[rows, cols])
            out_grad = stack_heads(mgrad[rows, cols])
            log_total = jnp.concatenate(
                [
                    jnp.sum(jnp.where(lane == 2 * kv + h, logs, 0.0), axis=1, keepdims=True)
                    for h in range(2)
                ],
                axis=0,
            )
            keys = kd[kv, :width, :]
            scores = jnp.where(keep, mm_nt(query, keys), FLOOR_SCORE)
            shares = jnp.exp(scores - log_total)
            share_grad = mm_nt(out_grad, vd[kv, :width, :])
            inner = jnp.sum(shares * share_grad, axis=-1, keepdims=True)
            score_grad = (shares * (share_grad - inner)).astype(BF)
            query_grad = join_heads(mm(score_grad, keys)) * 0.125
            query_grad = query_grad * cos_b - turn_halves(query_grad) * sin_b
            dqkv[rows, cols] = query_grad.astype(BF)
            dk[kv, :width, :] += mm_tn(score_grad, query)
            dv[kv, :width, :] += mm_tn(shares.astype(BF), out_grad)
    joined = []
    for acc in (dk, dv):
        pair = [acc[kv] + pltpu.roll(acc[kv], HEAD_SIZE, 1) for kv in range(2)]
        joined.append(jnp.where(lanes(pair[0].shape) < HEAD_SIZE, pair[0], pair[1]))
    key_grad = joined[0] * cosine[...] - turn_halves(joined[0]) * sine[...]
    dqkv[:, 256:384] = key_grad.astype(BF)
    dqkv[:, 384:512] = joined[1].astype(BF)
    flat[:, :512] = mm_tn(ain[...], dqkv[...]).astype(BF)
    ones = jnp.ones((BLK, 128), BF)
    gain_sum = jnp.zeros((ain.shape[1], 128), F32)
    for r in range(4):
        rows = pl.ds(pl.multiple_of(offs[r], BLK), BLK)
        part = mm_nt(dqkv[rows, :], wqkv[...])
        gain_sum += mm_tn((part * ain[rows, :].astype(F32)).astype(BF), ones)
        if r % 2 == 0:
            keep_o[r // 2] = part
        else:
            send_o[r // 2] = part.astype(BF)
    flat[:, 512:] = gain_sum.astype(BF)
    spread(flat, dests, wg_o)


def spread(flat, dests, outs):
    done = 0
    for out in outs:
        shard = out.shape[1]
        for i in range(out.shape[0]):
            at = pl.multiple_of(dests[done + i] * shard, shard)
            out[i] = flat[pl.ds(at, shard), :]
        done += out.shape[0]


def out_grad_kernel(n_blocks, dests, offs, a0, a1, a2, a3, mix, small, *refs):
    outs, (aog, flat) = refs[:n_blocks], refs[n_blocks:]
    for r, piece in enumerate((a0, a1, a2, a3)):
        aog[pl.ds(pl.multiple_of(offs[r], BLK), BLK), :] = piece[...]
    flat[:, :256] = mm_tn(aog[...], mix[...]).astype(BF)
    flat[:, 256:] = small[...].astype(BF)
    spread(flat, dests, outs)


def route_kernel(
    tok, keep, got, cross, gains, wob, routes, cot, after_o, ma_o, mb_o, mc_o, gates_o
):
    after = tok[...].astype(F32) + (keep[0] + got[0].astype(F32) + cross[...].astype(F32))
    after_o[...] = after
    factor = lax.rsqrt(jnp.mean(after * after, axis=-1, keepdims=True) + EPSILON)
    moe_in = (after * factor * gains[1:2, :]).astype(BF)
    logits = mm(moe_in, wob[:, 256:])
    lane = lanes(logits.shape)
    routed = lane < 0
    for k in range(routes.shape[1]):
        routed = routed | (routes[:, k : k + 1] == lane)
    top = jnp.max(jnp.where(routed, logits, FLOOR_SCORE), axis=1, keepdims=True)
    lifted = jnp.where(routed, jnp.exp(jnp.where(routed, logits - top, 0.0)), 0.0)
    gates = lifted / jnp.sum(lifted, axis=1, keepdims=True)
    gates_o[...] = gates
    high = gates.astype(BF).astype(F32)
    middle = (gates - high).astype(BF).astype(F32)
    low = gates - high - middle
    extra = high + pltpu.roll(middle, 32, 1) + pltpu.roll(low, 64, 1)
    for out, (a, b, c, d, at) in zip((ma_o, mb_o, mc_o), cuts(cot.shape[1])):
        out[:, : b - a] = moe_in[:, a:b]
        out[:, at:] = cot[:, c:d]
    mc_o[:, TOK[2] : TOK[2] + NOTES] = extra.astype(BF)


def place_weights(meta, parts, mat, kinds):
    hidden = mat.shape[1] // len(kinds)
    done = 0
    for part in parts:
        shard = part.shape[2]
        for b in range(part.shape[0]):
            block = done + b
            at = meta[5 + block // 16] + block % 16 // 4 * shard if len(parts) > 1 else block // 4 * shard
            at = pl.multiple_of(at, shard)
            for i, m in enumerate(kinds):
                col = i * hidden + block % 4 * 128
                mat[pl.ds(at, shard), col : col + 128] = part[b, m]
        done += part.shape[0]


def one_hot(rank):
    row_ids = lax.broadcasted_iota(jnp.int32, (BLK, rank.shape[-1]), 0)
    return jnp.where(rank == row_ids, 1.0, 0.0).astype(BF)


def expert_kernel(n_mats, first, meta, *refs):
    refs = list(refs)
    take = lambda n: [refs.pop(0) for _ in range(n)]
    pieces = [take(4) for _ in range(3)]
    (rank,) = take(1)
    mats = take(n_mats)
    prev_rank, prev = (None, None) if first else (take(1)[0], take(3))
    outs = take(3 if first else 6)
    pick_o, dy_o, pre_o, weighted_o, mat = take(5)
    hidden = mat.shape[1] // 3
    own_expert = meta[0]

    @pl.when(pl.program_id(0) == 0)
    def _():
        place_weights(meta, mats, mat, (0, 1, 2))

    pick = one_hot(rank[0])
    half = pick.shape[1] // 2
    pick_k, pick_c = pick[:, :half], pick[:, half:]
    step = pl.program_id(0)

    def rows_of(i, side):
        low, high = (ref[...].reshape(-1, ref.shape[-1]) for ref in pieces[i][2 * side : 2 * side + 2])
        if i == 0:
            return jnp.concatenate([low, high], axis=0)
        return jnp.where((step // 2 if i == 1 else step % 2) == 0, low, high)

    spans = cuts(pick_o.shape[1])
    for i, (a, b, c, d, at) in enumerate(spans):
        got = mm(pick_k, rows_of(i, 0)) + mm(pick_c, rows_of(i, 1))
        pick_o[:, a:b] = got[:, : b - a].astype(BF)
        dy_o[:, c:d] = got[:, at:].astype(BF)
    extra = got[:, TOK[2] : TOK[2] + NOTES]
    lane = lanes(extra.shape)
    mine = (lane % 32 == own_expert) & (lane < 96)
    gate = jnp.sum(jnp.where(mine, extra, 0.0), axis=1, keepdims=True)
    picked, dy = pick_o[...], dy_o[...]
    gate_pre = mm(picked, mat[:, :hidden])
    up_pre = mm(picked, mat[:, hidden : 2 * hidden])
    back = mm(dy, mat[:, 2 * hidden :])
    sigma = 1.0 / (1.0 + jnp.exp(-gate_pre))
    active = gate_pre * sigma
    hid = active * up_pre
    gate_dot = jnp.sum(hid.astype(BF).astype(F32) * back, axis=1, keepdims=True)
    weighted_o[...] = (gate * hid).astype(BF)
    back = back * gate
    pre_o[:, :hidden] = (back * up_pre * sigma * (1.0 + gate_pre * (1.0 - sigma))).astype(BF)
    pre_o[:, hidden:] = (back * active).astype(BF)
    picked_grad = mm_nt(pre_o[...], mat[:, : 2 * hidden]).astype(BF)
    expert_out = mm_nt(weighted_o[...], mat[:, 2 * hidden :]).astype(BF)
    dot_high = gate_dot.astype(BF).astype(F32)
    dot_low = gate_dot - dot_high
    note = jnp.where(lane == own_expert, dot_high, 0.0)
    note = jnp.where(lane == own_expert + 32, dot_low, note).astype(BF)
    if not first:
        pick = jnp.concatenate([one_hot(prev_rank[0]), pick], axis=0)
    for i, (a, b, c, d, _) in enumerate(spans):
        part = [picked_grad[:, a:b]] + ([note] if i == 2 else []) + [expert_out[:, c:d]]
        part = jnp.concatenate(part, axis=1)
        if first:
            outs[i][...] = part
            continue
        part = jnp.concatenate([prev[i][...], part], axis=0)
        for side in range(2):
            summed = mm_tn(pick[:, side * half : side * half + half], part)
            out = outs[i + 3 * side]
            out[...] = summed.astype(BF).reshape(out.shape)


def weight_grad_kernel(blocks, meta, picked, dy, pre, weighted, *outs):
    shard = outs[0].shape[2]
    grads = (mm_tn(picked[...], pre[...]).astype(BF), mm_tn(dy[...], weighted[...]).astype(BF))
    hidden = weighted.shape[1]
    for step in range(4):

        @pl.when(pl.program_id(0) == step)
        def _(step=step):
            for b in range(blocks):
                block, n = step * blocks + b, 0
                while block >= outs[n].shape[0]:
                    block -= outs[n].shape[0]
                    n += 1
                rows = slice(b // 4 * shard, b // 4 * shard + shard)
                for m in range(3):
                    col = m % 2 * hidden + b % 4 * 128
                    outs[n][block, m] = grads[m // 2][rows, col : col + 128]


def back_kernel(
    after, ak, ar, bk, br, ck, cr, gains, wob, gates, cot, after_grad_o, aog_o, small_o, block_o
):
    both = lambda a, b: a[...].astype(F32) + b[...].astype(F32)
    sums = [both(ak, ar), both(bk, br), both(ck, cr)]
    spans = cuts(after.shape[1])
    upstream = jnp.concatenate([v[:, : b - a] for v, (a, b, *_) in zip(sums, spans)], axis=1)
    moe_out = jnp.concatenate([v[:, span[4] :] for v, span in zip(sums, spans)], axis=1)
    block_o[...] = (after[...] + moe_out).astype(BF)
    extra = sums[2][:, TOK[2] : TOK[2] + NOTES]
    lane = lanes(extra.shape)
    gate_dot = jnp.where(lane < 32, extra + pltpu.roll(extra, 96, 1), 0.0)
    share = gates[...]
    logit_grad = share * (gate_dot - jnp.sum(share * gate_dot, axis=1, keepdims=True))
    high = logit_grad.astype(BF)
    low = (logit_grad - high.astype(F32)).astype(BF)
    router = wob[:, 256:]
    gain = gains[1:2, :]
    upstream += mm_nt(high, router) + mm_nt(low, router)
    value = after[...]
    factor = lax.rsqrt(jnp.mean(value * value, axis=-1, keepdims=True) + EPSILON)
    normed = value * factor
    moe_in = (normed * gain).astype(BF)
    scaled = upstream * gain
    inward = factor * (scaled - normed * jnp.mean(scaled * normed, axis=-1, keepdims=True))
    after_grad = cot[...].astype(F32) + inward
    after_grad_o[...] = after_grad
    aog_o[...] = after_grad.astype(BF)
    column = jnp.where(lane == 32, 1.0, 0.0).astype(BF)
    small_o[...] = (
        mm_tn(moe_in, high) + mm_tn(moe_in, low) + mm_tn((upstream * normed).astype(BF), column)
    )


def finish_kernel(tok, keep, got, cross, gains, after_grad, out):
    upstream = keep[0] + got[0].astype(F32) + cross[...].astype(F32)
    value = tok[...].astype(F32)
    factor = lax.rsqrt(jnp.mean(value * value, axis=-1, keepdims=True) + EPSILON)
    normed = value * factor
    scaled = upstream * gains[0:1, :]
    inward = factor * (scaled - normed * jnp.mean(scaled * normed, axis=-1, keepdims=True))
    out[...] = after_grad[...] + inward


def spec_of(space):
    return pl.BlockSpec(memory_space=space)


def cost(micros):
    return pl.CostEstimate(flops=1, bytes_accessed=int(micros * 750000), transcendentals=0)


def simple_call(kernel, outs, n_scalar, n_in, micros, scratch=()):
    return pl.pallas_call(
        kernel,
        out_shape=[jax.ShapeDtypeStruct(s, d) for s, d in outs],
        in_specs=[spec_of(pltpu.SMEM)] * n_scalar + [spec_of(pltpu.VMEM)] * n_in,
        out_specs=[spec_of(pltpu.VMEM)] * len(outs),
        scratch_shapes=list(scratch),
        compiler_params=pltpu.CompilerParams(vmem_limit_bytes=VMEM_LIMIT),
        cost_estimate=cost(micros),
    )


def gather_pool(pieces, beside, ready):
    bufs = pieces
    came = (ready,)
    for step in range(3):
        moving = beside(step)(*came)
        came = [swap(buf, order[step]) for buf, order in zip(bufs, ORDERS)]
        came = together(came, *moving)
        if step < 2:
            bufs = [jnp.stack([buf, new]) for buf, new in zip(bufs, came)]
    moving = beside(3)(*came)
    near = [swap(after_all(value, *came), "c") for value in bufs]
    far = [swap(value, "c") for value in came]
    values = together((*near, *far), *moving)
    return list(zip(bufs, came, values[:3], values[3:]))


def scatter_pool(kept, other, fill):
    add = lambda a, b: (a.astype(F32) + b.astype(F32)).astype(BF)
    moving = fill(0, other)
    came = together([swap(send, "c") for send in other], *moving)
    before = list(zip(kept, came))
    for step in range(1, 4):
        sends = together([add(a[1], b[1]) for a, b in before])
        moving = fill(step, came)
        came = [swap(send, order[3 - step]) for send, order in zip(sends, ORDERS)]
        flat = together([value for pair in before for value in pair], *sends)
        keeps = [add(flat[2 * i][0], flat[2 * i + 1][0]) for i in range(3)]
        values = together((*came, *keeps), *moving)
        before = list(zip(values[3:], values[:3]))
    return before


def gather_tensor(value):
    cross = swap(value, "x")
    return [value, swap(value, "c"), cross, swap(cross, "c")]


def sum_tensor(keep, send):
    got = swap(send, "c")
    cross = swap((keep[1] + got[1].astype(F32)).astype(BF), "x")
    return got, cross


def pool_specs(order, width):
    def spec(axes, half):
        shape = tuple(2 if axis == "x" else 1 for axis in reversed(axes)) + (BLK, width)

        def index(g, meta):
            place = {"x": 0, "u": g // 2, "y": g % 2}
            if half is not None and order[2] == "u":
                place["y"] = jnp.where(g // 2 == half, g % 2, 1 - half)
            return tuple(place[axis] for axis in reversed(axes)) + (0, 0)

        return pl.BlockSpec(shape, index)

    return [spec(order[:2], 0), spec(order[:2], 1)], spec(order, None)


def local(
    tokens, segments, routes, priority, norm_attn, w_query, w_key, w_value, w_out, norm_moe,
    w_router, w_gate, w_up, w_down, cotangent,
):
    _, rows, dim = tokens.shape
    n_outer = lax.axis_size("o")
    n_dp = 4 * n_outer
    shard = w_query.shape[0]
    length = 4 * rows
    top = routes.shape[2]
    experts = w_gate.shape[0]
    per_device = experts // 16
    capacity = length * top // experts
    hidden = 4 * w_gate.shape[2]
    widths = [at + d - c for _, _, c, d, at in cuts(dim)]
    at_x, at_c = lax.axis_index("x"), lax.axis_index("c")
    at_t = at_x * 2 + at_c
    at_pool = lax.axis_index(POOL)

    at_dp, at_z, at_y = lax.axis_index(DP), lax.axis_index(("o", "u")), lax.axis_index("y")
    steps = lambda n: jnp.arange(n, dtype=jnp.int32)

    tok = tokens[0]
    cot = cotangent[0]
    tok_near, tok_cross = swap(tok, "c"), swap(tok, "x")
    own_mats = []

    def weight_part(j):
        return jnp.stack([w[j * 16 : (j + 1) * 16] for w in (w_gate, w_up, w_down)], axis=1)

    parts_in = []

    def part_in(*markers):
        if n_outer != 2:
            return ()
        j, i = divmod(len(parts_in), 4)
        parts_in.append(swap(after_all(own_mats[j][4 * i : 4 * i + 4], *markers), "o"))
        return (parts_in[-1],)

    first_mats = after_all(weight_part(0), tok_near)
    first_mats = lax.all_to_all(first_mats, POOL, 0, 0, tiled=True)

    seg = segments[0]
    start = jnp.zeros_like(seg)
    for s in range(1, 5):
        start = jnp.where(seg >= s, jnp.sum((seg < s).astype(jnp.int32)), start)
    place = (jnp.arange(length, dtype=jnp.int32) - start).astype(F32)
    lane = jnp.arange(128, dtype=jnp.int32)
    half = HEAD_SIZE // 2
    inverse = jnp.exp((lane % half).astype(F32) * (-2.0 * math.log(10000.0) / HEAD_SIZE))
    angle = place[:, None] * inverse[None, :]
    cosine = jnp.cos(angle)
    sine = jnp.sin(angle) * jnp.where(lane % HEAD_SIZE < half, -1.0, 1.0)
    start_col = start[:, None]

    notes = jnp.pad(jnp.stack([norm_attn, norm_moe]), ((0, 14), (0, 512 - shard)))
    pack = jnp.concatenate([w_query, w_key, w_value], axis=1)
    pack_b = jnp.concatenate([w_out, w_router, jnp.zeros((shard, 128 - experts), BF)], axis=1)
    if n_dp == 8:
        pack = jnp.concatenate(
            [jnp.concatenate([pack, pack_b], axis=1), jnp.pad(notes, ((0, 0), (0, 384)))], axis=0
        )
        rest = [lax.ppermute(pack, ("o", "u"), [(i, i ^ s) for i in range(4)]) for s in (1, 2, 3)]
        *rest, tok_near, tok_cross = together(
            (*rest, tok_near, tok_cross), cosine, sine, start_col
        )
        near = jnp.stack([pack, *rest])
        wa = [near[:, :, :512]]
        wa.append(swap(wa[0], "y"))
        wb = [near[:, :shard, 512:]]
        wb.append(swap(wb[0], "y"))
        table = jnp.bitwise_xor(at_z, steps(8) % 4) * 2 + jnp.bitwise_xor(at_y, steps(8) // 4)
        gains = jnp.zeros((8, dim), F32)
    else:
        wa = [lax.all_gather(pack, DP, axis=0)]
        wb = [lax.all_gather(pack_b, DP, axis=0)]
        table = steps(n_dp)
        gains = jnp.stack([lax.all_gather(g, DP, axis=0, tiled=True) for g in (norm_attn, norm_moe)])
        gains = jnp.pad(gains.astype(F32), ((0, 6), (0, 0)))

    table = table.astype(jnp.int32)
    own_mats.append(first_mats)
    moving = part_in(wa[0])
    next_part = weight_part(1)
    tok_parts = [tok, tok_near, tok_cross, swap(tok_cross, "c")]
    *tok_parts, next_part = together((*tok_parts, next_part), *wa, *moving)
    own_mats.append(lax.all_to_all(next_part, POOL, 0, 0, tiled=True))
    moving = part_in(tok_parts[0])
    plan = after_all(jnp.concatenate([routes[0].T, priority], axis=0), tok_parts[0])
    plan = jnp.stack([plan, swap(plan, "y")])
    offs = (jnp.bitwise_xor(at_t, steps(4)) * rows).astype(jnp.int32)
    heads = w_query.shape[1]
    ain, wqkv, gains, q, kd, vd, mix, lse = simple_call(
        functools.partial(attend_forward_kernel, len(wa), shard),
        [
            ((length, dim), BF),
            ((dim, 512), BF),
            ((8, dim), F32),
            ((length, heads), BF),
            ((2, length, 128), BF),
            ((2, length, 128), BF),
            ((length, heads), BF),
            ((length, 128), F32),
        ],
        2,
        8 + len(wa),
        11,
    )(table, offs, *tok_parts, *wa, gains, cosine, sine, start_col)
    keep, send, wob = simple_call(
        functools.partial(project_kernel, len(wb)),
        [((2, rows, dim), F32), ((2, rows, dim), BF), ((dim, 384), BF)],
        2,
        1 + len(wb),
        4,
    )(table, offs, mix, *wb)
    keep, send, wob = together((keep, send, wob), *moving)
    moving = part_in(mix)
    got, cross = sum_tensor(keep, send)
    got, cross, plan, own_mats[1] = together((got, cross, plan, own_mats[1]), *moving)
    route_col = lax.dynamic_slice_in_dim(routes[0], at_t * rows, rows, 0)
    after, ma, mb, mc, gates = simple_call(
        route_kernel,
        [
            ((rows, dim), F32),
            *[((rows, width), BF) for width in widths],
            ((rows, 128), F32),
        ],
        0,
        8,
        4,
    )(tok, keep, got, cross, gains, wob, route_col, cot)

    own = [j * 16 + at_pool for j in range(per_device)]
    plan = jnp.concatenate([plan, swap(plan, "u")], axis=0)
    hits = jnp.stack([jnp.any(plan[:, :top] == e, axis=1) for e in own], axis=1)
    first = plan[:, top]
    less = (first[:, :, None] < first[:, None, :]).astype(BF)
    rank = jnp.einsum("gjs,gst->gjt", hits.astype(BF), less, preferred_element_type=F32)
    rank = rank.astype(jnp.int32)
    rank = jnp.where(hits & (rank < capacity), rank, -1)
    rank = rank.reshape(4, per_device, 2, 2, rows)
    rank = jnp.where(at_x == 1, rank[:, :, ::-1], rank)
    rank = jnp.where(at_c == 1, rank[:, :, :, ::-1], rank)
    rank = rank.swapaxes(2, 3).reshape(4, per_device, length)

    def beside(step):
        return lambda *markers: sum((part_in(*markers) for _ in range((1, 1, 2, 0)[step])), ()) + (
            (plan, plan, rank)[step : step + 1]
        )

    pool = [value for piece in gather_pool([ma, mb, mc], beside, cross) for value in piece]
    if n_outer == 2:
        ready_mats = lambda j: [own_mats[j]] + parts_in[4 * j : 4 * j + 4]
    else:
        all_mats = [lax.all_gather(m, "o", axis=0, tiled=True) for m in own_mats]
        ready_mats = lambda j: [all_mats[j]]
    at_o = lax.axis_index("o")
    bases = [at_o * 4 * shard, (1 - at_o) * 4 * shard] if n_outer == 2 else [0, 0]
    bases = jnp.stack([jnp.int32(base) for base in bases])

    params = dict(compiler_params=pltpu.CompilerParams(vmem_limit_bytes=VMEM_LIMIT))
    specs = [pool_specs(o, w) for o, w in zip(ORDERS, widths)]
    tok_specs = [spec for halves, _ in specs for spec in halves * 2]
    sum_specs = [whole for _, whole in specs]
    slot_spec = lambda width: pl.BlockSpec((BLK, width), lambda g, meta: (g, 0))
    rank_spec = pl.BlockSpec((1, 1, length), lambda g, meta: (g, 0, 0))
    mat_shape = (n_outer * 16, 3, shard, hidden // 4)
    mat_spec = lambda m: pl.BlockSpec(
        m.shape, lambda g, meta: (0, 0, 0, 0), pipeline_mode=pl.Buffered(1)
    )
    down_spec = lambda m: pl.BlockSpec(
        (m.shape[0], 1) + m.shape[2:], lambda g, meta: (0, 2, 0, 0), pipeline_mode=pl.Buffered(1)
    )
    pool_shapes = [jax.ShapeDtypeStruct((2, 2, 2, rows, w), BF) for w in widths]
    slots = 4 * capacity
    groups = steps(4)
    metas = [jnp.concatenate([e[None], groups, bases]).astype(jnp.int32) for e in own]
    chunk = dim // 4
    full = lambda width: pl.BlockSpec((slots, width), lambda i, meta: (0, 0))
    turned = lambda i, meta: jnp.where(meta[5] == 0, i ^ 2, i) if n_outer == 2 else i
    chunk_spec = pl.BlockSpec((slots, chunk), lambda i, meta: (0, turned(i, meta)))
    grad_shape = lambda n: jax.ShapeDtypeStruct((n,) + mat_shape[1:], BF)
    whole = lambda n: pl.BlockSpec((n,) + mat_shape[1:], lambda i, meta: (0, 0, 0, 0))

    def weight_grads_of(meta, saved):
        counts = [4, 4, 4, 4, 16] if n_outer == 2 else [16 * n_outer]
        return pl.pallas_call(
            functools.partial(weight_grad_kernel, chunk // shard * 4),
            grid_spec=pltpu.PrefetchScalarGridSpec(
                num_scalar_prefetch=1,
                grid=(4,),
                in_specs=[chunk_spec, chunk_spec, full(2 * hidden), full(hidden)],
                out_specs=[whole(n) for n in counts],
            ),
            out_shape=[grad_shape(n) for n in counts],
            cost_estimate=cost(9),
            **params,
        )(meta, *saved)

    prev, weighted, saved = [], [], []
    parts_out = []

    def part_out(sends, *markers):
        if n_outer != 2:
            return ()
        parts_out.append(swap(after_all(sends[len(parts_out) % 4], *markers), "o"))
        return (parts_out[-1],)

    for j in range(per_device):
        if j == 0:
            moving = part_in(*pool)
        else:
            prev = together(prev, *moving)
            first_grads = weight_grads_of(after_all(metas[0], prev[0]), saved[0])
            metas[j] = after_all(metas[j], first_grads[0])
            moving = part_out(first_grads[:4], first_grads[0])
            moving += part_out(first_grads[:4], first_grads[0])
        result = pl.pallas_call(
            functools.partial(expert_kernel, len(ready_mats(j)), j == 0),
            grid_spec=pltpu.PrefetchScalarGridSpec(
                num_scalar_prefetch=1,
                grid=(4,),
                in_specs=tok_specs
                + [rank_spec]
                + [mat_spec(m) for m in ready_mats(j)]
                + ([rank_spec] + [slot_spec(w) for w in widths] if j else []),
                out_specs=(sum_specs * 2 if j else [slot_spec(w) for w in widths])
                + [slot_spec(dim), slot_spec(dim), slot_spec(2 * hidden), slot_spec(hidden)],
                scratch_shapes=[pltpu.VMEM((dim, 3 * hidden), BF)],
            ),
            out_shape=(
                pool_shapes * 2 if j else [jax.ShapeDtypeStruct((slots, w), BF) for w in widths]
            )
            + [jax.ShapeDtypeStruct((slots, w), BF) for w in (dim, dim, 2 * hidden, hidden)],
            cost_estimate=cost(29),
            **params,
        )(
            metas[j], *pool, rank[:, j : j + 1], *ready_mats(j),
            *([rank[:, :1], *prev] if j else []),
        )
        prev, kept = (result[:6], result[6:]) if j else (result[:3], result[3:])
        saved.append(kept)

    prev = together(prev, *moving)
    last_grads = []

    moved = []

    def total(mine, parts):
        return (mine.astype(F32) + jnp.concatenate(parts, axis=0).astype(F32)).astype(BF)

    def fill(step, bufs):
        if step == 0:
            last_grads.extend(weight_grads_of(after_all(metas[1], prev[0]), saved[1]))
            return (*part_out(first_grads[:4], *bufs), last_grads[0])
        if step == 1:
            return part_out(first_grads[:4], *bufs) + part_out(last_grads[:4], *bufs)
        return part_out(last_grads[:4], *bufs) if step == 2 else ()

    pairs = scatter_pool(prev[:3], prev[3:], fill)

    after_grad, aog, small, block_out = simple_call(
        back_kernel,
        [((rows, dim), F32), ((rows, dim), BF), ((dim, 128), F32), ((rows, dim), BF)],
        0,
        11,
        5,
    )(after, *pairs[0], *pairs[1], *pairs[2], gains, wob, gates, cot)
    near, cross = swap(aog, "c"), swap(aog, "x")
    moving = part_out(last_grads[:4], pairs[0][1])
    near, cross = together((near, cross), *moving)
    aog_parts = [aog, near, cross, swap(cross, "c")]

    n_tails = 2 if n_dp == 8 else 1
    dests = jnp.bitwise_xor(at_z, steps(8) % 4) * 2 + jnp.bitwise_xor(at_y, steps(8) // 4)
    dests = (dests if n_dp == 8 else steps(n_dp)).astype(jnp.int32)
    tail_shape = lambda width: [((n_dp // n_tails, shard, width), BF)] * n_tails
    sides = simple_call(
        functools.partial(out_grad_kernel, n_tails),
        tail_shape(384),
        2,
        6,
        2,
        scratch=[pltpu.VMEM((length, dim), BF), pltpu.VMEM((dim, 384), BF)],
    )(dests, offs, *aog_parts, mix, small)

    aog_parts = together(aog_parts, *sides)
    moving = part_out(last_grads[:4], cross)
    if n_outer == 2:
        first_sum = after_all(total(first_grads[4], parts_out[:4]), *aog_parts)
    else:
        first_sum, last_sum = (
            lax.psum_scatter(g[0], "o", scatter_dimension=0, tiled=True)
            for g in (first_grads, last_grads)
        )
    moved.append(lax.all_to_all(first_sum, POOL, 0, 0, tiled=True))
    sides = list(sides)
    if n_tails == 2:
        sides[1] = swap(sides[1], "y")
    keep, send, *tails = simple_call(
        functools.partial(attend_backward_kernel, n_tails),
        [((2, rows, dim), F32), ((2, rows, dim), BF)] + tail_shape(640),
        2,
        14,
        60,
        scratch=[
            pltpu.VMEM((length, dim), BF),
            pltpu.VMEM((length, heads), BF),
            pltpu.VMEM((length, 512), BF),
            pltpu.VMEM((2, length, 128), F32),
            pltpu.VMEM((2, length, 128), F32),
            pltpu.VMEM((dim, 640), BF),
        ],
    )(dests, offs, *aog_parts, wqkv, wob, q, kd, vd, lse, start_col, ain, cosine, sine)
    keep, send, *tails = together((keep, send, *tails), *sides, *moving)

    if n_outer == 2:
        last_sum = total(last_grads[4], parts_out[4:])
    got = swap(send, "c")
    cross = swap((keep[1] + got[1].astype(F32)).astype(BF), "x")
    if n_tails == 2:
        add = lambda a, b: (a.astype(F32) + b.astype(F32)).astype(BF)
        side_sums = add(*sides)
        tails[1] = swap(tails[1], "y")

        def reduce_z(sums):
            return [sums[0]] + [
                lax.ppermute(sums[s], ("o", "u"), [(i, i ^ s) for i in range(4)]) for s in (1, 2, 3)
            ]

        side_parts = reduce_z(side_sums)
        *tails, cross, got, moved[0] = together((*tails, cross, got, moved[0]), *side_parts)
        tail_parts = reduce_z(add(*tails))
        side, tail = (sum(p.astype(F32) for p in parts) for parts in (side_parts, tail_parts))
    else:
        side, tail = (
            lax.psum_scatter(part[0].astype(F32).reshape(dim, -1), DP, scatter_dimension=0, tiled=True)
            for part in (sides, tails)
        )
    moved.append(lax.all_to_all(after_all(last_sum, *tails), POOL, 0, 0, tiled=True))
    tokens_grad = simple_call(finish_kernel, [((rows, dim), F32)], 0, 6, 4)(
        tok, keep, got, cross, gains, after_grad
    )[0]

    narrow = jnp.concatenate([side[:, 256 : 256 + experts + 1], tail[:, 512:513]], axis=1)
    narrow = narrow + sum(
        lax.ppermute(narrow, ("x", "c"), [(i, i ^ s) for i in range(4)]) for s in range(1, 4)
    )
    gate_grad, up_grad, down_grad = (
        jnp.concatenate([part[:, m] for part in moved], axis=0).astype(F32) for m in range(3)
    )
    return (
        block_out[None],
        tokens_grad[None],
        narrow[:, experts + 1] / norm_attn.astype(F32),
        tail[:, :256],
        tail[:, 256:384],
        tail[:, 384:512],
        side[:, :256],
        narrow[:, experts],
        narrow[:, :experts],
        gate_grad,
        up_grad,
        down_grad,
    )


def solution(mesh):
    devices = mesh.devices
    fine = Mesh(devices.reshape(devices.shape[0] // 4, 2, 2, 2, 2), ("o", "u", "y", "x", "c"))
    dp, tensor = DP, ("x", "c")
    in_specs = (
        P(dp, tensor, None),
        P(dp, None),
        P(dp, None, None),
        P(dp, None),
        P(dp),
        P(dp, tensor),
        P(dp, tensor),
        P(dp, tensor),
        P(dp, tensor),
        P(dp),
        P(dp, None),
        P(None, dp, tensor),
        P(None, dp, tensor),
        P(None, dp, tensor),
        P(dp, tensor, None),
    )
    out_specs = (
        P(dp, tensor, None),
        P(dp, tensor, None),
        P(dp),
        P(dp, tensor),
        P(dp, tensor),
        P(dp, tensor),
        P(dp, tensor),
        P(dp),
        P(dp, None),
        P(None, dp, tensor),
        P(None, dp, tensor),
        P(None, dp, tensor),
    )
    return jax.shard_map(local, mesh=fine, in_specs=in_specs, out_specs=out_specs, check_vma=False)
```

```python
import functools
import math

import jax
import jax.numpy as jnp
from jax import lax
from jax.experimental import pallas as pl
from jax.experimental.pallas import tpu as pltpu
from jax.sharding import Mesh, PartitionSpec as P

HEAD_SIZE = 64
EPSILON = 1e-06
FLOOR_SCORE = -1e30
VMEM_LIMIT = 60 * 1024 * 1024
DP = ("o", "u", "y")
POOL = ("u", "y", "x", "c")
ORDERS = (("u", "y", "x"), ("y", "x", "u"), ("x", "u", "y"))
TOK = (512, 256, 256)
SECOND = (384, 256, 384)
NOTES = 128
PARTS_IN = ((3, 4, 4, 2, 3), (8, 3, 5))
PARTS_OUT = ((7, 3, 6), (2, 4, 2, 3, 5))
BLK = 256
BF = jnp.bfloat16
F32 = jnp.float32


def after_all(value, *others):
    return lax.optimization_barrier((value,) + others)[0]


def together(values, *others):
    return lax.optimization_barrier((*values, *others))[: len(values)]


def cuts(dim):
    found, a, b = [], 0, 0
    for i, (first, second) in enumerate(zip(TOK, SECOND)):
        found.append((a, a + first, b, b + second, first + (NOTES if i == 2 else 0)))
        a, b = a + first, b + second
    assert a == b == dim
    return found


def swap(value, axis):
    return lax.ppermute(value, axis, [(0, 1), (1, 0)])


def mm(left, right):
    return lax.dot_general(left, right, (((1,), (0,)), ((), ())), preferred_element_type=F32)


def mm_nt(left, right):
    return lax.dot_general(left, right, (((1,), (1,)), ((), ())), preferred_element_type=F32)


def mm_tn(left, right):
    return lax.dot_general(left, right, (((0,), (0,)), ((), ())), preferred_element_type=F32)


def lanes(shape):
    return lax.broadcasted_iota(jnp.int32, shape, 1)


def turn_halves(value):
    first = lanes(value.shape) % HEAD_SIZE < HEAD_SIZE // 2
    half = HEAD_SIZE // 2
    return jnp.where(first, pltpu.roll(value, 128 - half, 1), pltpu.roll(value, half, 1))


def both_halves(value, which):
    low = lanes(value.shape) < HEAD_SIZE
    turned = pltpu.roll(value, HEAD_SIZE, 1)
    return jnp.where(low, value, turned) if which == 0 else jnp.where(low, turned, value)


def stack_heads(pair):
    low = lanes(pair.shape) < HEAD_SIZE
    zero = jnp.zeros_like(pair)
    return jnp.concatenate([jnp.where(low, pair, zero), jnp.where(low, zero, pair)], axis=0)


def join_heads(stacked):
    rows = stacked.shape[0] // 2
    low = lanes((rows, stacked.shape[1])) < HEAD_SIZE
    return jnp.where(low, stacked[:rows], stacked[rows:])


def allowed_keys(start_col, block, width):
    rows = start_col.shape[0]
    cols = lax.broadcasted_iota(jnp.int32, (rows, width), 1)
    row_ids = block * rows + lax.broadcasted_iota(jnp.int32, (rows, width), 0)
    keep = (cols >= start_col) & (cols <= row_ids)
    return jnp.concatenate([keep, keep], axis=0)


def attend_forward_kernel(n_parts, shard, table, offs, t0, t1, t2, t3, *refs):
    parts, refs = refs[:n_parts], refs[n_parts:]
    gain_in, cosine, sine, start, ain_o, wqkv_o, gains_o, q_o, kd_o, vd_o, mix_o, lse_o = refs
    gains_o[...] = gain_in[...]
    base = 0
    for part in parts:
        for b in range(part.shape[0]):
            at = pl.multiple_of(table[base + b] * shard, shard)
            wqkv_o[pl.ds(at, shard), :] = part[b, :shard, :]
            if shard == 128:
                note = part[b, shard:, :128].astype(F32)
                for row in range(2):
                    gains_o[row : row + 1, pl.ds(at, 128)] = note[row : row + 1]
        base += part.shape[0]
    gain = gains_o[0:1, :]
    for r, piece in enumerate((t0, t1, t2, t3)):
        at = pl.multiple_of(offs[r], BLK)
        rows = pl.ds(at, BLK)
        value = piece[...].astype(F32)
        factor = lax.rsqrt(jnp.mean(value * value, axis=-1, keepdims=True) + EPSILON)
        normed = (value * factor * gain).astype(BF)
        ain_o[rows, :] = normed
        qkv = mm(normed, wqkv_o[...])
        cos_b, sin_b = cosine[rows, :], sine[rows, :]
        for part in range(3):
            raw = qkv[:, part * 128 : part * 128 + 128]
            turned = (raw * cos_b + turn_halves(raw) * sin_b).astype(BF)
            if part < 2:
                q_o[rows, part * 128 : part * 128 + 128] = turned * 0.125
            else:
                wide = turned.astype(F32)
                for kv in range(2):
                    kd_o[kv, rows, :] = both_halves(wide, kv).astype(BF)
        value_rows = qkv[:, 384:512].astype(BF).astype(F32)
        for kv in range(2):
            vd_o[kv, rows, :] = both_halves(value_rows, kv).astype(BF)
    total = ain_o.shape[0]
    for block in range(total // BLK):
        width = (block + 1) * BLK
        rows = pl.ds(block * BLK, BLK)
        keep = allowed_keys(start[rows, :], block, width)
        logs = jnp.zeros((BLK, 128), F32)
        for kv in range(2):
            query = stack_heads(q_o[rows, kv * 128 : kv * 128 + 128])
            scores = jnp.where(keep, mm_nt(query, kd_o[kv, :width, :]), FLOOR_SCORE)
            top = jnp.max(scores, axis=-1, keepdims=True)
            lifted = jnp.exp(scores - top)
            summed = jnp.sum(lifted, axis=-1, keepdims=True)
            shares = (lifted * (1.0 / summed)).astype(BF)
            mixed = join_heads(mm(shares, vd_o[kv, :width, :]))
            mix_o[rows, kv * 128 : kv * 128 + 128] = mixed.astype(BF)
            log_total = top + jnp.log(summed)
            lane = lanes(logs.shape)
            logs = jnp.where(lane == 2 * kv, log_total[:BLK], logs)
            logs = jnp.where(lane == 2 * kv + 1, log_total[BLK:], logs)
        lse_o[rows, :] = logs


def project_kernel(n_parts, shard, table, offs, mix, *refs):
    parts, (keep_o, send_o, wob) = refs[:n_parts], refs[n_parts:]
    base = 0
    for part in parts:
        for b in range(part.shape[0]):
            at = pl.multiple_of(table[base + b] * shard, shard)
            wob[pl.ds(at, shard), :] = part[b]
        base += part.shape[0]
    for r in range(4):
        rows = pl.ds(pl.multiple_of(offs[r], BLK), BLK)
        part = mm_nt(mix[rows, :], wob[:, :256])
        if r % 2 == 0:
            keep_o[r // 2] = part
        else:
            send_o[r // 2] = part.astype(BF)


def attend_backward_kernel(
    n_blocks, dests, offs, a0, a1, a2, a3, wqkv, wob, q, kd, vd, lse, start, ain, cosine, sine,
    keep_o, send_o, *refs,
):
    wg_o, (aog, mgrad, dqkv, dk, dv, flat) = refs[:n_blocks], refs[n_blocks:]
    total = ain.shape[0]
    for r, piece in enumerate((a0, a1, a2, a3)):
        aog[pl.ds(pl.multiple_of(offs[r], BLK), BLK), :] = piece[...]
    mgrad[...] = mm(aog[...], wob[:, :256]).astype(BF)
    dk[...] = jnp.zeros_like(dk)
    dv[...] = jnp.zeros_like(dv)
    for block in range(total // BLK):
        width = (block + 1) * BLK
        rows = pl.ds(block * BLK, BLK)
        keep = allowed_keys(start[rows, :], block, width)
        logs = lse[rows, :]
        lane = lanes(logs.shape)
        cos_b, sin_b = cosine[rows, :], sine[rows, :]
        for kv in range(2):
            cols = slice(kv * 128, kv * 128 + 128)
            query = stack_heads(q[rows, cols])
            out_grad = stack_heads(mgrad[rows, cols])
            log_total = jnp.concatenate(
                [
                    jnp.sum(jnp.where(lane == 2 * kv + h, logs, 0.0), axis=1, keepdims=True)
                    for h in range(2)
                ],
                axis=0,
            )
            keys = kd[kv, :width, :]
            scores = jnp.where(keep, mm_nt(query, keys), FLOOR_SCORE)
            shares = jnp.exp(scores - log_total)
            share_grad = mm_nt(out_grad, vd[kv, :width, :])
            inner = jnp.sum(shares * share_grad, axis=-1, keepdims=True)
            score_grad = (shares * (share_grad - inner)).astype(BF)
            query_grad = join_heads(mm(score_grad, keys)) * 0.125
            query_grad = query_grad * cos_b - turn_halves(query_grad) * sin_b
            dqkv[rows, cols] = query_grad.astype(BF)
            dk[kv, :width, :] += mm_tn(score_grad, query)
            dv[kv, :width, :] += mm_tn(shares.astype(BF), out_grad)
    joined = []
    for acc in (dk, dv):
        pair = [acc[kv] + pltpu.roll(acc[kv], HEAD_SIZE, 1) for kv in range(2)]
        joined.append(jnp.where(lanes(pair[0].shape) < HEAD_SIZE, pair[0], pair[1]))
    key_grad = joined[0] * cosine[...] - turn_halves(joined[0]) * sine[...]
    dqkv[:, 256:384] = key_grad.astype(BF)
    dqkv[:, 384:512] = joined[1].astype(BF)
    flat[:, :512] = mm_tn(ain[...], dqkv[...]).astype(BF)
    ones = jnp.ones((BLK, 128), BF)
    gain_sum = jnp.zeros((ain.shape[1], 128), F32)
    for r in range(4):
        rows = pl.ds(pl.multiple_of(offs[r], BLK), BLK)
        part = mm_nt(dqkv[rows, :], wqkv[...])
        gain_sum += mm_tn((part * ain[rows, :].astype(F32)).astype(BF), ones)
        if r % 2 == 0:
            keep_o[r // 2] = part
        else:
            send_o[r // 2] = part.astype(BF)
    flat[:, 512:] = gain_sum.astype(BF)
    spread(flat, dests, wg_o)


def spread(flat, dests, outs):
    done = 0
    for out in outs:
        shard = out.shape[1]
        for i in range(out.shape[0]):
            at = pl.multiple_of(dests[done + i] * shard, shard)
            out[i] = flat[pl.ds(at, shard), :]
        done += out.shape[0]


def out_grad_kernel(n_blocks, dests, offs, a0, a1, a2, a3, mix, small, *refs):
    outs, (aog, flat) = refs[:n_blocks], refs[n_blocks:]
    for r, piece in enumerate((a0, a1, a2, a3)):
        aog[pl.ds(pl.multiple_of(offs[r], BLK), BLK), :] = piece[...]
    flat[:, :256] = mm_tn(aog[...], mix[...]).astype(BF)
    flat[:, 256:] = small[...].astype(BF)
    spread(flat, dests, outs)


def route_kernel(
    tok, keep, got, cross, gains, wob, routes, cot, after_o, ma_o, mb_o, mc_o, gates_o
):
    after = tok[...].astype(F32) + (keep[0] + got[0].astype(F32) + cross[...].astype(F32))
    after_o[...] = after
    factor = lax.rsqrt(jnp.mean(after * after, axis=-1, keepdims=True) + EPSILON)
    moe_in = (after * factor * gains[1:2, :]).astype(BF)
    logits = mm(moe_in, wob[:, 256:])
    lane = lanes(logits.shape)
    routed = lane < 0
    for k in range(routes.shape[1]):
        routed = routed | (routes[:, k : k + 1] == lane)
    top = jnp.max(jnp.where(routed, logits, FLOOR_SCORE), axis=1, keepdims=True)
    lifted = jnp.where(routed, jnp.exp(jnp.where(routed, logits - top, 0.0)), 0.0)
    gates = lifted / jnp.sum(lifted, axis=1, keepdims=True)
    gates_o[...] = gates
    high = gates.astype(BF).astype(F32)
    middle = (gates - high).astype(BF).astype(F32)
    low = gates - high - middle
    extra = high + pltpu.roll(middle, 32, 1) + pltpu.roll(low, 64, 1)
    for out, (a, b, c, d, at) in zip((ma_o, mb_o, mc_o), cuts(cot.shape[1])):
        out[:, : b - a] = moe_in[:, a:b]
        out[:, at:] = cot[:, c:d]
    mc_o[:, TOK[2] : TOK[2] + NOTES] = extra.astype(BF)


def place_weights(meta, parts, mat, kinds):
    hidden = mat.shape[1] // len(kinds)
    done = 0
    for part in parts:
        shard = part.shape[2]
        for b in range(part.shape[0]):
            block = done + b
            at = meta[5 + block // 16] + block % 16 // 4 * shard if len(parts) > 1 else block // 4 * shard
            at = pl.multiple_of(at, shard)
            for i, m in enumerate(kinds):
                col = i * hidden + block % 4 * 128
                mat[pl.ds(at, shard), col : col + 128] = part[b, m]
        done += part.shape[0]


def one_hot(rank):
    row_ids = lax.broadcasted_iota(jnp.int32, (BLK, rank.shape[-1]), 0)
    return jnp.where(rank == row_ids, 1.0, 0.0).astype(BF)


def expert_kernel(n_mats, first, meta, *refs):
    refs = list(refs)
    take = lambda n: [refs.pop(0) for _ in range(n)]
    pieces = [take(4) for _ in range(3)]
    (rank,) = take(1)
    mats = take(n_mats)
    prev_rank, prev = (None, None) if first else (take(1)[0], take(3))
    outs = take(3 if first else 6)
    pick_o, dy_o, pre_o, weighted_o, mat = take(5)
    hidden = mat.shape[1] // 3
    own_expert = meta[0]

    @pl.when(pl.program_id(0) == 0)
    def _():
        place_weights(meta, mats, mat, (0, 1, 2))

    pick = one_hot(rank[0])
    half = pick.shape[1] // 2
    pick_k, pick_c = pick[:, :half], pick[:, half:]
    step = pl.program_id(0)

    def rows_of(i, side):
        low, high = (ref[...].reshape(-1, ref.shape[-1]) for ref in pieces[i][2 * side : 2 * side + 2])
        if i == 0:
            return jnp.concatenate([low, high], axis=0)
        return jnp.where((step // 2 if i == 1 else step % 2) == 0, low, high)

    spans = cuts(pick_o.shape[1])
    for i, (a, b, c, d, at) in enumerate(spans):
        got = mm(pick_k, rows_of(i, 0)) + mm(pick_c, rows_of(i, 1))
        pick_o[:, a:b] = got[:, : b - a].astype(BF)
        dy_o[:, c:d] = got[:, at:].astype(BF)
    extra = got[:, TOK[2] : TOK[2] + NOTES]
    lane = lanes(extra.shape)
    mine = (lane % 32 == own_expert) & (lane < 96)
    gate = jnp.sum(jnp.where(mine, extra, 0.0), axis=1, keepdims=True)
    picked, dy = pick_o[...], dy_o[...]
    gate_pre = mm(picked, mat[:, :hidden])
    up_pre = mm(picked, mat[:, hidden : 2 * hidden])
    back = mm(dy, mat[:, 2 * hidden :])
    sigma = 1.0 / (1.0 + jnp.exp(-gate_pre))
    active = gate_pre * sigma
    hid = active * up_pre
    gate_dot = jnp.sum(hid.astype(BF).astype(F32) * back, axis=1, keepdims=True)
    weighted_o[...] = (gate * hid).astype(BF)
    back = back * gate
    pre_o[:, :hidden] = (back * up_pre * sigma * (1.0 + gate_pre * (1.0 - sigma))).astype(BF)
    pre_o[:, hidden:] = (back * active).astype(BF)
    picked_grad = mm_nt(pre_o[...], mat[:, : 2 * hidden]).astype(BF)
    expert_out = mm_nt(weighted_o[...], mat[:, 2 * hidden :]).astype(BF)
    dot_high = gate_dot.astype(BF).astype(F32)
    dot_low = gate_dot - dot_high
    note = jnp.where(lane == own_expert, dot_high, 0.0)
    note = jnp.where(lane == own_expert + 32, dot_low, note).astype(BF)
    if not first:
        pick = jnp.concatenate([one_hot(prev_rank[0]), pick], axis=0)
    for i, (a, b, c, d, _) in enumerate(spans):
        part = [picked_grad[:, a:b]] + ([note] if i == 2 else []) + [expert_out[:, c:d]]
        part = jnp.concatenate(part, axis=1)
        if first:
            outs[i][...] = part
            continue
        part = jnp.concatenate([prev[i][...], part], axis=0)
        for side in range(2):
            summed = mm_tn(pick[:, side * half : side * half + half], part)
            out = outs[i + 3 * side]
            out[...] = summed.astype(BF).reshape(out.shape)


def weight_grad_kernel(blocks, meta, picked, dy, pre, weighted, *outs):
    shard = outs[0].shape[2]
    grads = (mm_tn(picked[...], pre[...]).astype(BF), mm_tn(dy[...], weighted[...]).astype(BF))
    hidden = weighted.shape[1]
    for step in range(4):

        @pl.when(pl.program_id(0) == step)
        def _(step=step):
            for b in range(blocks):
                block, n = step * blocks + b, 0
                while block >= outs[n].shape[0]:
                    block -= outs[n].shape[0]
                    n += 1
                rows = slice(b // 4 * shard, b // 4 * shard + shard)
                for m in range(3):
                    col = m % 2 * hidden + b % 4 * 128
                    outs[n][block, m] = grads[m // 2][rows, col : col + 128]


def back_kernel(
    after, ak, ar, bk, br, ck, cr, gains, wob, gates, cot, after_grad_o, aog_o, small_o, block_o
):
    both = lambda a, b: a[...].astype(F32) + b[...].astype(F32)
    sums = [both(ak, ar), both(bk, br), both(ck, cr)]
    spans = cuts(after.shape[1])
    upstream = jnp.concatenate([v[:, : b - a] for v, (a, b, *_) in zip(sums, spans)], axis=1)
    moe_out = jnp.concatenate([v[:, span[4] :] for v, span in zip(sums, spans)], axis=1)
    block_o[...] = (after[...] + moe_out).astype(BF)
    extra = sums[2][:, TOK[2] : TOK[2] + NOTES]
    lane = lanes(extra.shape)
    gate_dot = jnp.where(lane < 32, extra + pltpu.roll(extra, 96, 1), 0.0)
    share = gates[...]
    logit_grad = share * (gate_dot - jnp.sum(share * gate_dot, axis=1, keepdims=True))
    high = logit_grad.astype(BF)
    low = (logit_grad - high.astype(F32)).astype(BF)
    router = wob[:, 256:]
    gain = gains[1:2, :]
    upstream += mm_nt(high, router) + mm_nt(low, router)
    value = after[...]
    factor = lax.rsqrt(jnp.mean(value * value, axis=-1, keepdims=True) + EPSILON)
    normed = value * factor
    moe_in = (normed * gain).astype(BF)
    scaled = upstream * gain
    inward = factor * (scaled - normed * jnp.mean(scaled * normed, axis=-1, keepdims=True))
    after_grad = cot[...].astype(F32) + inward
    after_grad_o[...] = after_grad
    aog_o[...] = after_grad.astype(BF)
    column = jnp.where(lane == 32, 1.0, 0.0).astype(BF)
    small_o[...] = (
        mm_tn(moe_in, high) + mm_tn(moe_in, low) + mm_tn((upstream * normed).astype(BF), column)
    )


def finish_kernel(tok, keep, got, cross, gains, after_grad, out):
    upstream = keep[0] + got[0].astype(F32) + cross[...].astype(F32)
    value = tok[...].astype(F32)
    factor = lax.rsqrt(jnp.mean(value * value, axis=-1, keepdims=True) + EPSILON)
    normed = value * factor
    scaled = upstream * gains[0:1, :]
    inward = factor * (scaled - normed * jnp.mean(scaled * normed, axis=-1, keepdims=True))
    out[...] = after_grad[...] + inward


def spec_of(space):
    return pl.BlockSpec(memory_space=space)


def cost(micros):
    return pl.CostEstimate(flops=1, bytes_accessed=int(micros * 750000), transcendentals=0)


def simple_call(kernel, outs, n_scalar, n_in, micros, scratch=()):
    return pl.pallas_call(
        kernel,
        out_shape=[jax.ShapeDtypeStruct(s, d) for s, d in outs],
        in_specs=[spec_of(pltpu.SMEM)] * n_scalar + [spec_of(pltpu.VMEM)] * n_in,
        out_specs=[spec_of(pltpu.VMEM)] * len(outs),
        scratch_shapes=list(scratch),
        compiler_params=pltpu.CompilerParams(vmem_limit_bytes=VMEM_LIMIT),
        cost_estimate=cost(micros),
    )


def gather_pool(pieces, beside, ready):
    bufs = pieces
    came = (ready,)
    for step in range(3):
        moving = beside(step)(*came)
        came = [swap(buf, order[step]) for buf, order in zip(bufs, ORDERS)]
        came = together(came, *moving)
        if step < 2:
            bufs = [jnp.stack([buf, new]) for buf, new in zip(bufs, came)]
    moving = beside(3)(*came)
    near = [swap(after_all(value, *came), "c") for value in bufs]
    far = [swap(value, "c") for value in came]
    values = together((*near, *far), *moving)
    return list(zip(bufs, came, values[:3], values[3:]))


def scatter_pool(kept, other, fill):
    add = lambda a, b: (a.astype(F32) + b.astype(F32)).astype(BF)
    moving = fill(0, other)
    came = together([swap(send, "c") for send in other], *moving)
    before = list(zip(kept, came))
    for step in range(1, 4):
        sends = together([add(a[1], b[1]) for a, b in before])
        moving = fill(step, came)
        came = [swap(send, order[3 - step]) for send, order in zip(sends, ORDERS)]
        flat = together([value for pair in before for value in pair], *sends)
        keeps = [add(flat[2 * i][0], flat[2 * i + 1][0]) for i in range(3)]
        values = together((*came, *keeps), *moving)
        before = list(zip(values[3:], values[:3]))
    return before


def gather_tensor(value):
    cross = swap(value, "x")
    return [value, swap(value, "c"), cross, swap(cross, "c")]


def sum_tensor(keep, send):
    got = swap(send, "c")
    cross = swap((keep[1] + got[1].astype(F32)).astype(BF), "x")
    return got, cross


def pool_specs(order, width):
    def spec(axes, half):
        shape = tuple(2 if axis == "x" else 1 for axis in reversed(axes)) + (BLK, width)

        def index(g, meta):
            place = {"x": 0, "u": g // 2, "y": g % 2}
            if half is not None and order[2] == "u":
                place["y"] = jnp.where(g // 2 == half, g % 2, 1 - half)
            return tuple(place[axis] for axis in reversed(axes)) + (0, 0)

        return pl.BlockSpec(shape, index)

    return [spec(order[:2], 0), spec(order[:2], 1)], spec(order, None)


def local(
    tokens, segments, routes, priority, norm_attn, w_query, w_key, w_value, w_out, norm_moe,
    w_router, w_gate, w_up, w_down, cotangent,
):
    _, rows, dim = tokens.shape
    n_outer = lax.axis_size("o")
    n_dp = 4 * n_outer
    shard = w_query.shape[0]
    length = 4 * rows
    top = routes.shape[2]
    experts = w_gate.shape[0]
    per_device = experts // 16
    capacity = length * top // experts
    hidden = 4 * w_gate.shape[2]
    widths = [at + d - c for _, _, c, d, at in cuts(dim)]
    at_x, at_c = lax.axis_index("x"), lax.axis_index("c")
    at_t = at_x * 2 + at_c
    at_pool = lax.axis_index(POOL)

    at_dp, at_z, at_y = lax.axis_index(DP), lax.axis_index(("o", "u")), lax.axis_index("y")
    steps = lambda n: jnp.arange(n, dtype=jnp.int32)

    tok = tokens[0]
    cot = cotangent[0]
    tok_near, tok_cross = swap(tok, "c"), swap(tok, "x")
    own_mats = []

    def weight_part(j):
        return jnp.stack([w[j * 16 : (j + 1) * 16] for w in (w_gate, w_up, w_down)], axis=1)

    parts_in = [[], []]

    def part_in(*markers):
        if n_outer != 2:
            return ()
        j = 1 if len(parts_in[0]) == len(PARTS_IN[0]) else 0
        count, i = PARTS_IN[j], len(parts_in[j])
        at = sum(count[:i])
        part = after_all(own_mats[j][at : at + count[i]], *markers)
        parts_in[j].append(swap(part, "o"))
        return (parts_in[j][-1],)

    first_mats = after_all(weight_part(0), tok_near)
    first_mats = lax.all_to_all(first_mats, POOL, 0, 0, tiled=True)

    seg = segments[0]
    start = jnp.zeros_like(seg)
    for s in range(1, 5):
        start = jnp.where(seg >= s, jnp.sum((seg < s).astype(jnp.int32)), start)
    place = (jnp.arange(length, dtype=jnp.int32) - start).astype(F32)
    lane = jnp.arange(128, dtype=jnp.int32)
    half = HEAD_SIZE // 2
    inverse = jnp.exp((lane % half).astype(F32) * (-2.0 * math.log(10000.0) / HEAD_SIZE))
    angle = place[:, None] * inverse[None, :]
    cosine = jnp.cos(angle)
    sine = jnp.sin(angle) * jnp.where(lane % HEAD_SIZE < half, -1.0, 1.0)
    start_col = start[:, None]

    notes = jnp.pad(jnp.stack([norm_attn, norm_moe]), ((0, 14), (0, 512 - shard)))
    pack = jnp.concatenate([w_query, w_key, w_value], axis=1)
    pack_b = jnp.concatenate([w_out, w_router, jnp.zeros((shard, 128 - experts), BF)], axis=1)
    if n_dp == 8:
        pack = jnp.concatenate(
            [jnp.concatenate([pack, pack_b], axis=1), jnp.pad(notes, ((0, 0), (0, 384)))], axis=0
        )
        rest = [lax.ppermute(pack, ("o", "u"), [(i, i ^ s) for i in range(4)]) for s in (1, 2, 3)]
        *rest, tok_near, tok_cross = together(
            (*rest, tok_near, tok_cross), cosine, sine, start_col
        )
        near = jnp.stack([pack, *rest])
        wa = [near[:, :, :512]]
        wa.append(swap(wa[0], "y"))
        wb = [near[:, :shard, 512:]]
        wb.append(swap(after_all(wb[0], wa[1]), "y"))
        table = jnp.bitwise_xor(at_z, steps(8) % 4) * 2 + jnp.bitwise_xor(at_y, steps(8) // 4)
        gains = jnp.zeros((8, dim), F32)
    else:
        wa = [lax.all_gather(pack, DP, axis=0)]
        wb = [lax.all_gather(pack_b, DP, axis=0)]
        table = steps(n_dp)
        gains = jnp.stack([lax.all_gather(g, DP, axis=0, tiled=True) for g in (norm_attn, norm_moe)])
        gains = jnp.pad(gains.astype(F32), ((0, 6), (0, 0)))

    table = table.astype(jnp.int32)
    own_mats.append(first_mats)
    moving = part_in(wa[0])
    next_part = weight_part(1)
    tok_parts = [tok, tok_near, tok_cross, swap(tok_cross, "c")]
    *tok_parts, next_part = together((*tok_parts, next_part), *wa, *moving)
    own_mats.append(lax.all_to_all(next_part, POOL, 0, 0, tiled=True))
    moving = part_in(tok_parts[0])
    plan = after_all(jnp.concatenate([routes[0].T, priority], axis=0), tok_parts[0])
    plan = jnp.stack([plan, swap(plan, "y")])
    offs = (jnp.bitwise_xor(at_t, steps(4)) * rows).astype(jnp.int32)
    heads = w_query.shape[1]
    ain, wqkv, gains, q, kd, vd, mix, lse = simple_call(
        functools.partial(attend_forward_kernel, len(wa), shard),
        [
            ((length, dim), BF),
            ((dim, 512), BF),
            ((8, dim), F32),
            ((length, heads), BF),
            ((2, length, 128), BF),
            ((2, length, 128), BF),
            ((length, heads), BF),
            ((length, 128), F32),
        ],
        2,
        8 + len(wa),
        11,
    )(table, offs, *tok_parts, *wa, gains, cosine, sine, start_col)
    keep, send, wob = simple_call(
        functools.partial(project_kernel, len(wb), shard),
        [((2, rows, dim), F32), ((2, rows, dim), BF), ((dim, 384), BF)],
        2,
        1 + len(wb),
        4,
    )(table, offs, mix, *wb)
    keep, send, wob = together((keep, send, wob), *moving)
    moving = part_in(mix)
    got, cross = sum_tensor(keep, send)
    got, cross, plan, own_mats[1] = together((got, cross, plan, own_mats[1]), *moving)
    route_col = lax.dynamic_slice_in_dim(routes[0], at_t * rows, rows, 0)
    after, ma, mb, mc, gates = simple_call(
        route_kernel,
        [
            ((rows, dim), F32),
            *[((rows, width), BF) for width in widths],
            ((rows, 128), F32),
        ],
        0,
        8,
        4,
    )(tok, keep, got, cross, gains, wob, route_col, cot)

    own = [j * 16 + at_pool for j in range(per_device)]
    plan = jnp.concatenate([plan, swap(plan, "u")], axis=0)
    hits = jnp.stack([jnp.any(plan[:, :top] == e, axis=1) for e in own], axis=1)
    first = plan[:, top]
    less = (first[:, :, None] < first[:, None, :]).astype(BF)
    rank = jnp.einsum("gjs,gst->gjt", hits.astype(BF), less, preferred_element_type=F32)
    rank = rank.astype(jnp.int32)
    rank = jnp.where(hits & (rank < capacity), rank, -1)
    rank = rank.reshape(4, per_device, 2, 2, rows)
    rank = jnp.where(at_x == 1, rank[:, :, ::-1], rank)
    rank = jnp.where(at_c == 1, rank[:, :, :, ::-1], rank)
    rank = rank.swapaxes(2, 3).reshape(4, per_device, length)

    def beside(step):
        return lambda *markers: part_in(*markers) + (
            (plan, plan, rank)[step : step + 1]
        )

    pool = [value for piece in gather_pool([ma, mb, mc], beside, cross) for value in piece]
    if n_outer == 2:
        ready_mats = lambda j: [own_mats[j]] + parts_in[j]
    else:
        all_mats = [lax.all_gather(m, "o", axis=0, tiled=True) for m in own_mats]
        ready_mats = lambda j: [all_mats[j]]
    at_o = lax.axis_index("o")
    bases = [at_o * 4 * shard, (1 - at_o) * 4 * shard] if n_outer == 2 else [0, 0]
    bases = jnp.stack([jnp.int32(base) for base in bases])

    params = dict(compiler_params=pltpu.CompilerParams(vmem_limit_bytes=VMEM_LIMIT))
    specs = [pool_specs(o, w) for o, w in zip(ORDERS, widths)]
    tok_specs = [spec for halves, _ in specs for spec in halves * 2]
    sum_specs = [whole for _, whole in specs]
    slot_spec = lambda width: pl.BlockSpec((BLK, width), lambda g, meta: (g, 0))
    rank_spec = pl.BlockSpec((1, 1, length), lambda g, meta: (g, 0, 0))
    mat_shape = (n_outer * 16, 3, shard, hidden // 4)
    mat_spec = lambda m: pl.BlockSpec(
        m.shape, lambda g, meta: (0, 0, 0, 0), pipeline_mode=pl.Buffered(1)
    )
    down_spec = lambda m: pl.BlockSpec(
        (m.shape[0], 1) + m.shape[2:], lambda g, meta: (0, 2, 0, 0), pipeline_mode=pl.Buffered(1)
    )
    pool_shapes = [jax.ShapeDtypeStruct((2, 2, 2, rows, w), BF) for w in widths]
    slots = 4 * capacity
    groups = steps(4)
    metas = [jnp.concatenate([e[None], groups, bases]).astype(jnp.int32) for e in own]
    chunk = dim // 4
    full = lambda width: pl.BlockSpec((slots, width), lambda i, meta: (0, 0))
    turned = lambda i, meta: jnp.where(meta[5] == 0, i ^ 2, i) if n_outer == 2 else i
    chunk_spec = pl.BlockSpec((slots, chunk), lambda i, meta: (0, turned(i, meta)))
    grad_shape = lambda n: jax.ShapeDtypeStruct((n,) + mat_shape[1:], BF)
    whole = lambda n: pl.BlockSpec((n,) + mat_shape[1:], lambda i, meta: (0, 0, 0, 0))

    def weight_grads_of(meta, saved, j):
        counts = [*PARTS_OUT[j], 16] if n_outer == 2 else [16 * n_outer]
        return pl.pallas_call(
            functools.partial(weight_grad_kernel, chunk // shard * 4),
            grid_spec=pltpu.PrefetchScalarGridSpec(
                num_scalar_prefetch=1,
                grid=(4,),
                in_specs=[chunk_spec, chunk_spec, full(2 * hidden), full(hidden)],
                out_specs=[whole(n) for n in counts],
            ),
            out_shape=[grad_shape(n) for n in counts],
            cost_estimate=cost(9),
            **params,
        )(meta, *saved)

    prev, weighted, saved = [], [], []
    parts_out, all_grads = [[], []], [[], []]

    def part_out(j, *markers):
        if n_outer != 2:
            return ()
        part = all_grads[j][len(parts_out[j])]
        parts_out[j].append(swap(after_all(part, *markers), "o"))
        return (parts_out[j][-1],)

    for j in range(per_device):
        if j == 0:
            moving = part_in(*pool)
        else:
            prev = together(prev, *moving)
            first_grads = weight_grads_of(after_all(metas[0], prev[0]), saved[0], 0)
            metas[j] = after_all(metas[j], first_grads[0])
            all_grads[0].extend(first_grads)
            moving = part_out(0, first_grads[0])
        result = pl.pallas_call(
            functools.partial(expert_kernel, len(ready_mats(j)), j == 0),
            grid_spec=pltpu.PrefetchScalarGridSpec(
                num_scalar_prefetch=1,
                grid=(4,),
                in_specs=tok_specs
                + [rank_spec]
                + [mat_spec(m) for m in ready_mats(j)]
                + ([rank_spec] + [slot_spec(w) for w in widths] if j else []),
                out_specs=(sum_specs * 2 if j else [slot_spec(w) for w in widths])
                + [slot_spec(dim), slot_spec(dim), slot_spec(2 * hidden), slot_spec(hidden)],
                scratch_shapes=[pltpu.VMEM((dim, 3 * hidden), BF)],
            ),
            out_shape=(
                pool_shapes * 2 if j else [jax.ShapeDtypeStruct((slots, w), BF) for w in widths]
            )
            + [jax.ShapeDtypeStruct((slots, w), BF) for w in (dim, dim, 2 * hidden, hidden)],
            cost_estimate=cost(29),
            **params,
        )(
            metas[j], *pool, rank[:, j : j + 1], *ready_mats(j),
            *([rank[:, :1], *prev] if j else []),
        )
        prev, kept = (result[:6], result[6:]) if j else (result[:3], result[3:])
        saved.append(kept)

    prev = together(prev, *moving)
    last_grads = all_grads[1]

    moved = []

    def total(mine, parts):
        return (mine.astype(F32) + jnp.concatenate(parts, axis=0).astype(F32)).astype(BF)

    def fill(step, bufs):
        if step == 0:
            last_grads.extend(weight_grads_of(after_all(metas[1], prev[0]), saved[1], 1))
            return (*part_out(0, *bufs), last_grads[0])
        return (part_out(0, *bufs) if step == 1 else ()) + part_out(1, *bufs)

    pairs = scatter_pool(prev[:3], prev[3:], fill)

    after_grad, aog, small, block_out = simple_call(
        back_kernel,
        [((rows, dim), F32), ((rows, dim), BF), ((dim, 128), F32), ((rows, dim), BF)],
        0,
        11,
        5,
    )(after, *pairs[0], *pairs[1], *pairs[2], gains, wob, gates, cot)
    near, cross = swap(aog, "c"), swap(aog, "x")
    moving = part_out(1, pairs[0][1])
    near, cross = together((near, cross), *moving)
    aog_parts = [aog, near, cross, swap(cross, "c")]

    n_tails = 2 if n_dp == 8 else 1
    dests = jnp.bitwise_xor(at_z, steps(8) % 4) * 2 + jnp.bitwise_xor(at_y, steps(8) // 4)
    dests = (dests if n_dp == 8 else steps(n_dp)).astype(jnp.int32)
    tail_shape = lambda width: [((n_dp // n_tails, shard, width), BF)] * n_tails
    sides = simple_call(
        functools.partial(out_grad_kernel, n_tails),
        tail_shape(384),
        2,
        6,
        2,
        scratch=[pltpu.VMEM((length, dim), BF), pltpu.VMEM((dim, 384), BF)],
    )(dests, offs, *aog_parts, mix, small)

    aog_parts = together(aog_parts, *sides)
    moving = part_out(1, cross)
    if n_outer == 2:
        first_sum = after_all(total(first_grads[-1], parts_out[0]), *aog_parts)
    else:
        first_sum, last_sum = (
            lax.psum_scatter(g[0], "o", scatter_dimension=0, tiled=True)
            for g in (first_grads, last_grads)
        )
    moved.append(lax.all_to_all(first_sum, POOL, 0, 0, tiled=True))
    sides = list(sides)
    if n_tails == 2:
        sides[1] = swap(sides[1], "y")
    keep, send, *tails = simple_call(
        functools.partial(attend_backward_kernel, n_tails),
        [((2, rows, dim), F32), ((2, rows, dim), BF)] + tail_shape(640),
        2,
        14,
        60,
        scratch=[
            pltpu.VMEM((length, dim), BF),
            pltpu.VMEM((length, heads), BF),
            pltpu.VMEM((length, 512), BF),
            pltpu.VMEM((2, length, 128), F32),
            pltpu.VMEM((2, length, 128), F32),
            pltpu.VMEM((dim, 640), BF),
        ],
    )(dests, offs, *aog_parts, wqkv, wob, q, kd, vd, lse, start_col, ain, cosine, sine)
    keep, send, *tails = together((keep, send, *tails), *sides, *moving)

    got = swap(send, "c")
    if n_outer == 2:
        last_sum = total(last_grads[-1], [*parts_out[1][:-1], after_all(parts_out[1][-1], got)])
    cross = swap((keep[1] + got[1].astype(F32)).astype(BF), "x")
    if n_tails == 2:
        add = lambda a, b: (a.astype(F32) + b.astype(F32)).astype(BF)
        side_sums = add(*sides)
        tails[1] = swap(tails[1], "y")

        def reduce_z(sums):
            return [sums[0]] + [
                lax.ppermute(sums[s], ("o", "u"), [(i, i ^ s) for i in range(4)]) for s in (1, 2, 3)
            ]

        side_parts = reduce_z(side_sums)
        *tails, cross, got, moved[0] = together((*tails, cross, got, moved[0]), *side_parts)
        tail_parts = reduce_z(add(*tails))
        side, tail = (sum(p.astype(F32) for p in parts) for parts in (side_parts, tail_parts))
    else:
        side, tail = (
            lax.psum_scatter(part[0].astype(F32).reshape(dim, -1), DP, scatter_dimension=0, tiled=True)
            for part in (sides, tails)
        )
    moved.append(lax.all_to_all(after_all(last_sum, *tails), POOL, 0, 0, tiled=True))
    tokens_grad = simple_call(finish_kernel, [((rows, dim), F32)], 0, 6, 4)(
        tok, keep, got, cross, gains, after_grad
    )[0]

    narrow = jnp.concatenate([side[:, 256 : 256 + experts + 1], tail[:, 512:513]], axis=1)
    narrow = narrow + sum(
        lax.ppermute(narrow, ("x", "c"), [(i, i ^ s) for i in range(4)]) for s in range(1, 4)
    )
    gate_grad, up_grad, down_grad = (
        jnp.concatenate([part[:, m] for part in moved], axis=0).astype(F32) for m in range(3)
    )
    return (
        block_out[None],
        tokens_grad[None],
        narrow[:, experts + 1] / norm_attn.astype(F32),
        tail[:, :256],
        tail[:, 256:384],
        tail[:, 384:512],
        side[:, :256],
        narrow[:, experts],
        narrow[:, :experts],
        gate_grad,
        up_grad,
        down_grad,
    )


def solution(mesh):
    devices = mesh.devices
    fine = Mesh(devices.reshape(devices.shape[0] // 4, 2, 2, 2, 2), ("o", "u", "y", "x", "c"))
    dp, tensor = DP, ("x", "c")
    in_specs = (
        P(dp, tensor, None),
        P(dp, None),
        P(dp, None, None),
        P(dp, None),
        P(dp),
        P(dp, tensor),
        P(dp, tensor),
        P(dp, tensor),
        P(dp, tensor),
        P(dp),
        P(dp, None),
        P(None, dp, tensor),
        P(None, dp, tensor),
        P(None, dp, tensor),
        P(dp, tensor, None),
    )
    out_specs = (
        P(dp, tensor, None),
        P(dp, tensor, None),
        P(dp),
        P(dp, tensor),
        P(dp, tensor),
        P(dp, tensor),
        P(dp, tensor),
        P(dp),
        P(dp, None),
        P(None, dp, tensor),
        P(None, dp, tensor),
        P(None, dp, tensor),
    )
    return jax.shard_map(local, mesh=fine, in_specs=in_specs, out_specs=out_specs, check_vma=False)
```

```python
import functools
import math

import jax
import jax.numpy as jnp
from jax import lax
from jax.experimental import pallas as pl
from jax.experimental.pallas import tpu as pltpu
from jax.sharding import Mesh, PartitionSpec as P

HEAD_SIZE = 64
EPSILON = 1e-06
FLOOR_SCORE = -1e30
VMEM_LIMIT = 60 * 1024 * 1024
DP = ("o", "u", "y")
POOL = ("u", "y", "x", "c")
ORDERS = (("u", "y", "x"), ("y", "x", "u"), ("x", "u", "y"))
TOK = (512, 256, 256)
SECOND = (384, 256, 384)
NOTES = 128
PARTS_IN = ((3, 6, 3, 2, 2), (8, 3, 5))
PARTS_OUT = ((7, 3, 6), (2, 4, 2, 3, 5))
BLK = 256
BF = jnp.bfloat16
F32 = jnp.float32


def after_all(value, *others):
    return lax.optimization_barrier((value,) + others)[0]


def together(values, *others):
    return lax.optimization_barrier((*values, *others))[: len(values)]


def cuts(dim):
    found, a, b = [], 0, 0
    for i, (first, second) in enumerate(zip(TOK, SECOND)):
        found.append((a, a + first, b, b + second, first + (NOTES if i == 2 else 0)))
        a, b = a + first, b + second
    assert a == b == dim
    return found


def swap(value, axis):
    return lax.ppermute(value, axis, [(0, 1), (1, 0)])


def mm(left, right):
    return lax.dot_general(left, right, (((1,), (0,)), ((), ())), preferred_element_type=F32)


def mm_nt(left, right):
    return lax.dot_general(left, right, (((1,), (1,)), ((), ())), preferred_element_type=F32)


def mm_tn(left, right):
    return lax.dot_general(left, right, (((0,), (0,)), ((), ())), preferred_element_type=F32)


def lanes(shape):
    return lax.broadcasted_iota(jnp.int32, shape, 1)


def turn_halves(value):
    first = lanes(value.shape) % HEAD_SIZE < HEAD_SIZE // 2
    half = HEAD_SIZE // 2
    return jnp.where(first, pltpu.roll(value, 128 - half, 1), pltpu.roll(value, half, 1))


def both_halves(value, which):
    low = lanes(value.shape) < HEAD_SIZE
    turned = pltpu.roll(value, HEAD_SIZE, 1)
    return jnp.where(low, value, turned) if which == 0 else jnp.where(low, turned, value)


def stack_heads(pair):
    low = lanes(pair.shape) < HEAD_SIZE
    zero = jnp.zeros_like(pair)
    return jnp.concatenate([jnp.where(low, pair, zero), jnp.where(low, zero, pair)], axis=0)


def join_heads(stacked):
    rows = stacked.shape[0] // 2
    low = lanes((rows, stacked.shape[1])) < HEAD_SIZE
    return jnp.where(low, stacked[:rows], stacked[rows:])


def allowed_keys(start_col, block, width):
    rows = start_col.shape[0]
    cols = lax.broadcasted_iota(jnp.int32, (rows, width), 1)
    row_ids = block * rows + lax.broadcasted_iota(jnp.int32, (rows, width), 0)
    keep = (cols >= start_col) & (cols <= row_ids)
    return jnp.concatenate([keep, keep], axis=0)


def attend_forward_kernel(n_parts, shard, table, offs, t0, t1, t2, t3, *refs):
    parts, refs = refs[:n_parts], refs[n_parts:]
    gain_in, cosine, sine, start, ain_o, wqkv_o, gains_o, q_o, kd_o, vd_o, mix_o, lse_o = refs
    gains_o[...] = gain_in[...]
    base = 0
    for part in parts:
        for b in range(part.shape[0]):
            at = pl.multiple_of(table[base + b] * shard, shard)
            wqkv_o[pl.ds(at, shard), :] = part[b, :shard, :]
            if shard == 128:
                note = part[b, shard:, :128].astype(F32)
                for row in range(2):
                    gains_o[row : row + 1, pl.ds(at, 128)] = note[row : row + 1]
        base += part.shape[0]
    gain = gains_o[0:1, :]
    for r, piece in enumerate((t0, t1, t2, t3)):
        at = pl.multiple_of(offs[r], BLK)
        rows = pl.ds(at, BLK)
        value = piece[...].astype(F32)
        factor = lax.rsqrt(jnp.mean(value * value, axis=-1, keepdims=True) + EPSILON)
        normed = (value * factor * gain).astype(BF)
        ain_o[rows, :] = normed
        qkv = mm(normed, wqkv_o[...])
        cos_b, sin_b = cosine[rows, :], sine[rows, :]
        for part in range(3):
            raw = qkv[:, part * 128 : part * 128 + 128]
            turned = (raw * cos_b + turn_halves(raw) * sin_b).astype(BF)
            if part < 2:
                q_o[rows, part * 128 : part * 128 + 128] = turned * 0.125
            else:
                wide = turned.astype(F32)
                for kv in range(2):
                    kd_o[kv, rows, :] = both_halves(wide, kv).astype(BF)
        value_rows = qkv[:, 384:512].astype(BF).astype(F32)
        for kv in range(2):
            vd_o[kv, rows, :] = both_halves(value_rows, kv).astype(BF)
    total = ain_o.shape[0]
    for block in range(total // BLK):
        width = (block + 1) * BLK
        rows = pl.ds(block * BLK, BLK)
        keep = allowed_keys(start[rows, :], block, width)
        logs = jnp.zeros((BLK, 128), F32)
        for kv in range(2):
            query = stack_heads(q_o[rows, kv * 128 : kv * 128 + 128])
            scores = jnp.where(keep, mm_nt(query, kd_o[kv, :width, :]), FLOOR_SCORE)
            top = jnp.max(scores, axis=-1, keepdims=True)
            lifted = jnp.exp(scores - top)
            summed = jnp.sum(lifted, axis=-1, keepdims=True)
            shares = (lifted * (1.0 / summed)).astype(BF)
            mixed = join_heads(mm(shares, vd_o[kv, :width, :]))
            mix_o[rows, kv * 128 : kv * 128 + 128] = mixed.astype(BF)
            log_total = top + jnp.log(summed)
            lane = lanes(logs.shape)
            logs = jnp.where(lane == 2 * kv, log_total[:BLK], logs)
            logs = jnp.where(lane == 2 * kv + 1, log_total[BLK:], logs)
        lse_o[rows, :] = logs


def project_kernel(n_parts, shard, table, offs, mix, *refs):
    parts, (keep_o, send_o, wob) = refs[:n_parts], refs[n_parts:]
    base = 0
    for part in parts:
        for b in range(part.shape[0]):
            at = pl.multiple_of(table[base + b] * shard, shard)
            wob[pl.ds(at, shard), :] = part[b]
        base += part.shape[0]
    for r in range(4):
        rows = pl.ds(pl.multiple_of(offs[r], BLK), BLK)
        part = mm_nt(mix[rows, :], wob[:, :256])
        if r % 2 == 0:
            keep_o[r // 2] = part
        else:
            send_o[r // 2] = part.astype(BF)


def attend_backward_kernel(
    n_blocks, dests, offs, a0, a1, a2, a3, wqkv, wob, q, kd, vd, lse, start, ain, cosine, sine,
    keep_o, send_o, *refs,
):
    wg_o, (aog, mgrad, dqkv, dk, dv, flat) = refs[:n_blocks], refs[n_blocks:]
    total = ain.shape[0]
    for r, piece in enumerate((a0, a1, a2, a3)):
        aog[pl.ds(pl.multiple_of(offs[r], BLK), BLK), :] = piece[...]
    mgrad[...] = mm(aog[...], wob[:, :256]).astype(BF)
    dk[...] = jnp.zeros_like(dk)
    dv[...] = jnp.zeros_like(dv)
    for block in range(total // BLK):
        width = (block + 1) * BLK
        rows = pl.ds(block * BLK, BLK)
        keep = allowed_keys(start[rows, :], block, width)
        logs = lse[rows, :]
        lane = lanes(logs.shape)
        cos_b, sin_b = cosine[rows, :], sine[rows, :]
        for kv in range(2):
            cols = slice(kv * 128, kv * 128 + 128)
            query = stack_heads(q[rows, cols])
            out_grad = stack_heads(mgrad[rows, cols])
            log_total = jnp.concatenate(
                [
                    jnp.sum(jnp.where(lane == 2 * kv + h, logs, 0.0), axis=1, keepdims=True)
                    for h in range(2)
                ],
                axis=0,
            )
            keys = kd[kv, :width, :]
            scores = jnp.where(keep, mm_nt(query, keys), FLOOR_SCORE)
            shares = jnp.exp(scores - log_total)
            share_grad = mm_nt(out_grad, vd[kv, :width, :])
            inner = jnp.sum(shares * share_grad, axis=-1, keepdims=True)
            score_grad = (shares * (share_grad - inner)).astype(BF)
            query_grad = join_heads(mm(score_grad, keys)) * 0.125
            query_grad = query_grad * cos_b - turn_halves(query_grad) * sin_b
            dqkv[rows, cols] = query_grad.astype(BF)
            dk[kv, :width, :] += mm_tn(score_grad, query)
            dv[kv, :width, :] += mm_tn(shares.astype(BF), out_grad)
    joined = []
    for acc in (dk, dv):
        pair = [acc[kv] + pltpu.roll(acc[kv], HEAD_SIZE, 1) for kv in range(2)]
        joined.append(jnp.where(lanes(pair[0].shape) < HEAD_SIZE, pair[0], pair[1]))
    key_grad = joined[0] * cosine[...] - turn_halves(joined[0]) * sine[...]
    dqkv[:, 256:384] = key_grad.astype(BF)
    dqkv[:, 384:512] = joined[1].astype(BF)
    flat[:, :512] = mm_tn(ain[...], dqkv[...]).astype(BF)
    ones = jnp.ones((BLK, 128), BF)
    gain_sum = jnp.zeros((ain.shape[1], 128), F32)
    for r in range(4):
        rows = pl.ds(pl.multiple_of(offs[r], BLK), BLK)
        part = mm_nt(dqkv[rows, :], wqkv[...])
        gain_sum += mm_tn((part * ain[rows, :].astype(F32)).astype(BF), ones)
        if r % 2 == 0:
            keep_o[r // 2] = part
        else:
            send_o[r // 2] = part.astype(BF)
    flat[:, 512:] = gain_sum.astype(BF)
    spread(flat, dests, wg_o)


def spread(flat, dests, outs):
    done = 0
    for out in outs:
        shard = out.shape[1]
        for i in range(out.shape[0]):
            at = pl.multiple_of(dests[done + i] * shard, shard)
            out[i] = flat[pl.ds(at, shard), :]
        done += out.shape[0]


def out_grad_kernel(n_blocks, dests, offs, a0, a1, a2, a3, mix, small, *refs):
    outs, (aog, flat) = refs[:n_blocks], refs[n_blocks:]
    for r, piece in enumerate((a0, a1, a2, a3)):
        aog[pl.ds(pl.multiple_of(offs[r], BLK), BLK), :] = piece[...]
    flat[:, :256] = mm_tn(aog[...], mix[...]).astype(BF)
    flat[:, 256:] = small[...].astype(BF)
    spread(flat, dests, outs)


def route_kernel(
    tok, keep, got, cross, gains, wob, routes, cot, after_o, ma_o, mb_o, mc_o, gates_o
):
    after = tok[...].astype(F32) + (keep[0] + got[0].astype(F32) + cross[...].astype(F32))
    after_o[...] = after
    factor = lax.rsqrt(jnp.mean(after * after, axis=-1, keepdims=True) + EPSILON)
    moe_in = (after * factor * gains[1:2, :]).astype(BF)
    logits = mm(moe_in, wob[:, 256:])
    lane = lanes(logits.shape)
    routed = lane < 0
    for k in range(routes.shape[1]):
        routed = routed | (routes[:, k : k + 1] == lane)
    top = jnp.max(jnp.where(routed, logits, FLOOR_SCORE), axis=1, keepdims=True)
    lifted = jnp.where(routed, jnp.exp(jnp.where(routed, logits - top, 0.0)), 0.0)
    gates = lifted / jnp.sum(lifted, axis=1, keepdims=True)
    gates_o[...] = gates
    high = gates.astype(BF).astype(F32)
    middle = (gates - high).astype(BF).astype(F32)
    low = gates - high - middle
    extra = high + pltpu.roll(middle, 32, 1) + pltpu.roll(low, 64, 1)
    for out, (a, b, c, d, at) in zip((ma_o, mb_o, mc_o), cuts(cot.shape[1])):
        out[:, : b - a] = moe_in[:, a:b]
        out[:, at:] = cot[:, c:d]
    mc_o[:, TOK[2] : TOK[2] + NOTES] = extra.astype(BF)


def place_weights(meta, parts, mat, kinds):
    hidden = mat.shape[1] // len(kinds)
    done = 0
    for part in parts:
        shard = part.shape[2]
        for b in range(part.shape[0]):
            block = done + b
            at = meta[5 + block // 16] + block % 16 // 4 * shard if len(parts) > 1 else block // 4 * shard
            at = pl.multiple_of(at, shard)
            for i, m in enumerate(kinds):
                col = i * hidden + block % 4 * 128
                mat[pl.ds(at, shard), col : col + 128] = part[b, m]
        done += part.shape[0]


def one_hot(rank):
    row_ids = lax.broadcasted_iota(jnp.int32, (BLK, rank.shape[-1]), 0)
    return jnp.where(rank == row_ids, 1.0, 0.0).astype(BF)


def expert_kernel(n_mats, first, meta, *refs):
    refs = list(refs)
    take = lambda n: [refs.pop(0) for _ in range(n)]
    pieces = [take(4) for _ in range(3)]
    (rank,) = take(1)
    mats = take(n_mats)
    prev_rank, prev = (None, None) if first else (take(1)[0], take(3))
    outs = take(3 if first else 6)
    pick_o, dy_o, pre_o, weighted_o, mat = take(5)
    hidden = mat.shape[1] // 3
    own_expert = meta[0]

    @pl.when(pl.program_id(0) == 0)
    def _():
        place_weights(meta, mats, mat, (0, 1, 2))

    pick = one_hot(rank[0])
    half = pick.shape[1] // 2
    pick_k, pick_c = pick[:, :half], pick[:, half:]
    step = pl.program_id(0)

    def rows_of(i, side):
        low, high = (ref[...].reshape(-1, ref.shape[-1]) for ref in pieces[i][2 * side : 2 * side + 2])
        if i == 0:
            return jnp.concatenate([low, high], axis=0)
        return jnp.where((step // 2 if i == 1 else step % 2) == 0, low, high)

    spans = cuts(pick_o.shape[1])
    for i, (a, b, c, d, at) in enumerate(spans):
        got = mm(pick_k, rows_of(i, 0)) + mm(pick_c, rows_of(i, 1))
        pick_o[:, a:b] = got[:, : b - a].astype(BF)
        dy_o[:, c:d] = got[:, at:].astype(BF)
    extra = got[:, TOK[2] : TOK[2] + NOTES]
    lane = lanes(extra.shape)
    mine = (lane % 32 == own_expert) & (lane < 96)
    gate = jnp.sum(jnp.where(mine, extra, 0.0), axis=1, keepdims=True)
    picked, dy = pick_o[...], dy_o[...]
    gate_pre = mm(picked, mat[:, :hidden])
    up_pre = mm(picked, mat[:, hidden : 2 * hidden])
    back = mm(dy, mat[:, 2 * hidden :])
    sigma = 1.0 / (1.0 + jnp.exp(-gate_pre))
    active = gate_pre * sigma
    hid = active * up_pre
    gate_dot = jnp.sum(hid.astype(BF).astype(F32) * back, axis=1, keepdims=True)
    weighted_o[...] = (gate * hid).astype(BF)
    back = back * gate
    pre_o[:, :hidden] = (back * up_pre * sigma * (1.0 + gate_pre * (1.0 - sigma))).astype(BF)
    pre_o[:, hidden:] = (back * active).astype(BF)
    picked_grad = mm_nt(pre_o[...], mat[:, : 2 * hidden]).astype(BF)
    expert_out = mm_nt(weighted_o[...], mat[:, 2 * hidden :]).astype(BF)
    dot_high = gate_dot.astype(BF).astype(F32)
    dot_low = gate_dot - dot_high
    note = jnp.where(lane == own_expert, dot_high, 0.0)
    note = jnp.where(lane == own_expert + 32, dot_low, note).astype(BF)
    if not first:
        pick = jnp.concatenate([one_hot(prev_rank[0]), pick], axis=0)
    for i, (a, b, c, d, _) in enumerate(spans):
        part = [picked_grad[:, a:b]] + ([note] if i == 2 else []) + [expert_out[:, c:d]]
        part = jnp.concatenate(part, axis=1)
        if first:
            outs[i][...] = part
            continue
        part = jnp.concatenate([prev[i][...], part], axis=0)
        for side in range(2):
            summed = mm_tn(pick[:, side * half : side * half + half], part)
            out = outs[i + 3 * side]
            out[...] = summed.astype(BF).reshape(out.shape)


def weight_grad_kernel(blocks, meta, picked, dy, pre, weighted, *outs):
    shard = outs[0].shape[2]
    grads = (mm_tn(picked[...], pre[...]).astype(BF), mm_tn(dy[...], weighted[...]).astype(BF))
    hidden = weighted.shape[1]
    for step in range(4):

        @pl.when(pl.program_id(0) == step)
        def _(step=step):
            for b in range(blocks):
                block, n = step * blocks + b, 0
                while block >= outs[n].shape[0]:
                    block -= outs[n].shape[0]
                    n += 1
                rows = slice(b // 4 * shard, b // 4 * shard + shard)
                for m in range(3):
                    col = m % 2 * hidden + b % 4 * 128
                    outs[n][block, m] = grads[m // 2][rows, col : col + 128]


def back_kernel(
    after, ak, ar, bk, br, ck, cr, gains, wob, gates, cot, after_grad_o, aog_o, small_o, block_o
):
    both = lambda a, b: a[...].astype(F32) + b[...].astype(F32)
    sums = [both(ak, ar), both(bk, br), both(ck, cr)]
    spans = cuts(after.shape[1])
    upstream = jnp.concatenate([v[:, : b - a] for v, (a, b, *_) in zip(sums, spans)], axis=1)
    moe_out = jnp.concatenate([v[:, span[4] :] for v, span in zip(sums, spans)], axis=1)
    block_o[...] = (after[...] + moe_out).astype(BF)
    extra = sums[2][:, TOK[2] : TOK[2] + NOTES]
    lane = lanes(extra.shape)
    gate_dot = jnp.where(lane < 32, extra + pltpu.roll(extra, 96, 1), 0.0)
    share = gates[...]
    logit_grad = share * (gate_dot - jnp.sum(share * gate_dot, axis=1, keepdims=True))
    high = logit_grad.astype(BF)
    low = (logit_grad - high.astype(F32)).astype(BF)
    router = wob[:, 256:]
    gain = gains[1:2, :]
    upstream += mm_nt(high, router) + mm_nt(low, router)
    value = after[...]
    factor = lax.rsqrt(jnp.mean(value * value, axis=-1, keepdims=True) + EPSILON)
    normed = value * factor
    moe_in = (normed * gain).astype(BF)
    scaled = upstream * gain
    inward = factor * (scaled - normed * jnp.mean(scaled * normed, axis=-1, keepdims=True))
    after_grad = cot[...].astype(F32) + inward
    after_grad_o[...] = after_grad
    aog_o[...] = after_grad.astype(BF)
    column = jnp.where(lane == 32, 1.0, 0.0).astype(BF)
    small_o[...] = (
        mm_tn(moe_in, high) + mm_tn(moe_in, low) + mm_tn((upstream * normed).astype(BF), column)
    )


def finish_kernel(tok, keep, got, cross, gains, after_grad, out):
    upstream = keep[0] + got[0].astype(F32) + cross[...].astype(F32)
    value = tok[...].astype(F32)
    factor = lax.rsqrt(jnp.mean(value * value, axis=-1, keepdims=True) + EPSILON)
    normed = value * factor
    scaled = upstream * gains[0:1, :]
    inward = factor * (scaled - normed * jnp.mean(scaled * normed, axis=-1, keepdims=True))
    out[...] = after_grad[...] + inward


def spec_of(space):
    return pl.BlockSpec(memory_space=space)


def cost(micros):
    return pl.CostEstimate(flops=1, bytes_accessed=int(micros * 750000), transcendentals=0)


def simple_call(kernel, outs, n_scalar, n_in, micros, scratch=()):
    return pl.pallas_call(
        kernel,
        out_shape=[jax.ShapeDtypeStruct(s, d) for s, d in outs],
        in_specs=[spec_of(pltpu.SMEM)] * n_scalar + [spec_of(pltpu.VMEM)] * n_in,
        out_specs=[spec_of(pltpu.VMEM)] * len(outs),
        scratch_shapes=list(scratch),
        compiler_params=pltpu.CompilerParams(vmem_limit_bytes=VMEM_LIMIT),
        cost_estimate=cost(micros),
    )


def gather_pool(pieces, beside, ready):
    bufs = pieces
    came = (ready,)
    for step in range(3):
        moving = beside(step)(*came)
        came = [swap(buf, order[step]) for buf, order in zip(bufs, ORDERS)]
        came = together(came, *moving)
        if step < 2:
            bufs = [jnp.stack([buf, new]) for buf, new in zip(bufs, came)]
    moving = beside(3)(*came)
    near = [swap(after_all(value, *came), "c") for value in bufs]
    far = [swap(value, "c") for value in came]
    values = together((*near, *far), *moving)
    return list(zip(bufs, came, values[:3], values[3:]))


def scatter_pool(kept, other, fill):
    add = lambda a, b: (a.astype(F32) + b.astype(F32)).astype(BF)
    moving = fill(0, other)
    came = together([swap(send, "c") for send in other], *moving)
    before = list(zip(kept, came))
    for step in range(1, 4):
        sends = [add(a[1], b[1]) for a, b in before]
        moving = fill(step, came)
        came = [swap(send, order[3 - step]) for send, order in zip(sends, ORDERS)]
        flat = together([value for pair in before for value in pair], *sends)
        keeps = [add(flat[2 * i][0], flat[2 * i + 1][0]) for i in range(3)]
        values = together((*came, *keeps), *moving)
        before = list(zip(values[3:], values[:3]))
    return before


def gather_tensor(value):
    cross = swap(value, "x")
    return [value, swap(value, "c"), cross, swap(cross, "c")]


def sum_tensor(keep, send):
    got = swap(send, "c")
    cross = swap((keep[1] + got[1].astype(F32)).astype(BF), "x")
    return got, cross


def pool_specs(order, width):
    def spec(axes, half):
        shape = tuple(2 if axis == "x" else 1 for axis in reversed(axes)) + (BLK, width)

        def index(g, meta):
            place = {"x": 0, "u": g // 2, "y": g % 2}
            if half is not None and order[2] == "u":
                place["y"] = jnp.where(g // 2 == half, g % 2, 1 - half)
            return tuple(place[axis] for axis in reversed(axes)) + (0, 0)

        return pl.BlockSpec(shape, index)

    return [spec(order[:2], 0), spec(order[:2], 1)], spec(order, None)


def local(
    tokens, segments, routes, priority, norm_attn, w_query, w_key, w_value, w_out, norm_moe,
    w_router, w_gate, w_up, w_down, cotangent,
):
    _, rows, dim = tokens.shape
    n_outer = lax.axis_size("o")
    n_dp = 4 * n_outer
    shard = w_query.shape[0]
    length = 4 * rows
    top = routes.shape[2]
    experts = w_gate.shape[0]
    per_device = experts // 16
    capacity = length * top // experts
    hidden = 4 * w_gate.shape[2]
    widths = [at + d - c for _, _, c, d, at in cuts(dim)]
    at_x, at_c = lax.axis_index("x"), lax.axis_index("c")
    at_t = at_x * 2 + at_c
    at_pool = lax.axis_index(POOL)

    at_dp, at_z, at_y = lax.axis_index(DP), lax.axis_index(("o", "u")), lax.axis_index("y")
    steps = lambda n: jnp.arange(n, dtype=jnp.int32)

    tok = tokens[0]
    cot = cotangent[0]
    tok_near, tok_cross = swap(tok, "c"), swap(tok, "x")
    own_mats = []

    def weight_part(j):
        return jnp.stack([w[j * 16 : (j + 1) * 16] for w in (w_gate, w_up, w_down)], axis=1)

    parts_in = [[], []]

    def part_in(*markers):
        if n_outer != 2:
            return ()
        j = 1 if len(parts_in[0]) == len(PARTS_IN[0]) else 0
        count, i = PARTS_IN[j], len(parts_in[j])
        at = sum(count[:i])
        part = after_all(own_mats[j][at : at + count[i]], *markers)
        parts_in[j].append(swap(part, "o"))
        return (parts_in[j][-1],)

    first_mats = after_all(weight_part(0), tok_near)
    first_mats = lax.all_to_all(first_mats, POOL, 0, 0, tiled=True)

    seg = segments[0]
    start = jnp.zeros_like(seg)
    for s in range(1, 5):
        start = jnp.where(seg >= s, jnp.sum((seg < s).astype(jnp.int32)), start)
    place = (jnp.arange(length, dtype=jnp.int32) - start).astype(F32)
    lane = jnp.arange(128, dtype=jnp.int32)
    half = HEAD_SIZE // 2
    inverse = jnp.exp((lane % half).astype(F32) * (-2.0 * math.log(10000.0) / HEAD_SIZE))
    angle = place[:, None] * inverse[None, :]
    cosine = jnp.cos(angle)
    sine = jnp.sin(angle) * jnp.where(lane % HEAD_SIZE < half, -1.0, 1.0)
    start_col = start[:, None]

    notes = jnp.pad(jnp.stack([norm_attn, norm_moe]), ((0, 14), (0, 512 - shard)))
    pack = jnp.concatenate([w_query, w_key, w_value], axis=1)
    pack_b = jnp.concatenate([w_out, w_router, jnp.zeros((shard, 128 - experts), BF)], axis=1)
    if n_dp == 8:
        pack = jnp.concatenate(
            [jnp.concatenate([pack, pack_b], axis=1), jnp.pad(notes, ((0, 0), (0, 384)))], axis=0
        )
        rest = [lax.ppermute(pack, ("o", "u"), [(i, i ^ s) for i in range(4)]) for s in (1, 2, 3)]
        *rest, tok_near, tok_cross = together(
            (*rest, tok_near, tok_cross), cosine, sine, start_col
        )
        near = jnp.stack([pack, *rest])
        wa = [near[:, :, :512]]
        wa.append(swap(wa[0], "y"))
        wb = [near[:, :shard, 512:]]
        wb.append(swap(after_all(wb[0], wa[1]), "y"))
        table = jnp.bitwise_xor(at_z, steps(8) % 4) * 2 + jnp.bitwise_xor(at_y, steps(8) // 4)
        gains = jnp.zeros((8, dim), F32)
    else:
        wa = [lax.all_gather(pack, DP, axis=0)]
        wb = [lax.all_gather(pack_b, DP, axis=0)]
        table = steps(n_dp)
        gains = jnp.stack([lax.all_gather(g, DP, axis=0, tiled=True) for g in (norm_attn, norm_moe)])
        gains = jnp.pad(gains.astype(F32), ((0, 6), (0, 0)))

    table = table.astype(jnp.int32)
    own_mats.append(first_mats)
    moving = part_in(wa[0])
    next_part = weight_part(1)
    tok_parts = [tok, tok_near, tok_cross, swap(tok_cross, "c")]
    *tok_parts, next_part = together((*tok_parts, next_part), *wa, *moving)
    own_mats.append(lax.all_to_all(next_part, POOL, 0, 0, tiled=True))
    moving = part_in(tok_parts[0])
    plan = after_all(jnp.concatenate([routes[0].T, priority], axis=0), tok_parts[0])
    plan = jnp.stack([plan, swap(plan, "y")])
    offs = (jnp.bitwise_xor(at_t, steps(4)) * rows).astype(jnp.int32)
    heads = w_query.shape[1]
    ain, wqkv, gains, q, kd, vd, mix, lse = simple_call(
        functools.partial(attend_forward_kernel, len(wa), shard),
        [
            ((length, dim), BF),
            ((dim, 512), BF),
            ((8, dim), F32),
            ((length, heads), BF),
            ((2, length, 128), BF),
            ((2, length, 128), BF),
            ((length, heads), BF),
            ((length, 128), F32),
        ],
        2,
        8 + len(wa),
        11,
    )(table, offs, *tok_parts, *wa, gains, cosine, sine, start_col)
    keep, send, wob = simple_call(
        functools.partial(project_kernel, len(wb), shard),
        [((2, rows, dim), F32), ((2, rows, dim), BF), ((dim, 384), BF)],
        2,
        1 + len(wb),
        4,
    )(table, offs, mix, *wb)
    keep, send, wob = together((keep, send, wob), *moving)
    moving = part_in(mix)
    got, cross = sum_tensor(keep, send)
    got, cross, plan, own_mats[1] = together((got, cross, plan, own_mats[1]), *moving)
    route_col = lax.dynamic_slice_in_dim(routes[0], at_t * rows, rows, 0)
    after, ma, mb, mc, gates = simple_call(
        route_kernel,
        [
            ((rows, dim), F32),
            *[((rows, width), BF) for width in widths],
            ((rows, 128), F32),
        ],
        0,
        8,
        4,
    )(tok, keep, got, cross, gains, wob, route_col, cot)

    own = [j * 16 + at_pool for j in range(per_device)]
    plan = jnp.concatenate([plan, swap(plan, "u")], axis=0)
    hits = jnp.stack([jnp.any(plan[:, :top] == e, axis=1) for e in own], axis=1)
    first = plan[:, top]
    less = (first[:, :, None] < first[:, None, :]).astype(BF)
    rank = jnp.einsum("gjs,gst->gjt", hits.astype(BF), less, preferred_element_type=F32)
    rank = rank.astype(jnp.int32)
    rank = jnp.where(hits & (rank < capacity), rank, -1)
    rank = rank.reshape(4, per_device, 2, 2, rows)
    rank = jnp.where(at_x == 1, rank[:, :, ::-1], rank)
    rank = jnp.where(at_c == 1, rank[:, :, :, ::-1], rank)
    rank = rank.swapaxes(2, 3).reshape(4, per_device, length)

    def beside(step):
        return lambda *markers: part_in(*markers) + (
            (plan, plan, rank)[step : step + 1]
        )

    pool = [value for piece in gather_pool([ma, mb, mc], beside, cross) for value in piece]
    if n_outer == 2:
        ready_mats = lambda j: [own_mats[j]] + parts_in[j]
    else:
        all_mats = [lax.all_gather(m, "o", axis=0, tiled=True) for m in own_mats]
        ready_mats = lambda j: [all_mats[j]]
    at_o = lax.axis_index("o")
    bases = [at_o * 4 * shard, (1 - at_o) * 4 * shard] if n_outer == 2 else [0, 0]
    bases = jnp.stack([jnp.int32(base) for base in bases])

    params = dict(compiler_params=pltpu.CompilerParams(vmem_limit_bytes=VMEM_LIMIT))
    specs = [pool_specs(o, w) for o, w in zip(ORDERS, widths)]
    tok_specs = [spec for halves, _ in specs for spec in halves * 2]
    sum_specs = [whole for _, whole in specs]
    slot_spec = lambda width: pl.BlockSpec((BLK, width), lambda g, meta: (g, 0))
    rank_spec = pl.BlockSpec((1, 1, length), lambda g, meta: (g, 0, 0))
    mat_shape = (n_outer * 16, 3, shard, hidden // 4)
    mat_spec = lambda m: pl.BlockSpec(
        m.shape, lambda g, meta: (0, 0, 0, 0), pipeline_mode=pl.Buffered(1)
    )
    down_spec = lambda m: pl.BlockSpec(
        (m.shape[0], 1) + m.shape[2:], lambda g, meta: (0, 2, 0, 0), pipeline_mode=pl.Buffered(1)
    )
    pool_shapes = [jax.ShapeDtypeStruct((2, 2, 2, rows, w), BF) for w in widths]
    slots = 4 * capacity
    groups = steps(4)
    metas = [jnp.concatenate([e[None], groups, bases]).astype(jnp.int32) for e in own]
    chunk = dim // 4
    full = lambda width: pl.BlockSpec((slots, width), lambda i, meta: (0, 0))
    turned = lambda i, meta: jnp.where(meta[5] == 0, i ^ 2, i) if n_outer == 2 else i
    chunk_spec = pl.BlockSpec((slots, chunk), lambda i, meta: (0, turned(i, meta)))
    grad_shape = lambda n: jax.ShapeDtypeStruct((n,) + mat_shape[1:], BF)
    whole = lambda n: pl.BlockSpec((n,) + mat_shape[1:], lambda i, meta: (0, 0, 0, 0))

    def weight_grads_of(meta, saved, j):
        counts = [*PARTS_OUT[j], 16] if n_outer == 2 else [16 * n_outer]
        return pl.pallas_call(
            functools.partial(weight_grad_kernel, chunk // shard * 4),
            grid_spec=pltpu.PrefetchScalarGridSpec(
                num_scalar_prefetch=1,
                grid=(4,),
                in_specs=[chunk_spec, chunk_spec, full(2 * hidden), full(hidden)],
                out_specs=[whole(n) for n in counts],
            ),
            out_shape=[grad_shape(n) for n in counts],
            cost_estimate=cost(9),
            **params,
        )(meta, *saved)

    prev, weighted, saved = [], [], []
    parts_out, all_grads = [[], []], [[], []]

    def part_out(j, *markers):
        if n_outer != 2:
            return ()
        part = all_grads[j][len(parts_out[j])]
        parts_out[j].append(swap(after_all(part, *markers), "o"))
        return (parts_out[j][-1],)

    for j in range(per_device):
        if j == 0:
            moving = part_in(*pool)
        else:
            prev = together(prev, *moving)
            first_grads = weight_grads_of(after_all(metas[0], prev[0]), saved[0], 0)
            metas[j] = after_all(metas[j], first_grads[0])
            all_grads[0].extend(first_grads)
            moving = part_out(0, first_grads[0])
        result = pl.pallas_call(
            functools.partial(expert_kernel, len(ready_mats(j)), j == 0),
            grid_spec=pltpu.PrefetchScalarGridSpec(
                num_scalar_prefetch=1,
                grid=(4,),
                in_specs=tok_specs
                + [rank_spec]
                + [mat_spec(m) for m in ready_mats(j)]
                + ([rank_spec] + [slot_spec(w) for w in widths] if j else []),
                out_specs=(sum_specs * 2 if j else [slot_spec(w) for w in widths])
                + [slot_spec(dim), slot_spec(dim), slot_spec(2 * hidden), slot_spec(hidden)],
                scratch_shapes=[pltpu.VMEM((dim, 3 * hidden), BF)],
            ),
            out_shape=(
                pool_shapes * 2 if j else [jax.ShapeDtypeStruct((slots, w), BF) for w in widths]
            )
            + [jax.ShapeDtypeStruct((slots, w), BF) for w in (dim, dim, 2 * hidden, hidden)],
            cost_estimate=cost(29),
            **params,
        )(
            metas[j], *pool, rank[:, j : j + 1], *ready_mats(j),
            *([rank[:, :1], *prev] if j else []),
        )
        prev, kept = (result[:6], result[6:]) if j else (result[:3], result[3:])
        saved.append(kept)

    prev = together(prev, *moving)
    last_grads = all_grads[1]

    moved = []

    def total(mine, parts):
        return (mine.astype(F32) + jnp.concatenate(parts, axis=0).astype(F32)).astype(BF)

    def fill(step, bufs):
        if step == 0:
            last_grads.extend(weight_grads_of(after_all(metas[1], prev[0]), saved[1], 1))
            return (*part_out(0, *bufs), last_grads[0])
        return (part_out(0, *bufs) if step == 1 else ()) + part_out(1, *bufs)

    pairs = scatter_pool(prev[:3], prev[3:], fill)

    after_grad, aog, small, block_out = simple_call(
        back_kernel,
        [((rows, dim), F32), ((rows, dim), BF), ((dim, 128), F32), ((rows, dim), BF)],
        0,
        11,
        5,
    )(after, *pairs[0], *pairs[1], *pairs[2], gains, wob, gates, cot)
    near, cross = swap(aog, "c"), swap(aog, "x")
    moving = part_out(1, pairs[0][1])
    if n_outer == 2:
        first_sum = total(first_grads[-1], parts_out[0])
        near, cross, first_sum = together((near, cross, first_sum), *moving)
    aog_parts = [aog, near, cross, swap(cross, "c")]

    n_tails = 2 if n_dp == 8 else 1
    dests = jnp.bitwise_xor(at_z, steps(8) % 4) * 2 + jnp.bitwise_xor(at_y, steps(8) // 4)
    dests = (dests if n_dp == 8 else steps(n_dp)).astype(jnp.int32)
    tail_shape = lambda width: [((n_dp // n_tails, shard, width), BF)] * n_tails
    sides = simple_call(
        functools.partial(out_grad_kernel, n_tails),
        tail_shape(384),
        2,
        6,
        2,
        scratch=[pltpu.VMEM((length, dim), BF), pltpu.VMEM((dim, 384), BF)],
    )(dests, offs, *aog_parts, mix, small)

    aog_parts = together(aog_parts, *sides)
    moving = part_out(1, cross)
    if n_outer == 2:
        first_sum = after_all(first_sum, *aog_parts)
    else:
        first_sum, last_sum = (
            lax.psum_scatter(g[0], "o", scatter_dimension=0, tiled=True)
            for g in (first_grads, last_grads)
        )
    moved.append(lax.all_to_all(first_sum, POOL, 0, 0, tiled=True))
    sides = list(sides)
    if n_tails == 2:
        sides[1] = swap(sides[1], "y")
    keep, send, *tails = simple_call(
        functools.partial(attend_backward_kernel, n_tails),
        [((2, rows, dim), F32), ((2, rows, dim), BF)] + tail_shape(640),
        2,
        14,
        60,
        scratch=[
            pltpu.VMEM((length, dim), BF),
            pltpu.VMEM((length, heads), BF),
            pltpu.VMEM((length, 512), BF),
            pltpu.VMEM((2, length, 128), F32),
            pltpu.VMEM((2, length, 128), F32),
            pltpu.VMEM((dim, 640), BF),
        ],
    )(dests, offs, *aog_parts, wqkv, wob, q, kd, vd, lse, start_col, ain, cosine, sine)
    keep, send, *tails = together((keep, send, *tails), *sides, *moving)

    got = swap(send, "c")
    if n_outer == 2:
        last_sum = total(last_grads[-1], [*parts_out[1][:-1], after_all(parts_out[1][-1], got)])
    cross = swap((keep[1] + got[1].astype(F32)).astype(BF), "x")
    if n_tails == 2:
        add = lambda a, b: (a.astype(F32) + b.astype(F32)).astype(BF)
        side_sums = add(*sides)
        tails[1] = swap(tails[1], "y")

        def reduce_z(sums):
            return [sums[0]] + [
                lax.ppermute(sums[s], ("o", "u"), [(i, i ^ s) for i in range(4)]) for s in (1, 2, 3)
            ]

        side_parts = reduce_z(side_sums)
        *tails, cross, got, moved[0] = together((*tails, cross, got, moved[0]), *side_parts)
        tail_parts = reduce_z(add(*tails))
        side, tail = (sum(p.astype(F32) for p in parts) for parts in (side_parts, tail_parts))
    else:
        side, tail = (
            lax.psum_scatter(part[0].astype(F32).reshape(dim, -1), DP, scatter_dimension=0, tiled=True)
            for part in (sides, tails)
        )
    moved.append(lax.all_to_all(after_all(last_sum, *tails), POOL, 0, 0, tiled=True))
    tokens_grad = simple_call(finish_kernel, [((rows, dim), F32)], 0, 6, 4)(
        tok, keep, got, cross, gains, after_grad
    )[0]

    narrow = jnp.concatenate([side[:, 256 : 256 + experts + 1], tail[:, 512:513]], axis=1)
    narrow = narrow + sum(
        lax.ppermute(narrow, ("x", "c"), [(i, i ^ s) for i in range(4)]) for s in range(1, 4)
    )
    gate_grad, up_grad, down_grad = (
        jnp.concatenate([part[:, m] for part in moved], axis=0).astype(F32) for m in range(3)
    )
    return (
        block_out[None],
        tokens_grad[None],
        narrow[:, experts + 1] / norm_attn.astype(F32),
        tail[:, :256],
        tail[:, 256:384],
        tail[:, 384:512],
        side[:, :256],
        narrow[:, experts],
        narrow[:, :experts],
        gate_grad,
        up_grad,
        down_grad,
    )


def solution(mesh):
    devices = mesh.devices
    fine = Mesh(devices.reshape(devices.shape[0] // 4, 2, 2, 2, 2), ("o", "u", "y", "x", "c"))
    dp, tensor = DP, ("x", "c")
    in_specs = (
        P(dp, tensor, None),
        P(dp, None),
        P(dp, None, None),
        P(dp, None),
        P(dp),
        P(dp, tensor),
        P(dp, tensor),
        P(dp, tensor),
        P(dp, tensor),
        P(dp),
        P(dp, None),
        P(None, dp, tensor),
        P(None, dp, tensor),
        P(None, dp, tensor),
        P(dp, tensor, None),
    )
    out_specs = (
        P(dp, tensor, None),
        P(dp, tensor, None),
        P(dp),
        P(dp, tensor),
        P(dp, tensor),
        P(dp, tensor),
        P(dp, tensor),
        P(dp),
        P(dp, None),
        P(None, dp, tensor),
        P(None, dp, tensor),
        P(None, dp, tensor),
    )
    return jax.shard_map(local, mesh=fine, in_specs=in_specs, out_specs=out_specs, check_vma=False)
```

```python
import functools
import math

import jax
import jax.numpy as jnp
from jax import lax
from jax.experimental import pallas as pl
from jax.experimental.pallas import tpu as pltpu
from jax.sharding import Mesh, PartitionSpec as P

HEAD_SIZE = 64
EPSILON = 1e-06
FLOOR_SCORE = -1e30
VMEM_LIMIT = 60 * 1024 * 1024
DP = ("o", "u", "y")
POOL = ("u", "y", "x", "c")
ORDERS = (("u", "y", "x"), ("y", "x", "u"), ("x", "u", "y"))
TOK = (512, 256, 256)
SECOND = (384, 256, 384)
NOTES = 128
PARTS_IN = ((3, 5, 3, 2, 3), (8, 3, 5))
PARTS_OUT = ((7, 3, 6), (2, 4, 2, 3, 5))
BLK = 256
BF = jnp.bfloat16
F32 = jnp.float32


def after_all(value, *others):
    return lax.optimization_barrier((value,) + others)[0]


def together(values, *others):
    return lax.optimization_barrier((*values, *others))[: len(values)]


def cuts(dim):
    found, a, b = [], 0, 0
    for i, (first, second) in enumerate(zip(TOK, SECOND)):
        found.append((a, a + first, b, b + second, first + (NOTES if i == 2 else 0)))
        a, b = a + first, b + second
    assert a == b == dim
    return found


def swap(value, axis):
    return lax.ppermute(value, axis, [(0, 1), (1, 0)])


def mm(left, right):
    return lax.dot_general(left, right, (((1,), (0,)), ((), ())), preferred_element_type=F32)


def mm_nt(left, right):
    return lax.dot_general(left, right, (((1,), (1,)), ((), ())), preferred_element_type=F32)


def mm_tn(left, right):
    return lax.dot_general(left, right, (((0,), (0,)), ((), ())), preferred_element_type=F32)


def lanes(shape):
    return lax.broadcasted_iota(jnp.int32, shape, 1)


def turn_halves(value):
    first = lanes(value.shape) % HEAD_SIZE < HEAD_SIZE // 2
    half = HEAD_SIZE // 2
    return jnp.where(first, pltpu.roll(value, 128 - half, 1), pltpu.roll(value, half, 1))


def both_halves(value, which):
    low = lanes(value.shape) < HEAD_SIZE
    turned = pltpu.roll(value, HEAD_SIZE, 1)
    return jnp.where(low, value, turned) if which == 0 else jnp.where(low, turned, value)


def stack_heads(pair):
    low = lanes(pair.shape) < HEAD_SIZE
    zero = jnp.zeros_like(pair)
    return jnp.concatenate([jnp.where(low, pair, zero), jnp.where(low, zero, pair)], axis=0)


def join_heads(stacked):
    rows = stacked.shape[0] // 2
    low = lanes((rows, stacked.shape[1])) < HEAD_SIZE
    return jnp.where(low, stacked[:rows], stacked[rows:])


def allowed_keys(start_col, block, width):
    rows = start_col.shape[0]
    cols = lax.broadcasted_iota(jnp.int32, (rows, width), 1)
    row_ids = block * rows + lax.broadcasted_iota(jnp.int32, (rows, width), 0)
    keep = (cols >= start_col) & (cols <= row_ids)
    return jnp.concatenate([keep, keep], axis=0)


def attend_forward_kernel(n_parts, shard, table, offs, t0, t1, t2, t3, *refs):
    parts, refs = refs[:n_parts], refs[n_parts:]
    gain_in, cosine, sine, start, ain_o, wqkv_o, gains_o, q_o, kd_o, vd_o, mix_o, lse_o = refs
    gains_o[...] = gain_in[...]
    base = 0
    for part in parts:
        for b in range(part.shape[0]):
            at = pl.multiple_of(table[base + b] * shard, shard)
            wqkv_o[pl.ds(at, shard), :] = part[b, :shard, :]
            if shard == 128:
                note = part[b, shard:, :128].astype(F32)
                for row in range(2):
                    gains_o[row : row + 1, pl.ds(at, 128)] = note[row : row + 1]
        base += part.shape[0]
    gain = gains_o[0:1, :]
    for r, piece in enumerate((t0, t1, t2, t3)):
        at = pl.multiple_of(offs[r], BLK)
        rows = pl.ds(at, BLK)
        value = piece[...].astype(F32)
        factor = lax.rsqrt(jnp.mean(value * value, axis=-1, keepdims=True) + EPSILON)
        normed = (value * factor * gain).astype(BF)
        ain_o[rows, :] = normed
        qkv = mm(normed, wqkv_o[...])
        cos_b, sin_b = cosine[rows, :], sine[rows, :]
        for part in range(3):
            raw = qkv[:, part * 128 : part * 128 + 128]
            turned = (raw * cos_b + turn_halves(raw) * sin_b).astype(BF)
            if part < 2:
                q_o[rows, part * 128 : part * 128 + 128] = turned * 0.125
            else:
                wide = turned.astype(F32)
                for kv in range(2):
                    kd_o[kv, rows, :] = both_halves(wide, kv).astype(BF)
        value_rows = qkv[:, 384:512].astype(BF).astype(F32)
        for kv in range(2):
            vd_o[kv, rows, :] = both_halves(value_rows, kv).astype(BF)
    total = ain_o.shape[0]
    for block in range(total // BLK):
        width = (block + 1) * BLK
        rows = pl.ds(block * BLK, BLK)
        keep = allowed_keys(start[rows, :], block, width)
        logs = jnp.zeros((BLK, 128), F32)
        for kv in range(2):
            query = stack_heads(q_o[rows, kv * 128 : kv * 128 + 128])
            scores = jnp.where(keep, mm_nt(query, kd_o[kv, :width, :]), FLOOR_SCORE)
            top = jnp.max(scores, axis=-1, keepdims=True)
            lifted = jnp.exp(scores - top)
            summed = jnp.sum(lifted, axis=-1, keepdims=True)
            shares = (lifted * (1.0 / summed)).astype(BF)
            mixed = join_heads(mm(shares, vd_o[kv, :width, :]))
            mix_o[rows, kv * 128 : kv * 128 + 128] = mixed.astype(BF)
            log_total = top + jnp.log(summed)
            lane = lanes(logs.shape)
            logs = jnp.where(lane == 2 * kv, log_total[:BLK], logs)
            logs = jnp.where(lane == 2 * kv + 1, log_total[BLK:], logs)
        lse_o[rows, :] = logs


def project_kernel(n_parts, shard, table, offs, mix, *refs):
    parts, (keep_o, send_o, wob) = refs[:n_parts], refs[n_parts:]
    base = 0
    for part in parts:
        for b in range(part.shape[0]):
            at = pl.multiple_of(table[base + b] * shard, shard)
            wob[pl.ds(at, shard), :] = part[b]
        base += part.shape[0]
    for r in range(4):
        rows = pl.ds(pl.multiple_of(offs[r], BLK), BLK)
        part = mm_nt(mix[rows, :], wob[:, :256])
        if r % 2 == 0:
            keep_o[r // 2] = part
        else:
            send_o[r // 2] = part.astype(BF)


def attend_backward_kernel(
    n_blocks, dests, offs, a0, a1, a2, a3, wqkv, wob, q, kd, vd, lse, start, ain, cosine, sine,
    keep_o, send_o, *refs,
):
    wg_o, (aog, mgrad, dqkv, dk, dv, flat) = refs[:n_blocks], refs[n_blocks:]
    total = ain.shape[0]
    for r, piece in enumerate((a0, a1, a2, a3)):
        aog[pl.ds(pl.multiple_of(offs[r], BLK), BLK), :] = piece[...]
    mgrad[...] = mm(aog[...], wob[:, :256]).astype(BF)
    dk[...] = jnp.zeros_like(dk)
    dv[...] = jnp.zeros_like(dv)
    for block in range(total // BLK):
        width = (block + 1) * BLK
        rows = pl.ds(block * BLK, BLK)
        keep = allowed_keys(start[rows, :], block, width)
        logs = lse[rows, :]
        lane = lanes(logs.shape)
        cos_b, sin_b = cosine[rows, :], sine[rows, :]
        for kv in range(2):
            cols = slice(kv * 128, kv * 128 + 128)
            query = stack_heads(q[rows, cols])
            out_grad = stack_heads(mgrad[rows, cols])
            log_total = jnp.concatenate(
                [
                    jnp.sum(jnp.where(lane == 2 * kv + h, logs, 0.0), axis=1, keepdims=True)
                    for h in range(2)
                ],
                axis=0,
            )
            keys = kd[kv, :width, :]
            scores = jnp.where(keep, mm_nt(query, keys), FLOOR_SCORE)
            shares = jnp.exp(scores - log_total)
            share_grad = mm_nt(out_grad, vd[kv, :width, :])
            inner = jnp.sum(shares * share_grad, axis=-1, keepdims=True)
            score_grad = (shares * (share_grad - inner)).astype(BF)
            query_grad = join_heads(mm(score_grad, keys)) * 0.125
            query_grad = query_grad * cos_b - turn_halves(query_grad) * sin_b
            dqkv[rows, cols] = query_grad.astype(BF)
            dk[kv, :width, :] += mm_tn(score_grad, query)
            dv[kv, :width, :] += mm_tn(shares.astype(BF), out_grad)
    joined = []
    for acc in (dk, dv):
        pair = [acc[kv] + pltpu.roll(acc[kv], HEAD_SIZE, 1) for kv in range(2)]
        joined.append(jnp.where(lanes(pair[0].shape) < HEAD_SIZE, pair[0], pair[1]))
    key_grad = joined[0] * cosine[...] - turn_halves(joined[0]) * sine[...]
    dqkv[:, 256:384] = key_grad.astype(BF)
    dqkv[:, 384:512] = joined[1].astype(BF)
    flat[:, :512] = mm_tn(ain[...], dqkv[...]).astype(BF)
    ones = jnp.ones((BLK, 128), BF)
    gain_sum = jnp.zeros((ain.shape[1], 128), F32)
    for r in range(4):
        rows = pl.ds(pl.multiple_of(offs[r], BLK), BLK)
        part = mm_nt(dqkv[rows, :], wqkv[...])
        gain_sum += mm_tn((part * ain[rows, :].astype(F32)).astype(BF), ones)
        if r % 2 == 0:
            keep_o[r // 2] = part
        else:
            send_o[r // 2] = part.astype(BF)
    flat[:, 512:] = gain_sum.astype(BF)
    spread(flat, dests, wg_o)


def spread(flat, dests, outs):
    done = 0
    for out in outs:
        shard = out.shape[1]
        for i in range(out.shape[0]):
            at = pl.multiple_of(dests[done + i] * shard, shard)
            out[i] = flat[pl.ds(at, shard), :]
        done += out.shape[0]


def out_grad_kernel(n_blocks, dests, offs, a0, a1, a2, a3, mix, small, *refs):
    outs, (aog, flat) = refs[:n_blocks], refs[n_blocks:]
    for r, piece in enumerate((a0, a1, a2, a3)):
        aog[pl.ds(pl.multiple_of(offs[r], BLK), BLK), :] = piece[...]
    flat[:, :256] = mm_tn(aog[...], mix[...]).astype(BF)
    flat[:, 256:] = small[...].astype(BF)
    spread(flat, dests, outs)


def route_kernel(
    tok, keep, got, cross, gains, wob, routes, cot, after_o, ma_o, mb_o, mc_o, gates_o
):
    after = tok[...].astype(F32) + (keep[0] + got[0].astype(F32) + cross[...].astype(F32))
    after_o[...] = after
    factor = lax.rsqrt(jnp.mean(after * after, axis=-1, keepdims=True) + EPSILON)
    moe_in = (after * factor * gains[1:2, :]).astype(BF)
    logits = mm(moe_in, wob[:, 256:])
    lane = lanes(logits.shape)
    routed = lane < 0
    for k in range(routes.shape[1]):
        routed = routed | (routes[:, k : k + 1] == lane)
    top = jnp.max(jnp.where(routed, logits, FLOOR_SCORE), axis=1, keepdims=True)
    lifted = jnp.where(routed, jnp.exp(jnp.where(routed, logits - top, 0.0)), 0.0)
    gates = lifted / jnp.sum(lifted, axis=1, keepdims=True)
    gates_o[...] = gates
    high = gates.astype(BF).astype(F32)
    middle = (gates - high).astype(BF).astype(F32)
    low = gates - high - middle
    extra = high + pltpu.roll(middle, 32, 1) + pltpu.roll(low, 64, 1)
    for out, (a, b, c, d, at) in zip((ma_o, mb_o, mc_o), cuts(cot.shape[1])):
        out[:, : b - a] = moe_in[:, a:b]
        out[:, at:] = cot[:, c:d]
    mc_o[:, TOK[2] : TOK[2] + NOTES] = extra.astype(BF)


def place_weights(meta, parts, mat, kinds):
    hidden = mat.shape[1] // len(kinds)
    done = 0
    for part in parts:
        shard = part.shape[2]
        for b in range(part.shape[0]):
            block = done + b
            at = meta[5 + block // 16] + block % 16 // 4 * shard if len(parts) > 1 else block // 4 * shard
            at = pl.multiple_of(at, shard)
            for i, m in enumerate(kinds):
                col = i * hidden + block % 4 * 128
                mat[pl.ds(at, shard), col : col + 128] = part[b, m]
        done += part.shape[0]


def one_hot(rank):
    row_ids = lax.broadcasted_iota(jnp.int32, (BLK, rank.shape[-1]), 0)
    return jnp.where(rank == row_ids, 1.0, 0.0).astype(BF)


def expert_kernel(n_mats, first, meta, *refs):
    refs = list(refs)
    take = lambda n: [refs.pop(0) for _ in range(n)]
    pieces = [take(4) for _ in range(3)]
    (rank,) = take(1)
    mats = take(n_mats)
    prev_rank, prev = (None, None) if first else (take(1)[0], take(3))
    outs = take(3 if first else 6)
    pick_o, dy_o, pre_o, weighted_o, mat = take(5)
    hidden = mat.shape[1] // 3
    own_expert = meta[0]

    @pl.when(pl.program_id(0) == 0)
    def _():
        place_weights(meta, mats, mat, (0, 1, 2))

    pick = one_hot(rank[0])
    half = pick.shape[1] // 2
    pick_k, pick_c = pick[:, :half], pick[:, half:]
    step = pl.program_id(0)

    def rows_of(i, side):
        low, high = (ref[...].reshape(-1, ref.shape[-1]) for ref in pieces[i][2 * side : 2 * side + 2])
        if i == 0:
            return jnp.concatenate([low, high], axis=0)
        return jnp.where((step // 2 if i == 1 else step % 2) == 0, low, high)

    spans = cuts(pick_o.shape[1])
    for i, (a, b, c, d, at) in enumerate(spans):
        got = mm(pick_k, rows_of(i, 0)) + mm(pick_c, rows_of(i, 1))
        pick_o[:, a:b] = got[:, : b - a].astype(BF)
        dy_o[:, c:d] = got[:, at:].astype(BF)
    extra = got[:, TOK[2] : TOK[2] + NOTES]
    lane = lanes(extra.shape)
    mine = (lane % 32 == own_expert) & (lane < 96)
    gate = jnp.sum(jnp.where(mine, extra, 0.0), axis=1, keepdims=True)
    picked, dy = pick_o[...], dy_o[...]
    gate_pre = mm(picked, mat[:, :hidden])
    up_pre = mm(picked, mat[:, hidden : 2 * hidden])
    back = mm(dy, mat[:, 2 * hidden :])
    sigma = 1.0 / (1.0 + jnp.exp(-gate_pre))
    active = gate_pre * sigma
    hid = active * up_pre
    gate_dot = jnp.sum(hid.astype(BF).astype(F32) * back, axis=1, keepdims=True)
    weighted_o[...] = (gate * hid).astype(BF)
    back = back * gate
    pre_o[:, :hidden] = (back * up_pre * sigma * (1.0 + gate_pre * (1.0 - sigma))).astype(BF)
    pre_o[:, hidden:] = (back * active).astype(BF)
    picked_grad = mm_nt(pre_o[...], mat[:, : 2 * hidden]).astype(BF)
    expert_out = mm_nt(weighted_o[...], mat[:, 2 * hidden :]).astype(BF)
    dot_high = gate_dot.astype(BF).astype(F32)
    dot_low = gate_dot - dot_high
    note = jnp.where(lane == own_expert, dot_high, 0.0)
    note = jnp.where(lane == own_expert + 32, dot_low, note).astype(BF)
    if not first:
        pick = jnp.concatenate([one_hot(prev_rank[0]), pick], axis=0)
    for i, (a, b, c, d, _) in enumerate(spans):
        part = [picked_grad[:, a:b]] + ([note] if i == 2 else []) + [expert_out[:, c:d]]
        part = jnp.concatenate(part, axis=1)
        if first:
            outs[i][...] = part
            continue
        part = jnp.concatenate([prev[i][...], part], axis=0)
        for side in range(2):
            summed = mm_tn(pick[:, side * half : side * half + half], part)
            out = outs[i + 3 * side]
            out[...] = summed.astype(BF).reshape(out.shape)


def weight_grad_kernel(blocks, meta, picked, dy, pre, weighted, *outs):
    shard = outs[0].shape[2]
    grads = (mm_tn(picked[...], pre[...]).astype(BF), mm_tn(dy[...], weighted[...]).astype(BF))
    hidden = weighted.shape[1]
    for step in range(4):

        @pl.when(pl.program_id(0) == step)
        def _(step=step):
            for b in range(blocks):
                block, n = step * blocks + b, 0
                while block >= outs[n].shape[0]:
                    block -= outs[n].shape[0]
                    n += 1
                rows = slice(b // 4 * shard, b // 4 * shard + shard)
                for m in range(3):
                    col = m % 2 * hidden + b % 4 * 128
                    outs[n][block, m] = grads[m // 2][rows, col : col + 128]


def back_kernel(
    after, ak, ar, bk, br, ck, cr, gains, wob, gates, cot, after_grad_o, aog_o, small_o, block_o
):
    both = lambda a, b: a[...].astype(F32) + b[...].astype(F32)
    sums = [both(ak, ar), both(bk, br), both(ck, cr)]
    spans = cuts(after.shape[1])
    upstream = jnp.concatenate([v[:, : b - a] for v, (a, b, *_) in zip(sums, spans)], axis=1)
    moe_out = jnp.concatenate([v[:, span[4] :] for v, span in zip(sums, spans)], axis=1)
    block_o[...] = (after[...] + moe_out).astype(BF)
    extra = sums[2][:, TOK[2] : TOK[2] + NOTES]
    lane = lanes(extra.shape)
    gate_dot = jnp.where(lane < 32, extra + pltpu.roll(extra, 96, 1), 0.0)
    share = gates[...]
    logit_grad = share * (gate_dot - jnp.sum(share * gate_dot, axis=1, keepdims=True))
    high = logit_grad.astype(BF)
    low = (logit_grad - high.astype(F32)).astype(BF)
    router = wob[:, 256:]
    gain = gains[1:2, :]
    upstream += mm_nt(high, router) + mm_nt(low, router)
    value = after[...]
    factor = lax.rsqrt(jnp.mean(value * value, axis=-1, keepdims=True) + EPSILON)
    normed = value * factor
    moe_in = (normed * gain).astype(BF)
    scaled = upstream * gain
    inward = factor * (scaled - normed * jnp.mean(scaled * normed, axis=-1, keepdims=True))
    after_grad = cot[...].astype(F32) + inward
    after_grad_o[...] = after_grad
    aog_o[...] = after_grad.astype(BF)
    column = jnp.where(lane == 32, 1.0, 0.0).astype(BF)
    small_o[...] = (
        mm_tn(moe_in, high) + mm_tn(moe_in, low) + mm_tn((upstream * normed).astype(BF), column)
    )


def finish_kernel(tok, keep, got, cross, gains, after_grad, out):
    upstream = keep[0] + got[0].astype(F32) + cross[...].astype(F32)
    value = tok[...].astype(F32)
    factor = lax.rsqrt(jnp.mean(value * value, axis=-1, keepdims=True) + EPSILON)
    normed = value * factor
    scaled = upstream * gains[0:1, :]
    inward = factor * (scaled - normed * jnp.mean(scaled * normed, axis=-1, keepdims=True))
    out[...] = after_grad[...] + inward


def spec_of(space):
    return pl.BlockSpec(memory_space=space)


def cost(micros):
    return pl.CostEstimate(flops=1, bytes_accessed=int(micros * 750000), transcendentals=0)


def simple_call(kernel, outs, n_scalar, n_in, micros, scratch=()):
    return pl.pallas_call(
        kernel,
        out_shape=[jax.ShapeDtypeStruct(s, d) for s, d in outs],
        in_specs=[spec_of(pltpu.SMEM)] * n_scalar + [spec_of(pltpu.VMEM)] * n_in,
        out_specs=[spec_of(pltpu.VMEM)] * len(outs),
        scratch_shapes=list(scratch),
        compiler_params=pltpu.CompilerParams(vmem_limit_bytes=VMEM_LIMIT),
        cost_estimate=cost(micros),
    )


def gather_pool(pieces, beside, ready):
    bufs = pieces
    came = (ready,)
    for step in range(3):
        moving = beside(step)(*came)
        came = [swap(buf, order[step]) for buf, order in zip(bufs, ORDERS)]
        came = together(came, *moving)
        if step < 2:
            bufs = [jnp.stack([buf, new]) for buf, new in zip(bufs, came)]
    moving = beside(3)(*came)
    near = [swap(after_all(value, *came), "c") for value in bufs]
    far = [swap(value, "c") for value in came]
    values = together((*near, *far), *moving)
    return list(zip(bufs, came, values[:3], values[3:]))


def scatter_pool(kept, other, fill):
    add = lambda a, b: (a.astype(F32) + b.astype(F32)).astype(BF)
    moving = fill(0, other)
    came = together([swap(send, "c") for send in other], *moving)
    before = list(zip(kept, came))
    for step in range(1, 4):
        sends = [add(a[1], b[1]) for a, b in before]
        moving = fill(step, came)
        came = [swap(send, order[3 - step]) for send, order in zip(sends, ORDERS)]
        flat = together([value for pair in before for value in pair], *sends)
        keeps = [add(flat[2 * i][0], flat[2 * i + 1][0]) for i in range(3)]
        values = together((*came, *keeps), *moving)
        before = list(zip(values[3:], values[:3]))
    return before


def gather_tensor(value):
    cross = swap(value, "x")
    return [value, swap(value, "c"), cross, swap(cross, "c")]


def sum_tensor(keep, send):
    got = swap(send, "c")
    cross = swap((keep[1] + got[1].astype(F32)).astype(BF), "x")
    return got, cross


def pool_specs(order, width):
    def spec(axes, half):
        shape = tuple(2 if axis == "x" else 1 for axis in reversed(axes)) + (BLK, width)

        def index(g, meta):
            place = {"x": 0, "u": g // 2, "y": g % 2}
            if half is not None and order[2] == "u":
                place["y"] = jnp.where(g // 2 == half, g % 2, 1 - half)
            return tuple(place[axis] for axis in reversed(axes)) + (0, 0)

        return pl.BlockSpec(shape, index)

    return [spec(order[:2], 0), spec(order[:2], 1)], spec(order, None)


def local(
    tokens, segments, routes, priority, norm_attn, w_query, w_key, w_value, w_out, norm_moe,
    w_router, w_gate, w_up, w_down, cotangent,
):
    _, rows, dim = tokens.shape
    n_outer = lax.axis_size("o")
    n_dp = 4 * n_outer
    shard = w_query.shape[0]
    length = 4 * rows
    top = routes.shape[2]
    experts = w_gate.shape[0]
    per_device = experts // 16
    capacity = length * top // experts
    hidden = 4 * w_gate.shape[2]
    widths = [at + d - c for _, _, c, d, at in cuts(dim)]
    at_x, at_c = lax.axis_index("x"), lax.axis_index("c")
    at_t = at_x * 2 + at_c
    at_pool = lax.axis_index(POOL)

    at_dp, at_z, at_y = lax.axis_index(DP), lax.axis_index(("o", "u")), lax.axis_index("y")
    steps = lambda n: jnp.arange(n, dtype=jnp.int32)

    tok = tokens[0]
    cot = cotangent[0]
    tok_near, tok_cross = swap(tok, "c"), swap(tok, "x")
    own_mats = []

    def weight_part(j):
        return jnp.stack([w[j * 16 : (j + 1) * 16] for w in (w_gate, w_up, w_down)], axis=1)

    parts_in = [[], []]

    def part_in(*markers):
        if n_outer != 2:
            return ()
        j = 1 if len(parts_in[0]) == len(PARTS_IN[0]) else 0
        count, i = PARTS_IN[j], len(parts_in[j])
        at = sum(count[:i])
        part = after_all(own_mats[j][at : at + count[i]], *markers)
        parts_in[j].append(swap(part, "o"))
        return (parts_in[j][-1],)

    first_mats = after_all(weight_part(0), tok_near)
    first_mats = lax.all_to_all(first_mats, POOL, 0, 0, tiled=True)

    seg = segments[0]
    start = jnp.zeros_like(seg)
    for s in range(1, 5):
        start = jnp.where(seg >= s, jnp.sum((seg < s).astype(jnp.int32)), start)
    place = (jnp.arange(length, dtype=jnp.int32) - start).astype(F32)
    lane = jnp.arange(128, dtype=jnp.int32)
    half = HEAD_SIZE // 2
    inverse = jnp.exp((lane % half).astype(F32) * (-2.0 * math.log(10000.0) / HEAD_SIZE))
    angle = place[:, None] * inverse[None, :]
    cosine = jnp.cos(angle)
    sine = jnp.sin(angle) * jnp.where(lane % HEAD_SIZE < half, -1.0, 1.0)
    start_col = start[:, None]

    notes = jnp.pad(jnp.stack([norm_attn, norm_moe]), ((0, 14), (0, 512 - shard)))
    pack = jnp.concatenate([w_query, w_key, w_value], axis=1)
    pack_b = jnp.concatenate([w_out, w_router, jnp.zeros((shard, 128 - experts), BF)], axis=1)
    if n_dp == 8:
        pack = jnp.concatenate(
            [jnp.concatenate([pack, pack_b], axis=1), jnp.pad(notes, ((0, 0), (0, 384)))], axis=0
        )
        rest = [lax.ppermute(pack, ("o", "u"), [(i, i ^ s) for i in range(4)]) for s in (1, 2, 3)]
        *rest, tok_near, tok_cross = together(
            (*rest, tok_near, tok_cross), cosine, sine, start_col
        )
        near = jnp.stack([pack, *rest])
        wa = [near[:, :, :512]]
        wa.append(swap(wa[0], "y"))
        wb = [near[:, :shard, 512:]]
        wb.append(swap(after_all(wb[0], wa[1]), "y"))
        table = jnp.bitwise_xor(at_z, steps(8) % 4) * 2 + jnp.bitwise_xor(at_y, steps(8) // 4)
        gains = jnp.zeros((8, dim), F32)
    else:
        wa = [lax.all_gather(pack, DP, axis=0)]
        wb = [lax.all_gather(pack_b, DP, axis=0)]
        table = steps(n_dp)
        gains = jnp.stack([lax.all_gather(g, DP, axis=0, tiled=True) for g in (norm_attn, norm_moe)])
        gains = jnp.pad(gains.astype(F32), ((0, 6), (0, 0)))

    table = table.astype(jnp.int32)
    own_mats.append(first_mats)
    moving = part_in(wa[0])
    next_part = weight_part(1)
    tok_parts = [tok, tok_near, tok_cross, swap(tok_cross, "c")]
    *tok_parts, next_part = together((*tok_parts, next_part), *wa, *moving)
    own_mats.append(lax.all_to_all(next_part, POOL, 0, 0, tiled=True))
    moving = part_in(tok_parts[0])
    plan = after_all(jnp.concatenate([routes[0].T, priority], axis=0), tok_parts[0])
    plan = jnp.stack([plan, swap(plan, "y")])
    offs = (jnp.bitwise_xor(at_t, steps(4)) * rows).astype(jnp.int32)
    heads = w_query.shape[1]
    ain, wqkv, gains, q, kd, vd, mix, lse = simple_call(
        functools.partial(attend_forward_kernel, len(wa), shard),
        [
            ((length, dim), BF),
            ((dim, 512), BF),
            ((8, dim), F32),
            ((length, heads), BF),
            ((2, length, 128), BF),
            ((2, length, 128), BF),
            ((length, heads), BF),
            ((length, 128), F32),
        ],
        2,
        8 + len(wa),
        11,
    )(table, offs, *tok_parts, *wa, gains, cosine, sine, start_col)
    keep, send, wob = simple_call(
        functools.partial(project_kernel, len(wb), shard),
        [((2, rows, dim), F32), ((2, rows, dim), BF), ((dim, 384), BF)],
        2,
        1 + len(wb),
        4,
    )(table, offs, mix, *wb)
    keep, send, wob = together((keep, send, wob), *moving)
    moving = part_in(mix)
    got, cross = sum_tensor(keep, send)
    got, cross, plan, own_mats[1] = together((got, cross, plan, own_mats[1]), *moving)
    route_col = lax.dynamic_slice_in_dim(routes[0], at_t * rows, rows, 0)
    after, ma, mb, mc, gates = simple_call(
        route_kernel,
        [
            ((rows, dim), F32),
            *[((rows, width), BF) for width in widths],
            ((rows, 128), F32),
        ],
        0,
        8,
        4,
    )(tok, keep, got, cross, gains, wob, route_col, cot)

    own = [j * 16 + at_pool for j in range(per_device)]
    plan = jnp.concatenate([plan, swap(plan, "u")], axis=0)
    hits = jnp.stack([jnp.any(plan[:, :top] == e, axis=1) for e in own], axis=1)
    first = plan[:, top]
    less = (first[:, :, None] < first[:, None, :]).astype(BF)
    rank = jnp.einsum("gjs,gst->gjt", hits.astype(BF), less, preferred_element_type=F32)
    rank = rank.astype(jnp.int32)
    rank = jnp.where(hits & (rank < capacity), rank, -1)
    rank = rank.reshape(4, per_device, 2, 2, rows)
    rank = jnp.where(at_x == 1, rank[:, :, ::-1], rank)
    rank = jnp.where(at_c == 1, rank[:, :, :, ::-1], rank)
    rank = rank.swapaxes(2, 3).reshape(4, per_device, length)

    def beside(step):
        return lambda *markers: part_in(*markers) + (
            (plan, plan, rank)[step : step + 1]
        )

    pool = [value for piece in gather_pool([ma, mb, mc], beside, cross) for value in piece]
    if n_outer == 2:
        ready_mats = lambda j: [own_mats[j]] + parts_in[j]
    else:
        all_mats = [lax.all_gather(m, "o", axis=0, tiled=True) for m in own_mats]
        ready_mats = lambda j: [all_mats[j]]
    at_o = lax.axis_index("o")
    bases = [at_o * 4 * shard, (1 - at_o) * 4 * shard] if n_outer == 2 else [0, 0]
    bases = jnp.stack([jnp.int32(base) for base in bases])

    params = dict(compiler_params=pltpu.CompilerParams(vmem_limit_bytes=VMEM_LIMIT))
    specs = [pool_specs(o, w) for o, w in zip(ORDERS, widths)]
    tok_specs = [spec for halves, _ in specs for spec in halves * 2]
    sum_specs = [whole for _, whole in specs]
    slot_spec = lambda width: pl.BlockSpec((BLK, width), lambda g, meta: (g, 0))
    rank_spec = pl.BlockSpec((1, 1, length), lambda g, meta: (g, 0, 0))
    mat_shape = (n_outer * 16, 3, shard, hidden // 4)
    mat_spec = lambda m: pl.BlockSpec(
        m.shape, lambda g, meta: (0, 0, 0, 0), pipeline_mode=pl.Buffered(1)
    )
    down_spec = lambda m: pl.BlockSpec(
        (m.shape[0], 1) + m.shape[2:], lambda g, meta: (0, 2, 0, 0), pipeline_mode=pl.Buffered(1)
    )
    pool_shapes = [jax.ShapeDtypeStruct((2, 2, 2, rows, w), BF) for w in widths]
    slots = 4 * capacity
    groups = steps(4)
    metas = [jnp.concatenate([e[None], groups, bases]).astype(jnp.int32) for e in own]
    chunk = dim // 4
    full = lambda width: pl.BlockSpec((slots, width), lambda i, meta: (0, 0))
    turned = lambda i, meta: jnp.where(meta[5] == 0, i ^ 2, i) if n_outer == 2 else i
    chunk_spec = pl.BlockSpec((slots, chunk), lambda i, meta: (0, turned(i, meta)))
    grad_shape = lambda n: jax.ShapeDtypeStruct((n,) + mat_shape[1:], BF)
    whole = lambda n: pl.BlockSpec((n,) + mat_shape[1:], lambda i, meta: (0, 0, 0, 0))

    def weight_grads_of(meta, saved, j):
        counts = [*PARTS_OUT[j], 16] if n_outer == 2 else [16 * n_outer]
        return pl.pallas_call(
            functools.partial(weight_grad_kernel, chunk // shard * 4),
            grid_spec=pltpu.PrefetchScalarGridSpec(
                num_scalar_prefetch=1,
                grid=(4,),
                in_specs=[chunk_spec, chunk_spec, full(2 * hidden), full(hidden)],
                out_specs=[whole(n) for n in counts],
            ),
            out_shape=[grad_shape(n) for n in counts],
            cost_estimate=cost(9),
            **params,
        )(meta, *saved)

    prev, weighted, saved = [], [], []
    parts_out, all_grads = [[], []], [[], []]

    def part_out(j, *markers):
        if n_outer != 2:
            return ()
        part = all_grads[j][len(parts_out[j])]
        parts_out[j].append(swap(after_all(part, *markers), "o"))
        return (parts_out[j][-1],)

    for j in range(per_device):
        if j == 0:
            moving = part_in(*pool)
        else:
            prev = together(prev, *moving)
            first_grads = weight_grads_of(after_all(metas[0], prev[0]), saved[0], 0)
            metas[j] = after_all(metas[j], first_grads[0])
            all_grads[0].extend(first_grads)
            moving = part_out(0, first_grads[0])
        result = pl.pallas_call(
            functools.partial(expert_kernel, len(ready_mats(j)), j == 0),
            grid_spec=pltpu.PrefetchScalarGridSpec(
                num_scalar_prefetch=1,
                grid=(4,),
                in_specs=tok_specs
                + [rank_spec]
                + [mat_spec(m) for m in ready_mats(j)]
                + ([rank_spec] + [slot_spec(w) for w in widths] if j else []),
                out_specs=(sum_specs * 2 if j else [slot_spec(w) for w in widths])
                + [slot_spec(dim), slot_spec(dim), slot_spec(2 * hidden), slot_spec(hidden)],
                scratch_shapes=[pltpu.VMEM((dim, 3 * hidden), BF)],
            ),
            out_shape=(
                pool_shapes * 2 if j else [jax.ShapeDtypeStruct((slots, w), BF) for w in widths]
            )
            + [jax.ShapeDtypeStruct((slots, w), BF) for w in (dim, dim, 2 * hidden, hidden)],
            cost_estimate=cost(29),
            **params,
        )(
            metas[j], *pool, rank[:, j : j + 1], *ready_mats(j),
            *([rank[:, :1], *prev] if j else []),
        )
        prev, kept = (result[:6], result[6:]) if j else (result[:3], result[3:])
        saved.append(kept)

    prev = together(prev, *moving)
    last_grads = all_grads[1]

    moved = []

    def total(mine, parts):
        return (mine.astype(F32) + jnp.concatenate(parts, axis=0).astype(F32)).astype(BF)

    def fill(step, bufs):
        if step == 0:
            last_grads.extend(weight_grads_of(after_all(metas[1], prev[0]), saved[1], 1))
            return (*part_out(0, *bufs), last_grads[0])
        return (part_out(0, *bufs) if step == 1 else ()) + part_out(1, *bufs)

    pairs = scatter_pool(prev[:3], prev[3:], fill)

    after_grad, aog, small, block_out = simple_call(
        back_kernel,
        [((rows, dim), F32), ((rows, dim), BF), ((dim, 128), F32), ((rows, dim), BF)],
        0,
        11,
        5,
    )(after, *pairs[0], *pairs[1], *pairs[2], gains, wob, gates, cot)
    near, cross = swap(aog, "c"), swap(aog, "x")
    moving = part_out(1, pairs[0][1])
    if n_outer == 2:
        first_sum = total(first_grads[-1], parts_out[0])
        near, cross, first_sum = together((near, cross, first_sum), *moving)
    aog_parts = [aog, near, cross, swap(cross, "c")]

    n_tails = 2 if n_dp == 8 else 1
    dests = jnp.bitwise_xor(at_z, steps(8) % 4) * 2 + jnp.bitwise_xor(at_y, steps(8) // 4)
    dests = (dests if n_dp == 8 else steps(n_dp)).astype(jnp.int32)
    tail_shape = lambda width: [((n_dp // n_tails, shard, width), BF)] * n_tails
    sides = simple_call(
        functools.partial(out_grad_kernel, n_tails),
        tail_shape(384),
        2,
        6,
        2,
        scratch=[pltpu.VMEM((length, dim), BF), pltpu.VMEM((dim, 384), BF)],
    )(dests, offs, *aog_parts, mix, small)

    aog_parts = together(aog_parts, *sides)
    moving = part_out(1, cross)
    if n_outer == 2:
        first_sum = after_all(first_sum, *aog_parts)
    else:
        first_sum, last_sum = (
            lax.psum_scatter(g[0], "o", scatter_dimension=0, tiled=True)
            for g in (first_grads, last_grads)
        )
    moved.append(lax.all_to_all(first_sum, POOL, 0, 0, tiled=True))
    sides = list(sides)
    if n_tails == 2:
        sides[1] = swap(sides[1], "y")
    keep, send, *tails = simple_call(
        functools.partial(attend_backward_kernel, n_tails),
        [((2, rows, dim), F32), ((2, rows, dim), BF)] + tail_shape(640),
        2,
        14,
        60,
        scratch=[
            pltpu.VMEM((length, dim), BF),
            pltpu.VMEM((length, heads), BF),
            pltpu.VMEM((length, 512), BF),
            pltpu.VMEM((2, length, 128), F32),
            pltpu.VMEM((2, length, 128), F32),
            pltpu.VMEM((dim, 640), BF),
        ],
    )(dests, offs, *aog_parts, wqkv, wob, q, kd, vd, lse, start_col, ain, cosine, sine)
    keep, send, *tails = together((keep, send, *tails), *sides, *moving)

    got = swap(send, "c")
    if n_outer == 2:
        last_sum = total(last_grads[-1], [*parts_out[1][:-1], after_all(parts_out[1][-1], got)])
    cross = swap((keep[1] + got[1].astype(F32)).astype(BF), "x")
    if n_tails == 2:
        add = lambda a, b: (a.astype(F32) + b.astype(F32)).astype(BF)
        side_sums = add(*sides)
        tails[1] = swap(tails[1], "y")

        def reduce_z(sums):
            return [sums[0]] + [
                lax.ppermute(sums[s], ("o", "u"), [(i, i ^ s) for i in range(4)]) for s in (1, 2, 3)
            ]

        side_parts = reduce_z(side_sums)
        *tails, cross, got, moved[0] = together((*tails, cross, got, moved[0]), *side_parts)
        tail_parts = reduce_z(add(*tails))
        side, tail = (sum(p.astype(F32) for p in parts) for parts in (side_parts, tail_parts))
    else:
        side, tail = (
            lax.psum_scatter(part[0].astype(F32).reshape(dim, -1), DP, scatter_dimension=0, tiled=True)
            for part in (sides, tails)
        )
    moved.append(lax.all_to_all(after_all(last_sum, *tails), POOL, 0, 0, tiled=True))
    tokens_grad = simple_call(finish_kernel, [((rows, dim), F32)], 0, 6, 4)(
        tok, keep, got, cross, gains, after_grad
    )[0]

    narrow = jnp.concatenate([side[:, 256 : 256 + experts + 1], tail[:, 512:513]], axis=1)
    narrow = narrow + sum(
        lax.ppermute(narrow, ("x", "c"), [(i, i ^ s) for i in range(4)]) for s in range(1, 4)
    )
    gate_grad, up_grad, down_grad = (
        jnp.concatenate([part[:, m] for part in moved], axis=0).astype(F32) for m in range(3)
    )
    return (
        block_out[None],
        tokens_grad[None],
        narrow[:, experts + 1] / norm_attn.astype(F32),
        tail[:, :256],
        tail[:, 256:384],
        tail[:, 384:512],
        side[:, :256],
        narrow[:, experts],
        narrow[:, :experts],
        gate_grad,
        up_grad,
        down_grad,
    )


def solution(mesh):
    devices = mesh.devices
    fine = Mesh(devices.reshape(devices.shape[0] // 4, 2, 2, 2, 2), ("o", "u", "y", "x", "c"))
    dp, tensor = DP, ("x", "c")
    in_specs = (
        P(dp, tensor, None),
        P(dp, None),
        P(dp, None, None),
        P(dp, None),
        P(dp),
        P(dp, tensor),
        P(dp, tensor),
        P(dp, tensor),
        P(dp, tensor),
        P(dp),
        P(dp, None),
        P(None, dp, tensor),
        P(None, dp, tensor),
        P(None, dp, tensor),
        P(dp, tensor, None),
    )
    out_specs = (
        P(dp, tensor, None),
        P(dp, tensor, None),
        P(dp),
        P(dp, tensor),
        P(dp, tensor),
        P(dp, tensor),
        P(dp, tensor),
        P(dp),
        P(dp, None),
        P(None, dp, tensor),
        P(None, dp, tensor),
        P(None, dp, tensor),
    )
    return jax.shard_map(local, mesh=fine, in_specs=in_specs, out_specs=out_specs, check_vma=False)
```
